128 devices in a mesh: visit: 8 (over y, core), sky: 16 (over z, x).
Axes of the slice: x: 4, y: 4, z: 4, core: 2. Of those that a mesh axis runs over, the one named last changes fastest.
Arguments:
- tiles: bfloat16 [2048, 256, 256], P(('visit', 'sky')), may hold values from -6 to 6
- shift_int: int32 [2048, 2], P(('visit', 'sky')), may hold values from -3 to 3
- shift_frac: float32 [2048, 2], P(('visit', 'sky')), may hold values from 0 to 1
- tile_weight: float32 [2048], replicated, may hold values from 0.25 to 4
- tile_patch: int32 [2048], replicated, may hold values from 0 to 63, as said below
- al_coeff: float32 [2048, 10], P(('visit', 'sky')), may hold values from -3 to 3
Outputs:
- coadd: float32 [64, 256, 256], P('sky', 'visit')
- difference: float32 [2048, 256, 256], P(('visit', 'sky'))
The draws below stay inside these ranges and needn't reach their ends.
Inputs may be any that keep to these rules, and one draw needn't show every extreme that they name: `tile_patch`: the owner of patch p is p // 4. Among the 16 tiles of one device (consecutive in the tile order) at most 2 have patches of one owner, and in every draw some owner has exactly 2 tiles from every device.
All inputs are finite; a program needn't handle non-finite values.
Results may differ from the reference program's by a relative error of at most 0.0053.
Values may be sent and summed in bfloat16 or wider, within the bound.
A program may use at most 192 MiB of HBM per device.

```python
import math
import jax
import jax.numpy as jnp
from jax import lax

TILE = 256
KHALF = 10
CAP = 2
NBASIS = 10
TILES_DEV = 16
PAT_SKY = 4
TILES = 2048
PATCHES = 64


def draw_tile_patch(key, part):
    key = jax.random.fold_in(key, 11)
    key_bias, key_top, key_noise, key_order, key_sub = jax.random.split(key, 5)
    owners = PATCHES // PAT_SKY
    devices = TILES // TILES_DEV
    slot_count = owners * CAP
    slot_owner = jnp.arange(slot_count) // CAP
    levels = jax.random.randint(key_bias, (owners,), 0, 4)
    favoured = jax.random.randint(key_top, (), 0, owners)
    levels = jnp.where(jnp.arange(owners) == favoured, 100000, levels)
    noise = jax.random.randint(key_noise, (devices, slot_count), 0, 64)
    score = (levels[slot_owner][None, :] * 64 + noise) * slot_count + jnp.arange(slot_count)[None, :]
    unused, chosen = lax.top_k(score, TILES_DEV)
    chosen = jax.random.permutation(key_order, chosen, axis=1, independent=True)
    owner = chosen // CAP
    sub = jax.random.randint(key_sub, (devices, TILES_DEV), 0, PAT_SKY)
    return (owner * PAT_SKY + sub).reshape(-1).astype(jnp.int32)


def plant(values, own_key, low, largest):
    extent = values.shape
    place = [jax.random.randint(jax.random.fold_in(own_key, axis), (), 0, extent[axis]) for axis in range(len(extent))]
    values = values.at[tuple(place)].set(low)
    longest = extent.index(max(extent))
    place[longest] = (place[longest] + 1) % extent[longest]
    return values.at[tuple(place)].set(largest)


def block_levels(key, dims, shards, least, high):
    factor_of = 1.0
    for position, parts in shards:
        draws = jax.random.uniform(jax.random.fold_in(jax.random.fold_in(key, 6), position), (parts,), jnp.float32, least / len(shards), high / len(shards))
        factor_of = factor_of * jnp.repeat(jnp.exp(draws), dims[position] // parts).reshape((-1,) + (1,) * (len(dims) - 1 - position))
    return factor_of


def centred(stream_key, dims, spread, most, pieces=(), kind=jnp.bfloat16):
    array = jax.random.normal(stream_key, dims, jnp.float32) * spread
    if len(pieces) > 0:
        array = block_levels(stream_key, dims, pieces, -0.22, 0.18) * array
    return jnp.clip(array, min=-most, max=most).astype(kind)


def setup_inputs(seed: int = 0) -> dict:
    key_of = jax.random.split(jax.random.key(seed), 7)
    tiles = centred(key_of[0], (TILES, TILE, TILE), 1.0, 6.0, ((0, 128),))
    shift_int = plant(jax.random.randint(key_of[1], (TILES, 2), -3, 4), jax.random.fold_in(key_of[1], 1), -3, 3).astype(jnp.int32)
    shift_frac = jnp.clip(1.0 * jax.random.uniform(key_of[2], (TILES, 2), jnp.float32) ** block_levels(key_of[2], (TILES, 2), ((0, 128),), -0.2, 0.2), 0.0, 1.0)
    tile_weight = jnp.clip(jnp.exp(jax.random.uniform(key_of[3], (TILES,), jnp.float32, math.log(0.25), math.log(4.0))), 0.25, 4.0)
    tile_patch = draw_tile_patch(jax.random.fold_in(key_of[6], 71), 0)
    al_coeff = centred(key_of[5], (TILES, NBASIS), 0.5, 3.0, ((0, 128),), jnp.float32)
    return {"tiles": tiles, "shift_int": shift_int, "shift_frac": shift_frac, "tile_weight": tile_weight, "tile_patch": tile_patch, "al_coeff": al_coeff}


sigma_list = (1.0, 2.5, 5.0)
factor_list = ((0, 0), (0, 1), (0, 2), (1, 0), (1, 1), (2, 0))
basis_rows = (0, 1, 0, 2, 0, 1, 3, 4, 3, 5)
basis_cols = (0, 0, 1, 0, 2, 1, 3, 3, 4, 5)


def lanczos(shift, count):
    index = jnp.arange(count)
    offset = (index[None, :] - index[:, None]).astype(jnp.float32) - shift
    return jnp.where(jnp.abs(offset) < 3.0, jnp.sinc(offset) * jnp.sinc(offset / 3.0), 0.0)


def factor_mats(count):
    index = jnp.arange(count)
    diffs = (index[:, None] - index[None, :]).astype(jnp.float32)
    offsets = jnp.arange(-KHALF, KHALF + 1).astype(jnp.float32)
    mats = []
    for sigma_index, power in factor_list:
        sigma = sigma_list[sigma_index]
        norm_sum = jnp.sum(jnp.exp(-offsets * offsets / (2.0 * sigma * sigma)))
        value = jnp.exp(-diffs * diffs / (2.0 * sigma * sigma)) * (diffs / sigma) ** power / norm_sum
        mats.append(jnp.where(jnp.abs(diffs) <= KHALF, value, 0.0))
    return jnp.stack(mats)


def warp_one(tile, shift_i, shift_f):
    shift = shift_i.astype(jnp.float32) + shift_f
    row_mat = lanczos(shift[0], TILE).astype(jnp.bfloat16)
    col_mat = lanczos(shift[1], TILE).astype(jnp.bfloat16)
    rowpass = jnp.dot(tile, col_mat.T, preferred_element_type=jnp.float32).astype(jnp.bfloat16)
    return jnp.dot(row_mat, rowpass, preferred_element_type=jnp.float32)


def reference(tiles, shift_int, shift_frac, tile_weight, tile_patch, al_coeff):
    def accumulate(total, item):
        tile, shift_i, shift_f, weight, patch = item
        weighted = (weight * warp_one(tile, shift_i, shift_f)).astype(jnp.bfloat16)
        return total.at[patch].add(weighted.astype(jnp.float32)), None

    start = jnp.zeros((PATCHES, TILE, TILE), jnp.float32)
    summed, unused = lax.scan(accumulate, start, (tiles, shift_int, shift_frac, tile_weight, tile_patch))
    weight_sum = jax.ops.segment_sum(tile_weight, tile_patch, num_segments=PATCHES)
    coadd = summed / (1.0 + weight_sum)[:, None, None]
    template = coadd.astype(jnp.bfloat16)
    factors = factor_mats(TILE)
    factors_low = factors.astype(jnp.bfloat16)

    def diff_one(item):
        tile, shift_i, shift_f, coeff, patch = item
        warp = warp_one(tile, shift_i, shift_f)
        patch_image = template[patch]
        convolved = jnp.zeros((TILE, TILE), jnp.float32)
        for column in range(len(factor_list)):
            filtered = jnp.dot(patch_image, factors_low[column].T, preferred_element_type=jnp.float32).astype(jnp.bfloat16)
            mixed = jnp.zeros((TILE, TILE), jnp.float32)
            for basis in range(NBASIS):
                if basis_cols[basis] == column:
                    mixed = mixed + coeff[basis] * factors[basis_rows[basis]]
            convolved = convolved + jnp.dot(mixed.astype(jnp.bfloat16), filtered, preferred_element_type=jnp.float32)
        return warp - convolved

    difference = lax.map(diff_one, (tiles, shift_int, shift_frac, al_coeff, tile_patch))
    return coadd, difference
```

```python
import functools
import math

import jax
import jax.numpy as jnp
import numpy as np
from jax import lax
from jax.experimental import pallas as pl
from jax.experimental.pallas import tpu as pltpu
from jax.sharding import PartitionSpec as P

MESH = pl.DeviceIdType.MESH
KHALF = 10
SIDE = 256
TILES_DEV = 16
SIGMAS = (1.0, 2.5, 5.0)
FACTORS = ((0, 0), (0, 1), (0, 2), (1, 0), (1, 1), (2, 0))
BASIS_ROWS = (0, 1, 0, 2, 0, 1, 3, 4, 3, 5)
BASIS_COLS = (0, 0, 1, 0, 2, 1, 3, 3, 4, 5)
NF = len(FACTORS)

UNITS = ((0, 3), (3, 6), (6, 8))
GROUPS = 2
TG = TILES_DEV // GROUPS
PG = TG // 2
RB = TG * 8


def wrapped_diff():
    diff = np.arange(128)[None, :] - np.arange(8)[:, None]
    return ((diff + 64) % 128) - 64


def factor_strips():
    diff = wrapped_diff().astype(np.float64)
    reach = np.arange(-KHALF, KHALF + 1).astype(np.float64)
    ahead, back = [], []
    for sigma_index, power in FACTORS:
        sigma = SIGMAS[sigma_index]
        norm = np.sum(np.exp(-reach * reach / (2.0 * sigma * sigma)))
        for out, u in ((ahead, diff), (back, -diff)):
            value = np.exp(-u * u / (2.0 * sigma * sigma)) * (u / sigma) ** power / norm
            out.append(np.where(np.abs(u) <= KHALF, value, 0.0))
    return np.stack(ahead).astype(np.float32), np.stack(back).astype(np.float32)


def lanczos_strips(shift):
    diff = jnp.asarray(wrapped_diff().astype(np.float32))
    offset = jnp.stack(
        [
            diff[None] - shift[:, 0, None, None],
            -diff[None] - shift[:, 1, None, None],
        ],
        axis=1,
    )
    return jnp.where(jnp.abs(offset) < 3.0, jnp.sinc(offset) * jnp.sinc(offset / 3.0), 0.0)


def toeplitz_blocks(strip):
    lane = lax.broadcasted_iota(jnp.int32, (8, 128), 1)
    rows = [strip if b == 0 else pltpu.roll(strip, 8 * b, 1) for b in range(16)]
    low = lane < 64
    zero = jnp.zeros_like(strip)
    left = [jnp.where(low, zero, rows[b]) for b in (0, 1)]
    right = [jnp.where(low, rows[b], zero) for b in (14, 15)]
    for b in (0, 1):
        rows[b] = jnp.where(low, rows[b], zero)
    for b in (14, 15):
        rows[b] = jnp.where(low, zero, rows[b])

    def pack(pair):
        return jnp.concatenate(pair, axis=0).astype(jnp.bfloat16)

    return [pack(rows[2 * i : 2 * i + 2]) for i in range(8)], pack(right), pack(left)


def write_square(strip, ref):
    diag, right, left = toeplitz_blocks(strip)
    for i in range(8):
        ref[16 * i : 16 * i + 16, 0:128] = diag[i]
        ref[128 + 16 * i : 144 + 16 * i, 128:256] = diag[i]
    ref[112:128, 128:256] = right
    ref[128:144, 0:128] = left


def kernel(
    tiles_hbm,
    patch_s,
    weight_s,
    coeff_s,
    patch_v,
    weight_v,
    strips,
    ahead,
    back,
    diff_hbm,
    coadd_out,
    tiles,
    warp,
    send1,
    recv1,
    sel,
    selt,
    asend,
    arecv,
    bsend,
    brecv,
    gath,
    send4,
    recv4,
    csend,
    crecv,
    fmat,
    mband,
    rmat,
    tbuf,
    hbuf,
    s1,
    r1,
    sa,
    ra,
    sb,
    rb,
    sgb,
    rgb,
    sga,
    rga,
    s4,
    r4,
    sc,
    rc,
    in_sem,
    own1,
    own4,
    out_sem,
):
    visit, sky = lax.axis_index("visit"), lax.axis_index("sky")
    y, c = lax.div(visit, 2), lax.rem(visit, 2)
    z, x = lax.div(sky, 4), lax.rem(sky, 4)

    def dev(y_, c_, z_, x_):
        return (y_ * 2 + c_, z_ * 4 + x_)

    ring_of = (y, z, x)
    plane_of = ((x, z), (y, x), (z, y))

    def on_ring(p, pos, core):
        return (
            dev(pos, core, z, x),
            dev(y, core, pos, x),
            dev(y, core, z, pos),
        )[p]

    def on_first(p, pos):
        return (dev(y, c, z, pos), dev(pos, c, z, x), dev(y, c, pos, x))[p]

    def on_second(p, pos):
        return (dev(y, c, pos, x), dev(y, c, z, pos), dev(pos, c, z, x))[p]

    swap = (dev(z, c, y, x), dev(x, c, z, y))
    moved = (y != z, y != x)

    def fetch(g):
        return pltpu.make_async_copy(
            tiles_hbm.at[pl.ds(g * TG, TG)], tiles.at[pl.ds(g * TG, TG)], in_sem.at[g]
        )

    for g in range(GROUPS):
        fetch(g).start()

    barrier = pltpu.get_barrier_semaphore()
    pl.semaphore_signal(barrier, inc=1, device_id=dev(y, 1 - c, z, x), device_id_type=MESH)
    for p in range(3):
        for d in range(1, 4):
            for other in (0, 1):
                pl.semaphore_signal(
                    barrier,
                    inc=1,
                    device_id=on_ring(p, lax.rem(ring_of[p] + d, 4), lax.rem(c + other, 2)),
                    device_id_type=MESH,
                )
    for i in range(2):

        @pl.when(moved[i])
        def _(i=i):
            pl.semaphore_signal(barrier, inc=1, device_id=swap[i], device_id_type=MESH)

    def clear(ref):
        ref[...] = jnp.zeros(ref.shape, ref.dtype)

    @pl.loop(0, NF)
    def _(j):
        clear(fmat.at[j])

    @pl.loop(0, 4)
    def _(j):
        clear(rmat.at[j])

    def first(p, g, k):
        lo, hi = UNITS[p]
        d, other = k // 2, k % 2
        pos, core = lax.rem(ring_of[p] + d, 4), lax.rem(c + other, 2)
        src = send1.at[g, pos * 2 + core, pl.ds(lo, hi - lo)]
        dst = recv1.at[g, k, pl.ds(lo, hi - lo)]
        if k == 0:
            return pltpu.make_async_copy(src, dst, own1.at[p, g])
        return pltpu.make_async_remote_copy(
            src_ref=src,
            dst_ref=dst,
            send_sem=s1.at[p, g, k - 1],
            recv_sem=r1.at[p, g, k - 1],
            device_id=on_ring(p, pos, core),
            device_id_type=MESH,
        )

    for g in range(GROUPS):
        fetch(g).wait()

        @pl.loop(0, PG)
        def _(pair, g=g):
            scaled = []
            for half in range(2):
                t = g * TG + pair * 2 + half
                write_square(strips[t, 0], rmat.at[2 * half])
                write_square(strips[t, 1], rmat.at[2 * half + 1])
                rowpass = jnp.dot(
                    tiles[t], rmat[2 * half + 1], preferred_element_type=jnp.float32
                ).astype(jnp.bfloat16)
                value = jnp.dot(rmat[2 * half], rowpass, preferred_element_type=jnp.float32)
                warp[t] = value
                scaled.append((weight_s[(visit * 16 + sky) * TILES_DEV + t] * value).reshape(32, 8, SIDE))
            both = jnp.concatenate(scaled, axis=1).astype(jnp.bfloat16)
            rows = pl.ds(pl.multiple_of(pair * 16, 16), 16)
            for q in range(8):
                for u in range(8):
                    send1[g, q, u, rows, :] = both[4 * q + u // 2, :, 128 * (u % 2) : 128 * (u % 2) + 128]

        if g == 0:
            pl.semaphore_wait(barrier, 19 + moved[0].astype(jnp.int32) + moved[1].astype(jnp.int32))
        for p in range(3):
            for k in range(8):
                first(p, g, k).start()

    def patch_row(p, g, k, tt):
        pos, core = lax.rem(ring_of[p] + 4 - lax.div(k, 2), 4), lax.rem(c + lax.rem(k, 2), 2)
        v, s = on_ring(p, pos, core)
        patch = patch_s[(v * 16 + s) * TILES_DEV + g * TG + tt]
        if p == 0:
            patch = ((patch >> 2) & 3) * 16 + (patch >> 4) * 4 + (patch & 3)
        return patch * 8

    lane = lax.broadcasted_iota(jnp.int32, (8, 128), 1)
    high = lax.broadcasted_iota(jnp.int32, (512, 128), 0)
    for p in range(3):

        @pl.loop(0, 8)
        def _(m, p=p):
            key = jnp.zeros((8, 128), jnp.int32)
            for tt in range(16):
                j = m * 16 + tt
                g, rest = lax.div(j, 8 * TG), lax.rem(j, 8 * TG)
                row = patch_row(p, g, lax.div(rest, TG), lax.rem(rest, TG))
                key = jnp.where((lane >> 3) == tt, row, key)
            key = key + (lane & 7)
            wide = jnp.broadcast_to(key[0:1], (512, 128))
            sel[p, :, pl.ds(pl.multiple_of(m * 128, 128), 128)] = jnp.where(
                wide == high, 1.0, 0.0
            ).astype(jnp.bfloat16)

        @pl.loop(0, 64)
        def _(m, p=p):
            rows = []
            for half in range(2):
                j = m * 2 + half
                g, rest = lax.div(j, 8 * TG), lax.rem(j, 8 * TG)
                row = patch_row(p, g, lax.div(rest, TG), lax.rem(rest, TG))
                across = lax.broadcasted_iota(jnp.int32, (8, 512), 1)
                down = lax.broadcasted_iota(jnp.int32, (8, 512), 0)
                rows.append(jnp.where(across == down + row, 1.0, 0.0))
            selt[p, pl.ds(pl.multiple_of(m * 16, 16), 16), :] = jnp.concatenate(rows, axis=0).astype(
                jnp.bfloat16
            )

    for j in range(NF):
        write_square(ahead[j], fmat.at[j])

    @pl.loop(0, TILES_DEV)
    def _(t):
        for j in range(NF):
            strip = None
            for k in range(len(BASIS_COLS)):
                if BASIS_COLS[k] == j:
                    term = coeff_s[t, k] * back[BASIS_ROWS[k]]
                    strip = term if strip is None else strip + term
            diag, right, left = toeplitz_blocks(strip)
            cols = slice(128 * j, 128 * j + 128)
            mband[t, 0:16, cols] = right
            for i in range(8):
                mband[t, 16 + 16 * i : 32 + 16 * i, cols] = diag[i]
            mband[t, 144:160, cols] = left

    def second(p, d):
        lo, hi = UNITS[p]
        pos = lax.rem(plane_of[p][0] + d, 4)
        return pltpu.make_async_remote_copy(
            src_ref=asend.at[pos, pl.ds(lo, hi - lo)],
            dst_ref=arecv.at[d - 1, pl.ds(lo, hi - lo)],
            send_sem=sa.at[p, d - 1],
            recv_sem=ra.at[p, d - 1],
            device_id=on_first(p, pos),
            device_id_type=MESH,
        )

    def third(p, d):
        lo, hi = UNITS[p]
        pos = lax.rem(plane_of[p][1] + d, 4)
        return pltpu.make_async_remote_copy(
            src_ref=bsend.at[pos, pl.ds(lo, hi - lo)],
            dst_ref=brecv.at[d - 1, pl.ds(lo, hi - lo)],
            send_sem=sb.at[p, d - 1],
            recv_sem=rb.at[p, d - 1],
            device_id=on_second(p, pos),
            device_id_type=MESH,
        )

    for p in range(3):
        lo, hi = UNITS[p]
        for g in range(GROUPS):
            first(p, g, 0).wait()
            for k in range(1, 8):
                first(p, g, k).wait_recv()
        wide = jnp.concatenate([recv1[:, :, u].reshape(1024, 128) for u in range(lo, hi)], axis=1)
        total = jnp.dot(sel[p], wide, preferred_element_type=jnp.float32).astype(jnp.bfloat16)
        for u in range(lo, hi):
            asend[:, u] = total[:, 128 * (u - lo) : 128 * (u - lo) + 128].reshape(4, 128, 128)
        for d in range(1, 4):
            second(p, d).start()

    for p in range(3):
        lo, hi = UNITS[p]
        for d in range(1, 4):
            second(p, d).wait_recv()
        total = asend[plane_of[p][0], lo:hi].astype(jnp.float32)
        for d in range(1, 4):
            total = total + arecv[d - 1, lo:hi].astype(jnp.float32)
        total = total.astype(jnp.bfloat16)
        for b in range(4):
            bsend[b, lo:hi] = total[:, 32 * b : 32 * b + 32]
        for d in range(1, 4):
            third(p, d).start()

    def fourth(p, d):
        lo, hi = UNITS[p]
        mine = gath.at[plane_of[p][0], plane_of[p][1], pl.ds(lo, hi - lo)]
        return pltpu.make_async_remote_copy(
            src_ref=mine,
            dst_ref=mine,
            send_sem=sgb.at[p, d - 1],
            recv_sem=rgb.at[p, d - 1],
            device_id=on_second(p, lax.rem(plane_of[p][1] + d, 4)),
            device_id_type=MESH,
        )

    def fifth(p, d):
        lo, hi = UNITS[p]
        mine = gath.at[plane_of[p][0], :, pl.ds(lo, hi - lo)]
        return pltpu.make_async_remote_copy(
            src_ref=mine,
            dst_ref=mine,
            send_sem=sga.at[p, d - 1],
            recv_sem=rga.at[p, d - 1],
            device_id=on_first(p, lax.rem(plane_of[p][0] + d, 4)),
            device_id_type=MESH,
        )

    def to_owner(i):
        lo, hi = UNITS[i + 1]
        return pltpu.make_async_remote_copy(
            src_ref=csend.at[pl.ds(lo, hi - lo)],
            dst_ref=crecv.at[pl.ds(lo, hi - lo)],
            send_sem=sc.at[i],
            recv_sem=rc.at[i],
            device_id=swap[i],
            device_id_type=MESH,
        )

    owner_of = (z * 4 + x, y * 4 + x, z * 4 + y)
    for p in range(3):
        lo, hi = UNITS[p]
        for d in range(1, 4):
            third(p, d).wait_recv()
        total = bsend[plane_of[p][1], lo:hi].astype(jnp.float32)
        for d in range(1, 4):
            total = total + brecv[d - 1, lo:hi].astype(jnp.float32)
        parts = []
        for k in range(4):
            hit = jnp.where(patch_v[...] == owner_of[p] * 4 + k, weight_v[...], 0.0)
            weight = jnp.sum(jnp.sum(hit, axis=0, keepdims=True), axis=1, keepdims=True)
            parts.append(total[:, 8 * k : 8 * k + 8] / (1.0 + weight)[None])
        coadd = jnp.concatenate(parts, axis=1)
        csend[lo:hi] = coadd
        gath[plane_of[p][0], plane_of[p][1], lo:hi] = coadd.astype(jnp.bfloat16)
        for d in range(1, 4):
            fourth(p, d).start()

    for i in range(2):

        @pl.when(moved[i])
        def _(i=i):
            to_owner(i).start()

    for p in range(3):
        for d in range(1, 4):
            fourth(p, d).wait_recv()
        for d in range(1, 4):
            fifth(p, d).start()

    def last(p, g, k):
        lo, hi = UNITS[p]
        d, other = k // 2, k % 2
        pos, core = lax.rem(ring_of[p] + 4 - d, 4), lax.rem(c + other, 2)
        src = send4.at[g, k, pl.ds(lo, hi - lo)]
        dst = recv4.at[g, ring_of[p] * 2 + c, pl.ds(lo, hi - lo)]
        if k == 0:
            return pltpu.make_async_copy(src, dst, own4.at[p, g])
        return pltpu.make_async_remote_copy(
            src_ref=src,
            dst_ref=dst,
            send_sem=s4.at[p, g, k - 1],
            recv_sem=r4.at[p, g, k - 1],
            device_id=on_ring(p, pos, core),
            device_id_type=MESH,
        )

    per_group = 1024 // GROUPS
    for g in range(GROUPS):
        for p in range(3):
            lo, hi = UNITS[p]
            if g == 0:
                for d in range(1, 4):
                    fifth(p, d).wait_recv()
            wide = jnp.concatenate([gath[:, :, u].reshape(512, 128) for u in range(lo, hi)], axis=1)
            picked = jnp.dot(
                selt[p, per_group * g : per_group * (g + 1), :], wide, preferred_element_type=jnp.float32
            ).astype(jnp.bfloat16)
            for u in range(lo, hi):
                send4[g, :, u] = picked[:, 128 * (u - lo) : 128 * (u - lo) + 128].reshape(8, RB, 128)
            for k in range(8):
                last(p, g, k).start()

    def leave(g, pair):
        t = g * TG + pair * 2
        return pltpu.make_async_copy(
            warp.at[pl.ds(t, 2)], diff_hbm.at[pl.ds(t, 2)], out_sem.at[g, pair]
        )

    for g in range(GROUPS):
        for p in range(3):
            last(p, g, 0).wait()
            for k in range(1, 8):
                last(p, g, k).wait_recv()

        @pl.loop(0, PG)
        def _(pair, g=g):
            rows = pl.ds(pl.multiple_of(pair * 16, 16), 16)
            for q in range(8):
                for i in range(2):
                    for b in range(2):
                        upper = recv4[g, q, 4 * i + b, rows, :].astype(jnp.float32)
                        lower = recv4[g, q, 4 * i + 2 + b, rows, :].astype(jnp.float32)
                        at = 32 * q + 16 * i
                        cols = slice(128 * b, 128 * b + 128)
                        tbuf[at : at + 16, cols] = jnp.concatenate(
                            [upper[0:8], lower[0:8]], axis=0
                        ).astype(jnp.bfloat16)
                        tbuf[SIDE + at : SIDE + at + 16, cols] = jnp.concatenate(
                            [upper[8:16], lower[8:16]], axis=0
                        ).astype(jnp.bfloat16)
            for j in range(NF):
                filtered = jnp.dot(
                    tbuf[...], fmat[j], preferred_element_type=jnp.float32
                ).astype(jnp.bfloat16)
                for i in range(4):
                    hbuf[i, 128 * j : 128 * j + 128, :] = filtered[128 * i : 128 * i + 128]
            for half in range(2):
                t = g * TG + pair * 2 + half
                top = jnp.dot(
                    mband[t, 16:160, :], hbuf[2 * half], preferred_element_type=jnp.float32
                )
                low = jnp.dot(
                    mband[t, 0:144, :], hbuf[2 * half + 1], preferred_element_type=jnp.float32
                )
                warp[t, 0:112] = warp[t, 0:112] - top[0:112]
                warp[t, 112:144] = warp[t, 112:144] - (top[112:144] + low[0:32])
                warp[t, 144:256] = warp[t, 144:256] - low[32:144]
            leave(g, pair).start()

    for i in range(2):
        lo, hi = UNITS[i + 1]

        @pl.when(moved[i])
        def _(i=i):
            to_owner(i).wait()

        @pl.when(jnp.logical_not(moved[i]))
        def _(lo=lo, hi=hi):
            crecv[lo:hi] = csend[lo:hi]

    for u in range(8):
        for k in range(4):
            held = csend if u < UNITS[0][1] else crecv
            coadd_out[k, 8 * (u // 2) : 8 * (u // 2) + 8, 128 * (u % 2) : 128 * (u % 2) + 128] = held[
                u, 8 * k : 8 * k + 8
            ]

    for p in range(3):
        for g in range(GROUPS):
            for k in range(1, 8):
                first(p, g, k).wait_send()
                last(p, g, k).wait_send()
        for d in range(1, 4):
            second(p, d).wait_send()
            third(p, d).wait_send()
            fourth(p, d).wait_send()
            fifth(p, d).wait_send()

    @pl.loop(0, PG)
    def _(pair):
        for g in range(GROUPS):
            leave(g, pair).wait()


def shards(tiles, shift_int, shift_frac, tile_weight, tile_patch, al_coeff):
    strips = lanczos_strips(shift_int.astype(jnp.float32) + shift_frac)
    ahead, back = factor_strips()
    vmem = pl.BlockSpec(memory_space=pltpu.VMEM)
    smem = pl.BlockSpec(memory_space=pltpu.SMEM)
    hbm = pl.BlockSpec(memory_space=pl.ANY)
    bf16, f32 = jnp.bfloat16, jnp.float32
    dma = pltpu.SemaphoreType.DMA
    block = (GROUPS, 8, 8, RB, 128)
    difference, coadd = pl.pallas_call(
        kernel,
        out_shape=(
            jax.ShapeDtypeStruct((TILES_DEV, SIDE, SIDE), f32),
            jax.ShapeDtypeStruct((4, 32, SIDE), f32),
        ),
        in_specs=[hbm, smem, smem, smem, vmem, vmem, vmem, vmem, vmem],
        out_specs=(hbm, vmem),
        scratch_shapes=[
            pltpu.VMEM((TILES_DEV, SIDE, SIDE), bf16),
            pltpu.VMEM((TILES_DEV, SIDE, SIDE), f32),
            pltpu.VMEM(block, bf16),
            pltpu.VMEM(block, bf16),
            pltpu.VMEM((3, 512, 1024), bf16),
            pltpu.VMEM((3, 1024, 512), bf16),
            pltpu.VMEM((4, 8, 128, 128), bf16),
            pltpu.VMEM((3, 8, 128, 128), bf16),
            pltpu.VMEM((4, 8, 32, 128), bf16),
            pltpu.VMEM((3, 8, 32, 128), bf16),
            pltpu.VMEM((4, 4, 8, 32, 128), bf16),
            pltpu.VMEM(block, bf16),
            pltpu.VMEM(block, bf16),
            pltpu.VMEM((8, 32, 128), f32),
            pltpu.VMEM((8, 32, 128), f32),
            pltpu.VMEM((NF, SIDE, SIDE), bf16),
            pltpu.VMEM((TILES_DEV, 160, 128 * NF), bf16),
            pltpu.VMEM((4, SIDE, SIDE), bf16),
            pltpu.VMEM((2 * SIDE, SIDE), bf16),
            pltpu.VMEM((4, 128 * NF, SIDE), bf16),
            dma((3, GROUPS, 7)),
            dma((3, GROUPS, 7)),
            dma((3, 3)),
            dma((3, 3)),
            dma((3, 3)),
            dma((3, 3)),
            dma((3, 3)),
            dma((3, 3)),
            dma((3, 3)),
            dma((3, 3)),
            dma((3, GROUPS, 7)),
            dma((3, GROUPS, 7)),
            dma((2,)),
            dma((2,)),
            dma((GROUPS,)),
            dma((3, GROUPS)),
            dma((3, GROUPS)),
            dma((GROUPS, PG)),
        ],
        compiler_params=pltpu.CompilerParams(
            collective_id=0, has_side_effects=True, vmem_limit_bytes=56 << 20
        ),
    )(
        tiles,
        tile_patch,
        tile_weight,
        al_coeff,
        tile_patch.reshape(16, 128),
        tile_weight.reshape(16, 128),
        strips,
        jnp.asarray(ahead),
        jnp.asarray(back),
    )
    return coadd, difference


def solution(mesh):
    return jax.shard_map(
        shards,
        mesh=mesh,
        in_specs=(
            P(("visit", "sky"), None, None),
            P(("visit", "sky"), None),
            P(("visit", "sky"), None),
            P(),
            P(),
            P(("visit", "sky"), None),
        ),
        out_specs=(P("sky", "visit", None), P(("visit", "sky"), None, None)),
        check_vma=False,
    )
```

```python
import functools
import math

import jax
import jax.numpy as jnp
import numpy as np
from jax import lax
from jax.experimental import pallas as pl
from jax.experimental.pallas import tpu as pltpu
from jax.sharding import PartitionSpec as P

MESH = pl.DeviceIdType.MESH
KHALF = 10
SIDE = 256
TILES_DEV = 16
SIGMAS = (1.0, 2.5, 5.0)
FACTORS = ((0, 0), (0, 1), (0, 2), (1, 0), (1, 1), (2, 0))
BASIS_ROWS = (0, 1, 0, 2, 0, 1, 3, 4, 3, 5)
BASIS_COLS = (0, 0, 1, 0, 2, 1, 3, 3, 4, 5)
NF = len(FACTORS)

UNITS = ((0, 3), (3, 6), (6, 8))
GROUPS = 2
TG = TILES_DEV // GROUPS
PG = TG // 2
RB = TG * 8


def wrapped_diff():
    diff = np.arange(128)[None, :] - np.arange(8)[:, None]
    return ((diff + 64) % 128) - 64


def factor_strips():
    diff = wrapped_diff().astype(np.float64)
    reach = np.arange(-KHALF, KHALF + 1).astype(np.float64)
    ahead, back = [], []
    for sigma_index, power in FACTORS:
        sigma = SIGMAS[sigma_index]
        norm = np.sum(np.exp(-reach * reach / (2.0 * sigma * sigma)))
        for out, u in ((ahead, diff), (back, -diff)):
            value = np.exp(-u * u / (2.0 * sigma * sigma)) * (u / sigma) ** power / norm
            out.append(np.where(np.abs(u) <= KHALF, value, 0.0))
    return np.stack(ahead).astype(np.float32), np.stack(back).astype(np.float32)


def sinc(v):
    scaled = math.pi * jnp.where(v == 0.0, 1.0, v)
    return jnp.where(v == 0.0, 1.0, jnp.sin(scaled) / scaled)


def lanczos(offset):
    return jnp.where(jnp.abs(offset) < 3.0, sinc(offset) * sinc(offset / 3.0), 0.0)


def by_portion(p, values):
    return jnp.where(p == 0, values[0], jnp.where(p == 1, values[1], values[2]))


def toeplitz_blocks(strip):
    lane = lax.broadcasted_iota(jnp.int32, (8, 128), 1)
    rows = [strip if b == 0 else pltpu.roll(strip, 8 * b, 1) for b in range(16)]
    low = lane < 64
    zero = jnp.zeros_like(strip)
    left = [jnp.where(low, zero, rows[b]) for b in (0, 1)]
    right = [jnp.where(low, rows[b], zero) for b in (14, 15)]
    for b in (0, 1):
        rows[b] = jnp.where(low, rows[b], zero)
    for b in (14, 15):
        rows[b] = jnp.where(low, zero, rows[b])

    def pack(pair):
        return jnp.concatenate(pair, axis=0).astype(jnp.bfloat16)

    return [pack(rows[2 * i : 2 * i + 2]) for i in range(8)], pack(right), pack(left)


def write_square(strip, ref):
    diag, right, left = toeplitz_blocks(strip)
    for i in range(8):
        ref[16 * i : 16 * i + 16, 0:128] = diag[i]
        ref[128 + 16 * i : 144 + 16 * i, 128:256] = diag[i]
    ref[112:128, 128:256] = right
    ref[128:144, 0:128] = left


def kernel(
    tiles_hbm,
    whole_s,
    part_s,
    patch_s,
    weight_s,
    coeff_s,
    patch_v,
    weight_v,
    ahead,
    back,
    diff_hbm,
    coadd_out,
    tiles,
    warp,
    send1,
    recv1,
    sel,
    asend,
    arecv,
    bsend,
    brecv,
    gath,
    gathf,
    send4,
    recv4,
    csend,
    crecv,
    den,
    strips,
    fmat,
    mband,
    rmat,
    tbuf,
    hbuf,
    rows_s,
    s1,
    r1,
    sa,
    ra,
    sb,
    rb,
    sgb,
    rgb,
    sga,
    rga,
    s4,
    r4,
    sc,
    rc,
    in_sem,
    own1,
    own4,
    out_sem,
):
    visit, sky = lax.axis_index("visit"), lax.axis_index("sky")
    y, c = lax.div(visit, 2), lax.rem(visit, 2)
    z, x = lax.div(sky, 4), lax.rem(sky, 4)

    def dev(y_, c_, z_, x_):
        return (y_ * 2 + c_, z_ * 4 + x_)

    ring_of = (y, z, x)
    first_of, second_of = (x, y, z), (z, x, y)

    def on_ring(p, pos, core):
        return (dev(pos, core, z, x), dev(y, core, pos, x), dev(y, core, z, pos))[p]

    def on_first(p, pos):
        return (dev(y, c, z, pos), dev(pos, c, z, x), dev(y, c, pos, x))[p]

    def on_second(p, pos):
        return (dev(y, c, pos, x), dev(y, c, z, pos), dev(pos, c, z, x))[p]

    def partner(p, k):
        d, core = lax.div(k, 2), lax.rem(c + lax.rem(k, 2), 2)
        return lax.rem(ring_of[p] + d, 4), lax.rem(ring_of[p] + 4 - d, 4), core

    swap = (dev(z, c, y, x), dev(x, c, z, y))
    moved = (y != z, y != x)

    def fetch(g):
        return pltpu.make_async_copy(
            tiles_hbm.at[pl.ds(g * TG, TG)], tiles.at[pl.ds(g * TG, TG)], in_sem.at[g]
        )

    for g in range(GROUPS):
        fetch(g).start()

    barrier = pltpu.get_barrier_semaphore()
    pl.semaphore_signal(barrier, inc=1, device_id=dev(y, 1 - c, z, x), device_id_type=MESH)
    for p in range(3):

        @pl.loop(2, 8)
        def _(k, p=p):
            pos, unused, core = partner(p, k)
            pl.semaphore_signal(barrier, inc=1, device_id=on_ring(p, pos, core), device_id_type=MESH)

    for i in range(2):

        @pl.when(moved[i])
        def _(i=i):
            pl.semaphore_signal(barrier, inc=1, device_id=swap[i], device_id_type=MESH)

    lane = lax.broadcasted_iota(jnp.int32, (8, 128), 1)
    down = lax.broadcasted_iota(jnp.int32, (8, 128), 0)
    reach = jnp.where(lane < 64, lane, lane - 128).astype(jnp.float32)
    reach = jnp.where((down & 1) == 0, reach, -reach)

    @pl.loop(0, 4)
    def _(i):
        shift = jnp.zeros((8, 128), jnp.float32)
        for r in range(8):
            t = i * 4 + r // 2
            value = whole_s[r % 2, t].astype(jnp.float32) + part_s[r % 2, t]
            shift = jnp.where(down == r, value, shift)
        taps = lanczos(reach - shift)
        for r in range(8):
            row = jnp.broadcast_to(taps[r : r + 1], (8, 128))
            strips[i * 8 + r] = pltpu.roll(row, 0, 1, stride=1, stride_axis=0)

    @pl.loop(0, 4)
    def _(j):
        rmat[j] = jnp.zeros((SIDE, SIDE), jnp.bfloat16)

    def own_first(p, g):
        lo, hi = UNITS[p]
        return pltpu.make_async_copy(
            send1.at[g, ring_of[p] * 2 + c, pl.ds(lo, hi - lo)],
            recv1.at[g, 0, pl.ds(lo, hi - lo)],
            own1.at[p, g],
        )

    def first(p, g, k):
        lo, hi = UNITS[p]
        pos, unused, core = partner(p, k)
        return pltpu.make_async_remote_copy(
            src_ref=send1.at[g, pos * 2 + core, pl.ds(lo, hi - lo)],
            dst_ref=recv1.at[g, k, pl.ds(lo, hi - lo)],
            send_sem=s1.at[p, g, k - 1],
            recv_sem=r1.at[p, g, k - 1],
            device_id=on_ring(p, pos, core),
            device_id_type=MESH,
        )

    @pl.loop(0, GROUPS)
    def _(g):
        fetch(g).wait()

        @pl.loop(0, PG)
        def _(pair):
            scaled = []
            for half in range(2):
                t = g * TG + pair * 2 + half
                write_square(strips[2 * t], rmat.at[2 * half])
                write_square(strips[2 * t + 1], rmat.at[2 * half + 1])
                rowpass = jnp.dot(
                    tiles[t], rmat[2 * half + 1], preferred_element_type=jnp.float32
                ).astype(jnp.bfloat16)
                value = jnp.dot(rmat[2 * half], rowpass, preferred_element_type=jnp.float32)
                warp[t] = value
                scaled.append((weight_s[(visit * 16 + sky) * TILES_DEV + t] * value).reshape(32, 8, SIDE))
            both = jnp.concatenate(scaled, axis=1).astype(jnp.bfloat16)
            rows = pl.ds(pl.multiple_of(pair * 16, 16), 16)
            for q in range(8):
                for u in range(8):
                    send1[g, q, u, rows, :] = both[4 * q + u // 2, :, 128 * (u % 2) : 128 * (u % 2) + 128]

        @pl.when(g == 0)
        def _():
            pl.semaphore_wait(barrier, 19 + moved[0].astype(jnp.int32) + moved[1].astype(jnp.int32))

        @pl.loop(1, 8)
        def _(k):
            for p in range(3):
                first(p, g, k).start()

        for p in range(3):
            own_first(p, g).start()

    for p in range(3):

        @pl.loop(0, 8)
        def _(k, p=p):
            unused, pos, core = partner(p, k)
            v, s = on_ring(p, pos, core)
            base = (v * 16 + s) * TILES_DEV
            for g in range(GROUPS):
                for tt in range(TG):
                    patch = patch_s[base + g * TG + tt]
                    if p == 0:
                        patch = ((patch >> 2) & 3) * 16 + (patch >> 4) * 4 + (patch & 3)
                    rows_s[p, g * 8 * TG + k * TG + tt] = patch

    high = lax.broadcasted_iota(jnp.int32, (512, 128), 0)

    @pl.loop(0, 24)
    def _(n):
        p, m = lax.div(n, 8), lax.rem(n, 8)
        key = jnp.zeros((8, 128), jnp.int32)
        for tt in range(16):
            key = jnp.where((lane >> 3) == tt, rows_s[p, m * 16 + tt], key)
        key = key * 8 + (lane & 7)
        wide = jnp.broadcast_to(key[0:1], (512, 128))
        sel[p, :, pl.ds(pl.multiple_of(m * 128, 128), 128)] = jnp.where(wide == high, 1.0, 0.0).astype(
            jnp.bfloat16
        )

    @pl.loop(0, 12)
    def _(n):
        p, k = lax.div(n, 4), lax.rem(n, 4)
        owner = by_portion(p, (z * 4 + x, y * 4 + x, z * 4 + y))
        hit = jnp.where(patch_v[...] == owner * 4 + k, weight_v[...], 0.0)
        weight = jnp.sum(jnp.sum(hit, axis=0, keepdims=True), axis=1, keepdims=True)
        den[p, pl.ds(pl.multiple_of(k * 8, 8), 8)] = jnp.broadcast_to(1.0 + weight, (8, 128))

    @pl.loop(0, NF)
    def _(j):
        fmat[j] = jnp.zeros((SIDE, SIDE), jnp.bfloat16)
        write_square(ahead[j], fmat.at[j])

    @pl.loop(0, TILES_DEV)
    def _(t):
        for j in range(NF):
            strip = None
            for k in range(len(BASIS_COLS)):
                if BASIS_COLS[k] == j:
                    term = coeff_s[t, k] * back[BASIS_ROWS[k]]
                    strip = term if strip is None else strip + term
            diag, right, left = toeplitz_blocks(strip)
            cols = slice(128 * j, 128 * j + 128)
            mband[t, 0:16, cols] = right
            for i in range(8):
                mband[t, 16 + 16 * i : 32 + 16 * i, cols] = diag[i]
            mband[t, 144:160, cols] = left

    def second(p, d):
        lo, hi = UNITS[p]
        pos = lax.rem(first_of[p] + d, 4)
        return pltpu.make_async_remote_copy(
            src_ref=asend.at[pos, pl.ds(lo, hi - lo)],
            dst_ref=arecv.at[d - 1, pl.ds(lo, hi - lo)],
            send_sem=sa.at[p, d - 1],
            recv_sem=ra.at[p, d - 1],
            device_id=on_first(p, pos),
            device_id_type=MESH,
        )

    def third(p, d):
        lo, hi = UNITS[p]
        pos = lax.rem(second_of[p] + d, 4)
        return pltpu.make_async_remote_copy(
            src_ref=bsend.at[pos, pl.ds(lo, hi - lo)],
            dst_ref=brecv.at[d - 1, pl.ds(lo, hi - lo)],
            send_sem=sb.at[p, d - 1],
            recv_sem=rb.at[p, d - 1],
            device_id=on_second(p, pos),
            device_id_type=MESH,
        )

    def fourth(p, d):
        lo, hi = UNITS[p]
        mine = gath.at[first_of[p], second_of[p], pl.ds(lo, hi - lo)]
        return pltpu.make_async_remote_copy(
            src_ref=mine,
            dst_ref=mine,
            send_sem=sgb.at[p, d - 1],
            recv_sem=rgb.at[p, d - 1],
            device_id=on_second(p, lax.rem(second_of[p] + d, 4)),
            device_id_type=MESH,
        )

    def fifth(p, d):
        lo, hi = UNITS[p]
        mine = gath.at[first_of[p], :, pl.ds(lo, hi - lo)]
        return pltpu.make_async_remote_copy(
            src_ref=mine,
            dst_ref=mine,
            send_sem=sga.at[p, d - 1],
            recv_sem=rga.at[p, d - 1],
            device_id=on_first(p, lax.rem(first_of[p] + d, 4)),
            device_id_type=MESH,
        )

    def each_unit(before, body, after):
        @pl.loop(0, 8)
        def _(u):
            for p in range(3):

                @pl.when(u == UNITS[p][0])
                def _(p=p):
                    before(p)

            body(u, lax.div(u, 3))
            for p in range(3):

                @pl.when(u == UNITS[p][1] - 1)
                def _(p=p):
                    after(p)

    def all_three(act):
        @pl.loop(1, 4)
        def _(d):
            act(d)

    def arrived(p):
        @pl.loop(0, GROUPS)
        def _(g):
            own_first(p, g).wait()

            @pl.loop(1, 8)
            def _(k):
                first(p, g, k).wait_recv()

    def add_tiles(u, p):
        total = jnp.dot(sel[p], recv1[:, :, u].reshape(1024, 128), preferred_element_type=jnp.float32)
        asend[:, u] = total.astype(jnp.bfloat16).reshape(4, 128, 128)

    each_unit(arrived, add_tiles, lambda p: all_three(lambda d: second(p, d).start()))

    def add_first(u, p):
        total = asend[by_portion(p, first_of), u].astype(jnp.float32)
        for d in range(3):
            total = total + arecv[d, u].astype(jnp.float32)
        total = total.astype(jnp.bfloat16)
        for b in range(4):
            bsend[b, u] = total[32 * b : 32 * b + 32]

    each_unit(
        lambda p: all_three(lambda d: second(p, d).wait_recv()),
        add_first,
        lambda p: all_three(lambda d: third(p, d).start()),
    )

    def add_second(u, p):
        mine = by_portion(p, second_of)
        total = bsend[mine, u].astype(jnp.float32)
        for d in range(3):
            total = total + brecv[d, u].astype(jnp.float32)
        coadd = total / den[p]
        csend[u] = coadd
        gath[by_portion(p, first_of), mine, u] = coadd.astype(jnp.bfloat16)

    each_unit(
        lambda p: all_three(lambda d: third(p, d).wait_recv()),
        add_second,
        lambda p: all_three(lambda d: fourth(p, d).start()),
    )

    def to_owner(i):
        lo, hi = UNITS[i + 1]
        return pltpu.make_async_remote_copy(
            src_ref=csend.at[pl.ds(lo, hi - lo)],
            dst_ref=crecv.at[pl.ds(lo, hi - lo)],
            send_sem=sc.at[i],
            recv_sem=rc.at[i],
            device_id=swap[i],
            device_id_type=MESH,
        )

    for i in range(2):

        @pl.when(moved[i])
        def _(i=i):
            to_owner(i).start()

    for p in range(3):
        all_three(lambda d, p=p: fourth(p, d).wait_recv())
        all_three(lambda d, p=p: fifth(p, d).start())

    def own_last(p, g):
        lo, hi = UNITS[p]
        return pltpu.make_async_copy(
            send4.at[g, 0, pl.ds(lo, hi - lo)],
            recv4.at[g, ring_of[p] * 2 + c, pl.ds(lo, hi - lo)],
            own4.at[p, g],
        )

    def last(p, g, k):
        lo, hi = UNITS[p]
        unused, pos, core = partner(p, k)
        return pltpu.make_async_remote_copy(
            src_ref=send4.at[g, k, pl.ds(lo, hi - lo)],
            dst_ref=recv4.at[g, ring_of[p] * 2 + c, pl.ds(lo, hi - lo)],
            send_sem=s4.at[p, g, k - 1],
            recv_sem=r4.at[p, g, k - 1],
            device_id=on_ring(p, pos, core),
            device_id_type=MESH,
        )

    @pl.loop(0, GROUPS)
    def _(g):
        for p in range(3):
            lo, hi = UNITS[p]

            @pl.when(g == 0)
            def _(p=p, lo=lo, hi=hi):
                all_three(lambda d: fifth(p, d).wait_recv())

                @pl.loop(lo, hi)
                def _(u):
                    gathf[u] = gath[:, :, u].reshape(64, 8, 128).astype(jnp.float32)

            @pl.loop(0, 8)
            def _(k, p=p, lo=lo, hi=hi):
                for pair in range(PG):
                    at = g * 8 * TG + k * TG + 2 * pair
                    one, two = rows_s[p, at], rows_s[p, at + 1]
                    for u in range(lo, hi):
                        send4[g, k, u, 16 * pair : 16 * pair + 16, :] = jnp.concatenate(
                            [gathf[u, one], gathf[u, two]], axis=0
                        ).astype(jnp.bfloat16)

            @pl.loop(1, 8)
            def _(k, p=p):
                last(p, g, k).start()

            own_last(p, g).start()

    def leave(g, pair):
        t = g * TG + pair * 2
        return pltpu.make_async_copy(
            warp.at[pl.ds(t, 2)], diff_hbm.at[pl.ds(t, 2)], out_sem.at[g, pair]
        )

    @pl.loop(0, GROUPS)
    def _(g):
        for p in range(3):
            own_last(p, g).wait()

            @pl.loop(1, 8)
            def _(k, p=p):
                last(p, g, k).wait_recv()

        @pl.loop(0, PG)
        def _(pair):
            rows = pl.ds(pl.multiple_of(pair * 16, 16), 16)
            for q in range(8):
                for i in range(2):
                    for b in range(2):
                        upper = recv4[g, q, 4 * i + b, rows, :].astype(jnp.float32)
                        lower = recv4[g, q, 4 * i + 2 + b, rows, :].astype(jnp.float32)
                        at = 32 * q + 16 * i
                        cols = slice(128 * b, 128 * b + 128)
                        tbuf[at : at + 16, cols] = jnp.concatenate(
                            [upper[0:8], lower[0:8]], axis=0
                        ).astype(jnp.bfloat16)
                        tbuf[SIDE + at : SIDE + at + 16, cols] = jnp.concatenate(
                            [upper[8:16], lower[8:16]], axis=0
                        ).astype(jnp.bfloat16)
            for j in range(NF):
                filtered = jnp.dot(
                    tbuf[...], fmat[j], preferred_element_type=jnp.float32
                ).astype(jnp.bfloat16)
                for i in range(4):
                    hbuf[i, 128 * j : 128 * j + 128, :] = filtered[128 * i : 128 * i + 128]
            for half in range(2):
                t = g * TG + pair * 2 + half
                top = jnp.dot(
                    mband[t, 16:160, :], hbuf[2 * half], preferred_element_type=jnp.float32
                )
                low = jnp.dot(
                    mband[t, 0:144, :], hbuf[2 * half + 1], preferred_element_type=jnp.float32
                )
                warp[t, 0:112] = warp[t, 0:112] - top[0:112]
                warp[t, 112:144] = warp[t, 112:144] - (top[112:144] + low[0:32])
                warp[t, 144:256] = warp[t, 144:256] - low[32:144]
            leave(g, pair).start()

    for i in range(2):
        lo, hi = UNITS[i + 1]

        @pl.when(moved[i])
        def _(i=i):
            to_owner(i).wait()

        @pl.when(jnp.logical_not(moved[i]))
        def _(lo=lo, hi=hi):
            crecv[lo:hi] = csend[lo:hi]

    for u in range(8):
        held = csend if u < UNITS[0][1] else crecv
        for k in range(4):
            coadd_out[k, 8 * (u // 2) : 8 * (u // 2) + 8, 128 * (u % 2) : 128 * (u % 2) + 128] = held[
                u, 8 * k : 8 * k + 8
            ]

    for p in range(3):

        @pl.loop(0, GROUPS)
        def _(g, p=p):
            @pl.loop(1, 8)
            def _(k):
                first(p, g, k).wait_send()
                last(p, g, k).wait_send()

        @pl.loop(1, 4)
        def _(d, p=p):
            second(p, d).wait_send()
            third(p, d).wait_send()
            fourth(p, d).wait_send()
            fifth(p, d).wait_send()

    @pl.loop(0, GROUPS)
    def _(g):
        @pl.loop(0, PG)
        def _(pair):
            leave(g, pair).wait()


def shards(tiles, shift_int, shift_frac, tile_weight, tile_patch, al_coeff):
    ahead, back = factor_strips()
    vmem = pl.BlockSpec(memory_space=pltpu.VMEM)
    smem = pl.BlockSpec(memory_space=pltpu.SMEM)
    hbm = pl.BlockSpec(memory_space=pl.ANY)
    bf16, f32 = jnp.bfloat16, jnp.float32
    dma = pltpu.SemaphoreType.DMA
    block = (GROUPS, 8, 8, RB, 128)
    difference, coadd = pl.pallas_call(
        kernel,
        out_shape=(
            jax.ShapeDtypeStruct((TILES_DEV, SIDE, SIDE), f32),
            jax.ShapeDtypeStruct((4, 32, SIDE), f32),
        ),
        in_specs=[hbm, smem, smem, smem, smem, smem, vmem, vmem, vmem, vmem],
        out_specs=(hbm, vmem),
        scratch_shapes=[
            pltpu.VMEM((TILES_DEV, SIDE, SIDE), bf16),
            pltpu.VMEM((TILES_DEV, SIDE, SIDE), f32),
            pltpu.VMEM(block, bf16),
            pltpu.VMEM(block, bf16),
            pltpu.VMEM((3, 512, 1024), bf16),
            pltpu.VMEM((4, 8, 128, 128), bf16),
            pltpu.VMEM((3, 8, 128, 128), bf16),
            pltpu.VMEM((4, 8, 32, 128), bf16),
            pltpu.VMEM((3, 8, 32, 128), bf16),
            pltpu.VMEM((4, 4, 8, 32, 128), bf16),
            pltpu.VMEM((8, 64, 8, 128), f32),
            pltpu.VMEM(block, bf16),
            pltpu.VMEM(block, bf16),
            pltpu.VMEM((8, 32, 128), f32),
            pltpu.VMEM((8, 32, 128), f32),
            pltpu.VMEM((3, 32, 128), f32),
            pltpu.VMEM((2 * TILES_DEV, 8, 128), f32),
            pltpu.VMEM((NF, SIDE, SIDE), bf16),
            pltpu.VMEM((TILES_DEV, 160, 128 * NF), bf16),
            pltpu.VMEM((4, SIDE, SIDE), bf16),
            pltpu.VMEM((2 * SIDE, SIDE), bf16),
            pltpu.VMEM((4, 128 * NF, SIDE), bf16),
            pltpu.SMEM((3, 128), jnp.int32),
            dma((3, GROUPS, 7)),
            dma((3, GROUPS, 7)),
            dma((3, 3)),
            dma((3, 3)),
            dma((3, 3)),
            dma((3, 3)),
            dma((3, 3)),
            dma((3, 3)),
            dma((3, 3)),
            dma((3, 3)),
            dma((3, GROUPS, 7)),
            dma((3, GROUPS, 7)),
            dma((2,)),
            dma((2,)),
            dma((GROUPS,)),
            dma((3, GROUPS)),
            dma((3, GROUPS)),
            dma((GROUPS, PG)),
        ],
        compiler_params=pltpu.CompilerParams(
            collective_id=0, has_side_effects=True, vmem_limit_bytes=56 << 20
        ),
    )(
        tiles,
        shift_int.T,
        shift_frac.T,
        tile_patch,
        tile_weight,
        al_coeff,
        tile_patch.reshape(16, 128),
        tile_weight.reshape(16, 128),
        jnp.asarray(ahead),
        jnp.asarray(back),
    )
    return coadd, difference


def solution(mesh):
    return jax.shard_map(
        shards,
        mesh=mesh,
        in_specs=(
            P(("visit", "sky"), None, None),
            P(("visit", "sky"), None),
            P(("visit", "sky"), None),
            P(),
            P(),
            P(("visit", "sky"), None),
        ),
        out_specs=(P("sky", "visit", None), P(("visit", "sky"), None, None)),
        check_vma=False,
    )
```

```python
import functools
import math

import jax
import jax.numpy as jnp
import numpy as np
from jax import lax
from jax.experimental import pallas as pl
from jax.experimental.pallas import tpu as pltpu
from jax.sharding import PartitionSpec as P

MESH = pl.DeviceIdType.MESH
KHALF = 10
SIDE = 256
TILES_DEV = 16
SIGMAS = (1.0, 2.5, 5.0)
FACTORS = ((0, 0), (0, 1), (0, 2), (1, 0), (1, 1), (2, 0))
BASIS_ROWS = (0, 1, 0, 2, 0, 1, 3, 4, 3, 5)
BASIS_COLS = (0, 0, 1, 0, 2, 1, 3, 3, 4, 5)
NF = len(FACTORS)

SEGMENTS = ((0, 0, 2), (1, 2, 3), (2, 3, 4), (0, 4, 5), (1, 5, 7), (2, 7, 8))
FIRST_WAVE, SECOND_WAVE = (0, 1, 2), (3, 4, 5)
GROUPS = 2
TG = TILES_DEV // GROUPS
PG = TG // 2
RB = TG * 8


def wrapped_diff():
    diff = np.arange(128)[None, :] - np.arange(8)[:, None]
    return ((diff + 64) % 128) - 64


def factor_strips():
    diff = wrapped_diff().astype(np.float64)
    reach = np.arange(-KHALF, KHALF + 1).astype(np.float64)
    ahead, back = [], []
    for sigma_index, power in FACTORS:
        sigma = SIGMAS[sigma_index]
        norm = np.sum(np.exp(-reach * reach / (2.0 * sigma * sigma)))
        for out, u in ((ahead, diff), (back, -diff)):
            value = np.exp(-u * u / (2.0 * sigma * sigma)) * (u / sigma) ** power / norm
            out.append(np.where(np.abs(u) <= KHALF, value, 0.0))
    return np.stack(ahead).astype(np.float32), np.stack(back).astype(np.float32)


def sinc(v):
    scaled = math.pi * jnp.where(v == 0.0, 1.0, v)
    return jnp.where(v == 0.0, 1.0, jnp.sin(scaled) / scaled)


def lanczos(offset):
    return jnp.where(jnp.abs(offset) < 3.0, sinc(offset) * sinc(offset / 3.0), 0.0)


def by_portion(p, values):
    return jnp.where(p == 0, values[0], jnp.where(p == 1, values[1], values[2]))


def portion_of(u):
    return jnp.where((u == 3) | (u == 7), 2, jnp.where((u == 2) | (u == 5) | (u == 6), 1, 0))


def toeplitz_blocks(strip):
    lane = lax.broadcasted_iota(jnp.int32, (8, 128), 1)
    rows = [strip if b == 0 else pltpu.roll(strip, 8 * b, 1) for b in range(16)]
    low = lane < 64
    zero = jnp.zeros_like(strip)
    left = [jnp.where(low, zero, rows[b]) for b in (0, 1)]
    right = [jnp.where(low, rows[b], zero) for b in (14, 15)]
    for b in (0, 1):
        rows[b] = jnp.where(low, rows[b], zero)
    for b in (14, 15):
        rows[b] = jnp.where(low, zero, rows[b])

    def pack(pair):
        return jnp.concatenate(pair, axis=0).astype(jnp.bfloat16)

    return [pack(rows[2 * i : 2 * i + 2]) for i in range(8)], pack(right), pack(left)


def write_square(strip, ref):
    diag, right, left = toeplitz_blocks(strip)
    for i in range(8):
        ref[16 * i : 16 * i + 16, 0:128] = diag[i]
        ref[128 + 16 * i : 144 + 16 * i, 128:256] = diag[i]
    ref[112:128, 128:256] = right
    ref[128:144, 0:128] = left


def exchange(
    tiles_hbm,
    whole_s,
    part_s,
    coeff_s,
    patch_1d,
    weight_1d,
    patch_2d,
    weight_2d,
    back_hbm,
    warp_hbm,
    mband_hbm,
    recv4,
    coadd_hbm,
    tiles,
    warp,
    send1,
    recv1,
    sel,
    asend,
    arecv,
    bsend,
    brecv,
    gath,
    gathf,
    send4,
    cfull,
    crecv,
    hits,
    den,
    strips,
    mband,
    rmat,
    patch_v,
    weight_v,
    back,
    rows_s,
    patch_s,
    weight_s,
    s1,
    r1,
    s1b,
    r1b,
    sa,
    ra,
    sb,
    rb,
    sga,
    rga,
    s4,
    r4,
    sc,
    rc,
    in_sem,
    small_sem,
    own1,
    own4,
    out_sem,
):
    visit, sky = lax.axis_index("visit"), lax.axis_index("sky")
    y, c = lax.div(visit, 2), lax.rem(visit, 2)
    z, x = lax.div(sky, 4), lax.rem(sky, 4)

    def dev(y_, c_, z_, x_):
        return (y_ * 2 + c_, z_ * 4 + x_)

    ring_of = (y, z, x)
    first_of, second_of = (x, y, z), (z, x, y)

    def on_ring(p, pos, core):
        return (dev(pos, core, z, x), dev(y, core, pos, x), dev(y, core, z, pos))[p]

    def on_first(p, pos):
        return (dev(y, c, z, pos), dev(pos, c, z, x), dev(y, c, pos, x))[p]

    def on_second(p, pos):
        return (dev(y, c, pos, x), dev(y, c, z, pos), dev(pos, c, z, x))[p]

    def partner(p, k):
        d, core = lax.div(k, 2), lax.rem(c + lax.rem(k, 2), 2)
        return lax.rem(ring_of[p] + d, 4), lax.rem(ring_of[p] + 4 - d, 4), core

    swap = (dev(z, c, y, x), dev(x, c, z, y))
    moved = (y != z, y != x)

    def fetch(g):
        return pltpu.make_async_copy(
            tiles_hbm.at[pl.ds(g * TG, TG)], tiles.at[pl.ds(g * TG, TG)], in_sem.at[g]
        )

    small = [
        pltpu.make_async_copy(here, there, small_sem.at[i])
        for i, (here, there) in enumerate(
            (
                (weight_1d, weight_s),
                (patch_1d, patch_s),
                (patch_2d, patch_v),
                (weight_2d, weight_v),
                (back_hbm, back),
            )
        )
    ]

    barrier = pltpu.get_barrier_semaphore()
    pl.semaphore_signal(barrier, inc=1, device_id=dev(y, 1 - c, z, x), device_id_type=MESH)
    for p in range(3):

        @pl.loop(2, 8)
        def _(k, p=p):
            pos, unused, core = partner(p, k)
            pl.semaphore_signal(barrier, inc=1, device_id=on_ring(p, pos, core), device_id_type=MESH)

    for i in range(2):

        @pl.when(moved[i])
        def _(i=i):
            pl.semaphore_signal(barrier, inc=1, device_id=swap[i], device_id_type=MESH)

    for g in range(GROUPS):
        fetch(g).start()
    for copy in small:
        copy.start()

    lane = lax.broadcasted_iota(jnp.int32, (8, 128), 1)
    down = lax.broadcasted_iota(jnp.int32, (8, 128), 0)
    reach = jnp.where(lane < 64, lane, lane - 128).astype(jnp.float32)
    reach = jnp.where((down & 1) == 0, reach, -reach)

    @pl.loop(0, 4)
    def _(i):
        shift = jnp.zeros((8, 128), jnp.float32)
        for r in range(8):
            t = i * 4 + r // 2
            value = whole_s[r % 2, t].astype(jnp.float32) + part_s[r % 2, t]
            shift = jnp.where(down == r, value, shift)
        taps = lanczos(reach - shift)
        for r in range(8):
            row = jnp.broadcast_to(taps[r : r + 1], (8, 128))
            strips[i * 8 + r] = pltpu.roll(row, 0, 1, stride=1, stride_axis=0)

    @pl.loop(0, 4)
    def _(j):
        rmat[j] = jnp.zeros((SIDE, SIDE), jnp.bfloat16)

    def at_group(ref, g, slot, lo, hi):
        units = pl.ds(lo, hi - lo)
        return ref.at[:, slot, units] if g is None else ref.at[g, slot, units]

    def own_first(n, g):
        p, lo, hi = SEGMENTS[n]
        return pltpu.make_async_copy(
            at_group(send1, g, ring_of[p] * 2 + c, lo, hi),
            at_group(recv1, g, 0, lo, hi),
            own1.at[n, 0 if g is None else g],
        )

    def first(n, g, k):
        p, lo, hi = SEGMENTS[n]
        pos, unused, core = partner(p, k)
        return pltpu.make_async_remote_copy(
            src_ref=at_group(send1, g, pos * 2 + core, lo, hi),
            dst_ref=at_group(recv1, g, k, lo, hi),
            send_sem=s1b.at[p, k - 1] if g is None else s1.at[p, g, k - 1],
            recv_sem=r1b.at[p, k - 1] if g is None else r1.at[p, g, k - 1],
            device_id=on_ring(p, pos, core),
            device_id_type=MESH,
        )

    small[0].wait()

    @pl.loop(0, GROUPS)
    def _(g):
        fetch(g).wait()

        @pl.loop(0, PG)
        def _(pair):
            scaled = []
            for half in range(2):
                t = g * TG + pair * 2 + half
                write_square(strips[2 * t], rmat.at[2 * half])
                write_square(strips[2 * t + 1], rmat.at[2 * half + 1])
                rowpass = jnp.dot(
                    tiles[t], rmat[2 * half + 1], preferred_element_type=jnp.float32
                ).astype(jnp.bfloat16)
                value = jnp.dot(rmat[2 * half], rowpass, preferred_element_type=jnp.float32)
                warp[t] = value
                scaled.append((weight_s[(visit * 16 + sky) * TILES_DEV + t] * value).reshape(32, 8, SIDE))
            both = jnp.concatenate(scaled, axis=1).astype(jnp.bfloat16)
            rows = pl.ds(pl.multiple_of(pair * 16, 16), 16)
            for q in range(8):
                for u in range(8):
                    send1[g, q, u, rows, :] = both[4 * q + u // 2, :, 128 * (u % 2) : 128 * (u % 2) + 128]

        @pl.when(g == 0)
        def _():
            pl.semaphore_wait(barrier, 19 + moved[0].astype(jnp.int32) + moved[1].astype(jnp.int32))

        @pl.loop(1, 8)
        def _(k):
            for n in FIRST_WAVE:
                first(n, g, k).start()

        for n in FIRST_WAVE:
            own_first(n, g).start()

    @pl.loop(1, 8)
    def _(k):
        for n in SECOND_WAVE:
            first(n, None, k).start()

    for n in SECOND_WAVE:
        own_first(n, None).start()

    keep_warp = pltpu.make_async_copy(warp, warp_hbm, out_sem.at[0])
    keep_warp.start()
    for copy in small[1:]:
        copy.wait()

    for p in range(3):

        @pl.loop(0, 8)
        def _(k, p=p):
            unused, pos, core = partner(p, k)
            v, s = on_ring(p, pos, core)
            base = (v * 16 + s) * TILES_DEV
            for g in range(GROUPS):
                for tt in range(TG):
                    patch = patch_s[base + g * TG + tt]
                    if p == 0:
                        patch = ((patch >> 2) & 3) * 16 + (patch >> 4) * 4 + (patch & 3)
                    rows_s[p, g * 8 * TG + k * TG + tt] = patch

    high = lax.broadcasted_iota(jnp.int32, (512, 128), 0)

    @pl.loop(0, 24)
    def _(n):
        p, m = lax.div(n, 8), lax.rem(n, 8)
        key = jnp.zeros((8, 128), jnp.int32)
        for tt in range(16):
            key = jnp.where((lane >> 3) == tt, rows_s[p, m * 16 + tt], key)
        key = key * 8 + (lane & 7)
        wide = jnp.broadcast_to(key[0:1], (512, 128))
        sel[p, :, pl.ds(pl.multiple_of(m * 128, 128), 128)] = jnp.where(wide == high, 1.0, 0.0).astype(
            jnp.bfloat16
        )

    @pl.loop(0, 48)
    def _(n):
        p, second, k = lax.div(n, 16), lax.rem(lax.div(n, 4), 4), lax.rem(n, 4)
        owner = by_portion(p, (second * 4 + x, y * 4 + second, z * 4 + second))
        hit = jnp.where(patch_v[...] == owner * 4 + k, weight_v[...], 0.0)
        hits[n] = hit[0:8] + hit[8:16]

    weights = 1.0 + jnp.sum(jnp.sum(hits[...], axis=1), axis=1, keepdims=True)
    for n in range(48):
        den[n // 16, 8 * (n % 16) : 8 * (n % 16) + 8] = jnp.broadcast_to(weights[n : n + 1], (8, 128))

    @pl.loop(0, TILES_DEV)
    def _(t):
        for j in range(NF):
            strip = None
            for k in range(len(BASIS_COLS)):
                if BASIS_COLS[k] == j:
                    term = coeff_s[t, k] * back[BASIS_ROWS[k]]
                    strip = term if strip is None else strip + term
            diag, right, left = toeplitz_blocks(strip)
            cols = slice(128 * j, 128 * j + 128)
            mband[t, 0:16, cols] = right
            for i in range(8):
                mband[t, 16 + 16 * i : 32 + 16 * i, cols] = diag[i]
            mband[t, 144:160, cols] = left

    keep_mband = pltpu.make_async_copy(mband, mband_hbm, out_sem.at[1])
    keep_mband.start()

    def second(n, d):
        p, lo, hi = SEGMENTS[n]
        pos = lax.rem(first_of[p] + d, 4)
        return pltpu.make_async_remote_copy(
            src_ref=asend.at[pos, pl.ds(lo, hi - lo)],
            dst_ref=arecv.at[d - 1, pl.ds(lo, hi - lo)],
            send_sem=sa.at[n, d - 1],
            recv_sem=ra.at[n, d - 1],
            device_id=on_first(p, pos),
            device_id_type=MESH,
        )

    def third(n, d):
        p, lo, hi = SEGMENTS[n]
        return pltpu.make_async_remote_copy(
            src_ref=bsend.at[pl.ds(lo, hi - lo)],
            dst_ref=brecv.at[d - 1, pl.ds(lo, hi - lo)],
            send_sem=sb.at[n, d - 1],
            recv_sem=rb.at[n, d - 1],
            device_id=on_second(p, lax.rem(second_of[p] + d, 4)),
            device_id_type=MESH,
        )

    def fourth(n, d):
        p, lo, hi = SEGMENTS[n]
        mine = gath.at[first_of[p], pl.ds(lo, hi - lo)]
        return pltpu.make_async_remote_copy(
            src_ref=mine,
            dst_ref=mine,
            send_sem=sga.at[n, d - 1],
            recv_sem=rga.at[n, d - 1],
            device_id=on_first(p, lax.rem(first_of[p] + d, 4)),
            device_id_type=MESH,
        )

    def each_unit(before, body, after):
        @pl.loop(0, 8)
        def _(u):
            for n, (unused, lo, hi) in enumerate(SEGMENTS):

                @pl.when(u == lo)
                def _(n=n):
                    before(n)

            body(u, portion_of(u))
            for n, (unused, lo, hi) in enumerate(SEGMENTS):

                @pl.when(u == hi - 1)
                def _(n=n):
                    after(n)

    def all_three(act):
        @pl.loop(1, 4)
        def _(d):
            act(d)

    def arrived(n):
        if n in FIRST_WAVE:

            @pl.loop(0, GROUPS)
            def _(g):
                own_first(n, g).wait()

                @pl.loop(1, 8)
                def _(k):
                    first(n, g, k).wait_recv()

        else:
            own_first(n, None).wait()

            @pl.loop(1, 8)
            def _(k):
                first(n, None, k).wait_recv()

    def add_tiles(u, p):
        total = jnp.dot(sel[p], recv1[:, :, u].reshape(1024, 128), preferred_element_type=jnp.float32)
        asend[:, u] = total.astype(jnp.bfloat16).reshape(4, 128, 128)

    each_unit(arrived, add_tiles, lambda n: all_three(lambda d: second(n, d).start()))

    def add_first(u, p):
        total = asend[by_portion(p, first_of), u].astype(jnp.float32)
        for d in range(3):
            total = total + arecv[d, u].astype(jnp.float32)
        bsend[u] = total.astype(jnp.bfloat16)

    each_unit(
        lambda n: all_three(lambda d: second(n, d).wait_recv()),
        add_first,
        lambda n: all_three(lambda d: third(n, d).start()),
    )

    def add_second(u, p):
        total = bsend[u].astype(jnp.float32)
        for d in range(3):
            total = total + brecv[d, u].astype(jnp.float32)
        coadd = total / den[p]
        cfull[u] = coadd
        gath[by_portion(p, first_of), u] = coadd.astype(jnp.bfloat16)

    each_unit(
        lambda n: all_three(lambda d: third(n, d).wait_recv()),
        add_second,
        lambda n: all_three(lambda d: fourth(n, d).start()),
    )

    def kept(p):
        return pl.ds(pl.multiple_of(second_of[p] * 32, 32), 32)

    def to_owner(n):
        p, lo, hi = SEGMENTS[n]
        return pltpu.make_async_remote_copy(
            src_ref=cfull.at[pl.ds(lo, hi - lo), kept(p)],
            dst_ref=crecv.at[pl.ds(lo, hi - lo)],
            send_sem=sc.at[n],
            recv_sem=rc.at[n],
            device_id=swap[p - 1],
            device_id_type=MESH,
        )

    for n, (p, lo, hi) in enumerate(SEGMENTS):
        if p > 0:

            @pl.when(moved[p - 1])
            def _(n=n):
                to_owner(n).start()

    def own_last(n):
        p, lo, hi = SEGMENTS[n]
        return pltpu.make_async_copy(
            at_group(send4, None, 0, lo, hi),
            at_group(recv4, None, ring_of[p] * 2 + c, lo, hi),
            own4.at[n],
        )

    def last(n, k):
        p, lo, hi = SEGMENTS[n]
        unused, pos, core = partner(p, k)
        return pltpu.make_async_remote_copy(
            src_ref=at_group(send4, None, k, lo, hi),
            dst_ref=at_group(recv4, None, ring_of[p] * 2 + c, lo, hi),
            send_sem=s4.at[n, k - 1],
            recv_sem=r4.at[n, k - 1],
            device_id=on_ring(p, pos, core),
            device_id_type=MESH,
        )

    def templates_here(n):
        p, lo, hi = SEGMENTS[n]
        all_three(lambda d: fourth(n, d).wait_recv())

        @pl.loop(lo, hi)
        def _(u):
            gathf[u] = gath[:, u].reshape(64, 8, 128).astype(jnp.float32)

    def pick(n, g):
        p, lo, hi = SEGMENTS[n]

        @pl.loop(0, 8)
        def _(k):
            for pair in range(PG):
                at = g * 8 * TG + k * TG + 2 * pair
                one, two = rows_s[p, at], rows_s[p, at + 1]
                for u in range(lo, hi):
                    send4[g, k, u, 16 * pair : 16 * pair + 16, :] = jnp.concatenate(
                        [gathf[u, one], gathf[u, two]], axis=0
                    ).astype(jnp.bfloat16)

    for n in range(len(SEGMENTS)):
        templates_here(n)

        @pl.loop(0, GROUPS)
        def _(g, n=n):
            pick(n, g)

        @pl.loop(1, 8)
        def _(k, n=n):
            last(n, k).start()

        own_last(n).start()

    for n, (p, lo, hi) in enumerate(SEGMENTS):
        if p == 0:
            crecv[lo:hi] = cfull[lo:hi, kept(p)]
        else:

            @pl.when(moved[p - 1])
            def _(n=n):
                to_owner(n).wait()

            @pl.when(jnp.logical_not(moved[p - 1]))
            def _(p=p, lo=lo, hi=hi):
                crecv[lo:hi] = cfull[lo:hi, kept(p)]

    keep_coadd = pltpu.make_async_copy(crecv, coadd_hbm, out_sem.at[2])
    keep_coadd.start()

    for n in range(len(SEGMENTS)):
        own_last(n).wait()

    @pl.loop(1, 8)
    def _(k):
        for n in range(len(SEGMENTS)):
            last(n, k).wait()
        for n in SECOND_WAVE:
            first(n, None, k).wait_send()

        @pl.loop(0, GROUPS)
        def _(g):
            for n in FIRST_WAVE:
                first(n, g, k).wait_send()

    @pl.loop(1, 4)
    def _(d):
        for n in range(len(SEGMENTS)):
            second(n, d).wait_send()
            third(n, d).wait_send()
            fourth(n, d).wait_send()

    keep_warp.wait()
    keep_mband.wait()
    keep_coadd.wait()


def subtract(warp, mband, picked, ahead, coadd_units, diff, coadd, fmat, tbuf, hbuf):
    @pl.when(pl.program_id(0) == 0)
    def _():
        @pl.loop(0, NF)
        def _(j):
            fmat[j] = jnp.zeros((SIDE, SIDE), jnp.bfloat16)
            write_square(ahead[j], fmat.at[j])

        for u in range(8):
            for k in range(4):
                coadd[k, 8 * (u // 2) : 8 * (u // 2) + 8, 128 * (u % 2) : 128 * (u % 2) + 128] = (
                    coadd_units[u, 8 * k : 8 * k + 8]
                )

    @pl.loop(0, 2)
    def _(pair):
        rows = pl.ds(pl.multiple_of(pair * 16, 16), 16)
        for q in range(8):
            for i in range(2):
                for b in range(2):
                    upper = picked[0, q, 4 * i + b, rows, :].astype(jnp.float32)
                    lower = picked[0, q, 4 * i + 2 + b, rows, :].astype(jnp.float32)
                    at = 32 * q + 16 * i
                    cols = slice(128 * b, 128 * b + 128)
                    tbuf[at : at + 16, cols] = jnp.concatenate([upper[0:8], lower[0:8]], axis=0).astype(
                        jnp.bfloat16
                    )
                    tbuf[SIDE + at : SIDE + at + 16, cols] = jnp.concatenate(
                        [upper[8:16], lower[8:16]], axis=0
                    ).astype(jnp.bfloat16)
        for j in range(NF):
            filtered = jnp.dot(tbuf[...], fmat[j], preferred_element_type=jnp.float32).astype(jnp.bfloat16)
            for i in range(4):
                hbuf[i, 128 * j : 128 * j + 128, :] = filtered[128 * i : 128 * i + 128]
        for half in range(2):
            t = pair * 2 + half
            top = jnp.dot(mband[t, 16:160, :], hbuf[2 * half], preferred_element_type=jnp.float32)
            low = jnp.dot(mband[t, 0:144, :], hbuf[2 * half + 1], preferred_element_type=jnp.float32)
            diff[t, 0:112] = warp[t, 0:112] - top[0:112]
            diff[t, 112:144] = warp[t, 112:144] - (top[112:144] + low[0:32])
            diff[t, 144:256] = warp[t, 144:256] - low[32:144]


def shards(tiles, shift_int, shift_frac, tile_weight, tile_patch, al_coeff):
    ahead, back = factor_strips()
    smem = pl.BlockSpec(memory_space=pltpu.SMEM)
    hbm = pl.BlockSpec(memory_space=pl.ANY)
    bf16, f32, i32 = jnp.bfloat16, jnp.float32, jnp.int32
    dma = pltpu.SemaphoreType.DMA
    block = (GROUPS, 8, 8, RB, 128)
    warp, mband, picked, coadd_units = pl.pallas_call(
        exchange,
        out_shape=(
            jax.ShapeDtypeStruct((TILES_DEV, SIDE, SIDE), f32),
            jax.ShapeDtypeStruct((TILES_DEV, 160, 128 * NF), bf16),
            jax.ShapeDtypeStruct(block, bf16),
            jax.ShapeDtypeStruct((8, 32, 128), f32),
        ),
        in_specs=[hbm, smem, smem, smem, hbm, hbm, hbm, hbm, hbm],
        out_specs=(hbm, hbm, hbm, hbm),
        scratch_shapes=[
            pltpu.VMEM((TILES_DEV, SIDE, SIDE), bf16),
            pltpu.VMEM((TILES_DEV, SIDE, SIDE), f32),
            pltpu.VMEM(block, bf16),
            pltpu.VMEM(block, bf16),
            pltpu.VMEM((3, 512, 1024), bf16),
            pltpu.VMEM((4, 8, 128, 128), bf16),
            pltpu.VMEM((3, 8, 128, 128), bf16),
            pltpu.VMEM((8, 128, 128), bf16),
            pltpu.VMEM((3, 8, 128, 128), bf16),
            pltpu.VMEM((4, 8, 128, 128), bf16),
            pltpu.VMEM((8, 64, 8, 128), f32),
            pltpu.VMEM(block, bf16),
            pltpu.VMEM((8, 128, 128), f32),
            pltpu.VMEM((8, 32, 128), f32),
            pltpu.VMEM((48, 8, 128), f32),
            pltpu.VMEM((3, 128, 128), f32),
            pltpu.VMEM((2 * TILES_DEV, 8, 128), f32),
            pltpu.VMEM((TILES_DEV, 160, 128 * NF), bf16),
            pltpu.VMEM((4, SIDE, SIDE), bf16),
            pltpu.VMEM((16, 128), i32),
            pltpu.VMEM((16, 128), f32),
            pltpu.VMEM((NF, 8, 128), f32),
            pltpu.SMEM((3, 128), i32),
            pltpu.SMEM((2048,), i32),
            pltpu.SMEM((2048,), f32),
            dma((3, GROUPS, 7)),
            dma((3, GROUPS, 7)),
            dma((3, 7)),
            dma((3, 7)),
            dma((6, 3)),
            dma((6, 3)),
            dma((6, 3)),
            dma((6, 3)),
            dma((6, 3)),
            dma((6, 3)),
            dma((6, 7)),
            dma((6, 7)),
            dma((6,)),
            dma((6,)),
            dma((GROUPS,)),
            dma((5,)),
            dma((6, GROUPS)),
            dma((6,)),
            dma((3,)),
        ],
        compiler_params=pltpu.CompilerParams(
            collective_id=0, has_side_effects=True, vmem_limit_bytes=56 << 20
        ),
    )(
        tiles,
        shift_int.T,
        shift_frac.T,
        al_coeff,
        tile_patch,
        tile_weight,
        tile_patch.reshape(16, 128),
        tile_weight.reshape(16, 128),
        jnp.asarray(back),
    )
    per = TG // 4
    difference, coadd = pl.pallas_call(
        subtract,
        grid=(TILES_DEV // 4,),
        out_shape=(
            jax.ShapeDtypeStruct((TILES_DEV, SIDE, SIDE), f32),
            jax.ShapeDtypeStruct((4, 32, SIDE), f32),
        ),
        in_specs=[
            pl.BlockSpec((4, SIDE, SIDE), lambda i: (i, 0, 0)),
            pl.BlockSpec((4, 160, 128 * NF), lambda i: (i, 0, 0)),
            pl.BlockSpec((1, 8, 8, 32, 128), lambda i: (i // per, 0, 0, i % per, 0)),
            pl.BlockSpec((NF, 8, 128), lambda i: (0, 0, 0)),
            pl.BlockSpec((8, 32, 128), lambda i: (0, 0, 0)),
        ],
        out_specs=(
            pl.BlockSpec((4, SIDE, SIDE), lambda i: (i, 0, 0)),
            pl.BlockSpec((4, 32, SIDE), lambda i: (0, 0, 0)),
        ),
        scratch_shapes=[
            pltpu.VMEM((NF, SIDE, SIDE), bf16),
            pltpu.VMEM((2 * SIDE, SIDE), bf16),
            pltpu.VMEM((4, 128 * NF, SIDE), bf16),
        ],
        compiler_params=pltpu.CompilerParams(vmem_limit_bytes=60 << 20),
    )(warp, mband, picked, jnp.asarray(ahead), coadd_units)
    return coadd, difference


def solution(mesh):
    return jax.shard_map(
        shards,
        mesh=mesh,
        in_specs=(
            P(("visit", "sky"), None, None),
            P(("visit", "sky"), None),
            P(("visit", "sky"), None),
            P(),
            P(),
            P(("visit", "sky"), None),
        ),
        out_specs=(P("sky", "visit", None), P(("visit", "sky"), None, None)),
        check_vma=False,
    )
```

```python
import functools
import math

import jax
import jax.numpy as jnp
import numpy as np
from jax import lax
from jax.experimental import pallas as pl
from jax.experimental.pallas import tpu as pltpu
from jax.sharding import PartitionSpec as P

MESH = pl.DeviceIdType.MESH
KHALF = 10
SIDE = 256
TILES_DEV = 16
SIGMAS = (1.0, 2.5, 5.0)
FACTORS = ((0, 0), (0, 1), (0, 2), (1, 0), (1, 1), (2, 0))
BASIS_ROWS = (0, 1, 0, 2, 0, 1, 3, 4, 3, 5)
BASIS_COLS = (0, 0, 1, 0, 2, 1, 3, 3, 4, 5)
NF = len(FACTORS)

UNITS = 8
WAVES = 3


def wrapped_diff():
    diff = np.arange(128)[None, :] - np.arange(8)[:, None]
    return ((diff + 64) % 128) - 64


def factor_strips():
    diff = wrapped_diff().astype(np.float64)
    reach = np.arange(-KHALF, KHALF + 1).astype(np.float64)
    ahead, back = [], []
    for sigma_index, power in FACTORS:
        sigma = SIGMAS[sigma_index]
        norm = np.sum(np.exp(-reach * reach / (2.0 * sigma * sigma)))
        for out, u in ((ahead, diff), (back, -diff)):
            value = np.exp(-u * u / (2.0 * sigma * sigma)) * (u / sigma) ** power / norm
            out.append(np.where(np.abs(u) <= KHALF, value, 0.0))
    return np.stack(ahead).astype(np.float32), np.stack(back).astype(np.float32)


def sinc(v):
    scaled = math.pi * jnp.where(v == 0.0, 1.0, v)
    return jnp.where(v == 0.0, 1.0, jnp.sin(scaled) / scaled)


def lanczos(offset):
    return jnp.where(jnp.abs(offset) < 3.0, sinc(offset) * sinc(offset / 3.0), 0.0)


def by_portion(p, values):
    return jnp.where(p == 0, values[0], jnp.where(p == 1, values[1], values[2]))


def toeplitz_blocks(strip):
    lane = lax.broadcasted_iota(jnp.int32, (8, 128), 1)
    rows = [strip if b == 0 else pltpu.roll(strip, 8 * b, 1) for b in range(16)]
    low = lane < 64
    zero = jnp.zeros_like(strip)
    left = [jnp.where(low, zero, rows[b]) for b in (0, 1)]
    right = [jnp.where(low, rows[b], zero) for b in (14, 15)]
    for b in (0, 1):
        rows[b] = jnp.where(low, rows[b], zero)
    for b in (14, 15):
        rows[b] = jnp.where(low, zero, rows[b])

    def pack(pair):
        return jnp.concatenate(pair, axis=0).astype(jnp.bfloat16)

    return [pack(rows[2 * i : 2 * i + 2]) for i in range(8)], pack(right), pack(left)


def write_square(strip, ref):
    diag, right, left = toeplitz_blocks(strip)
    for i in range(8):
        ref[16 * i : 16 * i + 16, 0:128] = diag[i]
        ref[128 + 16 * i : 144 + 16 * i, 128:256] = diag[i]
    ref[112:128, 128:256] = right
    ref[128:144, 0:128] = left


def exchange(
    tiles_hbm,
    whole_s,
    part_s,
    patch_2d,
    weight_2d,
    warp_hbm,
    recv4,
    coadd_hbm,
    tiles,
    warp,
    send1,
    recv1,
    sel,
    selt,
    asend,
    arecv,
    bsend,
    brecv,
    gath,
    spread,
    send4,
    cfull,
    crecv,
    hits,
    den,
    strips,
    rmat,
    patch_v,
    weight_v,
    wcol,
    s1,
    r1,
    sa,
    ra,
    sb,
    rb,
    sga,
    rga,
    s4,
    r4,
    sc,
    rc,
    in_sem,
    small_sem,
    own1,
    own4,
    out_sem,
):
    visit, sky = lax.axis_index("visit"), lax.axis_index("sky")
    y, c = lax.div(visit, 2), lax.rem(visit, 2)
    z, x = lax.div(sky, 4), lax.rem(sky, 4)

    def dev(y_, c_, z_, x_):
        return (y_ * 2 + c_, z_ * 4 + x_)

    ring_of = (y, z, x)
    first_of, second_of = (x, y, z), (z, x, y)

    def on_ring(p, pos, core):
        return (dev(pos, core, z, x), dev(y, core, pos, x), dev(y, core, z, pos))[p]

    def on_first(p, pos):
        return (dev(y, c, z, pos), dev(pos, c, z, x), dev(y, c, pos, x))[p]

    def on_second(p, pos):
        return (dev(y, c, pos, x), dev(y, c, z, pos), dev(pos, c, z, x))[p]

    def partner(p, k):
        d, core = lax.div(k, 2), lax.rem(c + lax.rem(k, 2), 2)
        return lax.rem(ring_of[p] + d, 4), lax.rem(ring_of[p] + 4 - d, 4), core

    swap = (dev(z, c, y, x), dev(x, c, z, y))
    moved = (y != z, y != x)

    def fetch(i):
        half = pl.ds(i * (TILES_DEV // 2), TILES_DEV // 2)
        return pltpu.make_async_copy(tiles_hbm.at[half], tiles.at[half], in_sem.at[i])

    small = [
        pltpu.make_async_copy(here, there, small_sem.at[i])
        for i, (here, there) in enumerate(
            (
                (weight_2d, weight_v),
                (patch_2d, patch_v),
            )
        )
    ]

    barrier = pltpu.get_barrier_semaphore()
    pl.semaphore_signal(barrier, inc=1, device_id=dev(y, 1 - c, z, x), device_id_type=MESH)
    for p in range(3):

        @pl.loop(2, 8)
        def _(k, p=p):
            pos, unused, core = partner(p, k)
            pl.semaphore_signal(barrier, inc=1, device_id=on_ring(p, pos, core), device_id_type=MESH)

    for i in range(2):

        @pl.when(moved[i])
        def _(i=i):
            pl.semaphore_signal(barrier, inc=1, device_id=swap[i], device_id_type=MESH)

    for i in range(2):
        fetch(i).start()
    for copy in small:
        copy.start()

    lane = lax.broadcasted_iota(jnp.int32, (8, 128), 1)
    down = lax.broadcasted_iota(jnp.int32, (8, 128), 0)
    reach = jnp.where(lane < 64, lane, lane - 128).astype(jnp.float32)
    reach = jnp.where((down & 1) == 0, reach, -reach)

    @pl.loop(0, 4)
    def _(i):
        shift = jnp.zeros((8, 128), jnp.float32)
        for r in range(8):
            t = i * 4 + r // 2
            value = whole_s[r % 2, t].astype(jnp.float32) + part_s[r % 2, t]
            shift = jnp.where(down == r, value, shift)
        taps = lanczos(reach - shift)
        for r in range(8):
            row = jnp.broadcast_to(taps[r : r + 1], (8, 128))
            strips[i * 8 + r] = pltpu.roll(row, 0, 1, stride=1, stride_axis=0)

    @pl.loop(0, 4)
    def _(j):
        rmat[j] = jnp.zeros((SIDE, SIDE), jnp.bfloat16)

    def own_first(p, u):
        return pltpu.make_async_copy(send1.at[ring_of[p] * 2 + c, u], recv1.at[0, u], own1.at[u])

    def first(p, u, k):
        pos, unused, core = partner(p, k)
        return pltpu.make_async_remote_copy(
            src_ref=send1.at[pos * 2 + core, u],
            dst_ref=recv1.at[k, u],
            send_sem=s1.at[u],
            recv_sem=r1.at[u],
            device_id=on_ring(p, pos, core),
            device_id_type=MESH,
        )

    def start_wave(w):
        for p in range(3):
            u = 3 * w + p
            if u < UNITS:

                @pl.loop(0, 8)
                def _(q, u=u):
                    for r in range(8):
                        row = pl.ds(32 * q + 8 * (u // 2) + r, TILES_DEV, stride=SIDE)
                        send1[q, u, :, 128 * r : 128 * r + 128] = (wcol[...] * warp[u % 2, row]).astype(
                            jnp.bfloat16
                        )

                @pl.loop(1, 8)
                def _(k, p=p, u=u):
                    first(p, u, k).start()

                own_first(p, u).start()

    fetch(0).wait()

    @pl.loop(0, TILES_DEV // 2)
    def _(pair):
        @pl.when(pair == TILES_DEV // 4)
        def _():
            fetch(1).wait()

        for half in range(2):
            t = pair * 2 + half
            write_square(strips[2 * t], rmat.at[2 * half])
            write_square(strips[2 * t + 1], rmat.at[2 * half + 1])
            rowpass = jnp.dot(
                tiles[t], rmat[2 * half + 1], preferred_element_type=jnp.float32
            ).astype(jnp.bfloat16)
            value = jnp.dot(rmat[2 * half], rowpass, preferred_element_type=jnp.float32)
            for b in range(2):
                warp[b, pl.ds(pl.multiple_of(t * SIDE, SIDE), SIDE), :] = value[:, 128 * b : 128 * b + 128]

    small[0].wait()
    mine_row = weight_v[pl.ds(visit * 2 + lax.div(sky, 8), 1), :]
    mine_row = pltpu.roll(jnp.broadcast_to(mine_row, (8, 128)), lax.rem(128 - lax.rem(sky, 8) * 16, 128), 1)
    diagonal = lax.broadcasted_iota(jnp.int32, (TILES_DEV, 128), 0) == lax.broadcasted_iota(
        jnp.int32, (TILES_DEV, 128), 1
    )
    one_each = jnp.where(diagonal, jnp.broadcast_to(mine_row[0:1], (TILES_DEV, 128)), 0.0)
    wcol[...] = jnp.broadcast_to(jnp.sum(one_each, axis=1, keepdims=True), (TILES_DEV, 128))

    pl.semaphore_wait(barrier, 19 + moved[0].astype(jnp.int32) + moved[1].astype(jnp.int32))
    start_wave(0)

    keep_warp = pltpu.make_async_copy(warp, warp_hbm, out_sem.at[0])
    keep_warp.start()
    for copy in small[1:]:
        copy.wait()

    line = lax.broadcasted_iota(jnp.int32, (1, 128), 1)
    for p in range(3):
        key = jnp.zeros((1, 128), jnp.int32)
        for k in range(8):
            unused, pos, core = partner(p, k)
            v, s = on_ring(p, pos, core)
            found = jnp.broadcast_to(patch_v[pl.ds(v * 2 + lax.div(s, 8), 1), :], (8, 128))
            found = pltpu.roll(found, lax.rem(128 + 16 * k - lax.rem(s, 8) * 16, 128), 1)
            key = jnp.where((line >> 4) == k, found[0:1], key)
        if p == 0:
            key = ((key >> 2) & 3) * 16 + (key >> 4) * 4 + (key & 3)
        hot = jnp.where(
            jnp.broadcast_to(key, (128, 128)) == lax.broadcasted_iota(jnp.int32, (128, 128), 0), 1.0, 0.0
        )
        sel[p] = hot[0:64].astype(jnp.bfloat16)
        selt[p] = hot.T.astype(jnp.bfloat16)

    start_wave(1)

    @pl.loop(0, 48)
    def _(n):
        p, second, k = lax.div(n, 16), lax.rem(lax.div(n, 4), 4), lax.rem(n, 4)
        owner = by_portion(p, (second * 4 + x, y * 4 + second, z * 4 + second))
        hit = jnp.where(patch_v[...] == owner * 4 + k, weight_v[...], 0.0)
        hits[n] = hit[0:8] + hit[8:16]

    weights = 1.0 + jnp.sum(jnp.sum(hits[...], axis=1), axis=1, keepdims=True)
    for p in range(3):
        den[p] = jnp.broadcast_to(weights[16 * p : 16 * p + 16], (16, 128))

    start_wave(2)

    def second(p, u, d):
        pos = lax.rem(first_of[p] + d, 4)
        return pltpu.make_async_remote_copy(
            src_ref=asend.at[pos, u],
            dst_ref=arecv.at[d - 1, u],
            send_sem=sa.at[u],
            recv_sem=ra.at[u],
            device_id=on_first(p, pos),
            device_id_type=MESH,
        )

    def third(p, u, d):
        return pltpu.make_async_remote_copy(
            src_ref=bsend.at[u],
            dst_ref=brecv.at[d - 1, u],
            send_sem=sb.at[u],
            recv_sem=rb.at[u],
            device_id=on_second(p, lax.rem(second_of[p] + d, 4)),
            device_id_type=MESH,
        )

    def fourth(p, u, d):
        mine = gath.at[first_of[p], u]
        return pltpu.make_async_remote_copy(
            src_ref=mine,
            dst_ref=mine,
            send_sem=sga.at[u],
            recv_sem=rga.at[u],
            device_id=on_first(p, lax.rem(first_of[p] + d, 4)),
            device_id_type=MESH,
        )

    def to_owner(p, u):
        return pltpu.make_async_remote_copy(
            src_ref=cfull.at[u, second_of[p]],
            dst_ref=crecv.at[u],
            send_sem=sc.at[u],
            recv_sem=rc.at[u],
            device_id=swap[p - 1],
            device_id_type=MESH,
        )

    def own_last(p, u):
        return pltpu.make_async_copy(send4.at[0, u], recv4.at[ring_of[p] * 2 + c, u], own4.at[u])

    def last(p, u, k):
        unused, pos, core = partner(p, k)
        return pltpu.make_async_remote_copy(
            src_ref=send4.at[k, u],
            dst_ref=recv4.at[ring_of[p] * 2 + c, u],
            send_sem=s4.at[u],
            recv_sem=r4.at[u],
            device_id=on_ring(p, pos, core),
            device_id_type=MESH,
        )

    def each_unit(w, before, body, after):
        @pl.loop(0, 3)
        def _(i):
            u = 3 * w + i

            @pl.when(u < UNITS)
            def _():
                for p in range(3):

                    @pl.when(i == p)
                    def _(p=p):
                        before(p, u)

                body(u, i)
                for p in range(3):

                    @pl.when(i == p)
                    def _(p=p):
                        after(p, u)

    def all_three(act):
        @pl.loop(1, 4)
        def _(d):
            act(d)

    def all_seven(act):
        @pl.loop(1, 8)
        def _(k):
            act(k)

    def await_bytes(ref, sem):
        pltpu.make_async_copy(ref, ref, sem).wait()

    def seven(ref, u):
        return ref.at[pl.ds(1, 7), u]

    def three(ref, u):
        return ref.at[pl.ds(0, 3), u]

    def tiles_here(p, u):
        own_first(p, u).wait()
        await_bytes(seven(recv1, u), r1.at[u])

    def add_tiles(u, p):
        total = jnp.dot(sel[p], recv1[:, u].reshape(128, 1024), preferred_element_type=jnp.float32)
        asend[:, u] = total.astype(jnp.bfloat16).reshape(4, 16, 1024)

    def add_first(u, p):
        total = asend[by_portion(p, first_of), u].astype(jnp.float32)
        for d in range(3):
            total = total + arecv[d, u].astype(jnp.float32)
        bsend[u] = total.astype(jnp.bfloat16)

    def add_second(u, p):
        total = bsend[u].astype(jnp.float32)
        for d in range(3):
            total = total + brecv[d, u].astype(jnp.float32)
        coadd = total / jnp.concatenate([den[p]] * 8, axis=1)
        for b in range(4):
            cfull[u, b] = coadd[4 * b : 4 * b + 4]
        gath[by_portion(p, first_of), u] = coadd.astype(jnp.bfloat16)

    def templates_out(p, u):
        all_three(lambda d: fourth(p, u, d).start())
        if p > 0:

            @pl.when(moved[p - 1])
            def _():
                to_owner(p, u).start()

    def pick(u, p):
        found = jnp.dot(
            selt[p, :, 0:64], gath[:, u].reshape(64, 1024), preferred_element_type=jnp.float32
        )
        for r in range(8):
            spread[pl.ds(r, 128, stride=8), :] = found[:, 128 * r : 128 * r + 128]
        send4[:, u] = spread[...].astype(jnp.bfloat16).reshape(8, 128, 128)

    def picks_out(p, u):
        all_seven(lambda k: last(p, u, k).start())
        own_last(p, u).start()

    @pl.loop(0, WAVES + 3)
    def _(step):
        @pl.when(step < WAVES)
        def _():
            each_unit(
                step, tiles_here, add_tiles, lambda p, u: all_three(lambda d: second(p, u, d).start())
            )

        @pl.when((step >= 1) & (step < WAVES + 1))
        def _():
            each_unit(
                step - 1,
                lambda p, u: await_bytes(three(arecv, u), ra.at[u]),
                add_first,
                lambda p, u: all_three(lambda d: third(p, u, d).start()),
            )

        @pl.when((step >= 2) & (step < WAVES + 2))
        def _():
            each_unit(
                step - 2,
                lambda p, u: await_bytes(three(brecv, u), rb.at[u]),
                add_second,
                templates_out,
            )

        @pl.when(step >= 3)
        def _():
            each_unit(
                step - 3,
                lambda p, u: await_bytes(three(gath, u), rga.at[u]),
                pick,
                picks_out,
            )

    for u in range(UNITS):
        p = u % 3
        if p == 0:
            crecv[u] = cfull[u, second_of[p]]
        else:

            @pl.when(moved[p - 1])
            def _(p=p, u=u):
                to_owner(p, u).wait()

            @pl.when(jnp.logical_not(moved[p - 1]))
            def _(p=p, u=u):
                crecv[u] = cfull[u, second_of[p]]

    keep_coadd = pltpu.make_async_copy(crecv, coadd_hbm, out_sem.at[2])
    keep_coadd.start()

    @pl.loop(0, UNITS)
    def _(u):
        own_last(0, u).wait()
        await_bytes(seven(recv4, u), r4.at[u])
        await_bytes(seven(send4, u), s4.at[u])
        await_bytes(seven(send1, u), s1.at[u])
        await_bytes(three(asend, u), sa.at[u])
        await_bytes(three(brecv, u), sb.at[u])
        await_bytes(three(gath, u), sga.at[u])

    keep_warp.wait()
    keep_coadd.wait()


def subtract(coeff_s, warp, picked, ahead, back, coadd_units, diff, coadd, fmat, mband, tbuf, hbuf):
    @pl.when(pl.program_id(0) == 0)
    def _():
        @pl.loop(0, NF)
        def _(j):
            fmat[j] = jnp.zeros((SIDE, SIDE), jnp.bfloat16)
            write_square(ahead[j], fmat.at[j])

        @pl.loop(0, UNITS // 2)
        def _(rb):
            down = lax.broadcasted_iota(jnp.int32, (8, 128), 0)
            for cb in range(2):
                unit = coadd_units[2 * rb + cb]
                for k in range(4):
                    rows = jnp.zeros((8, 128), jnp.float32)
                    for r in range(8):
                        row = jnp.broadcast_to(unit[k : k + 1, 128 * r : 128 * r + 128], (8, 128))
                        rows = jnp.where(down == r, row, rows)
                    coadd[k, pl.ds(pl.multiple_of(rb * 8, 8), 8), 128 * cb : 128 * cb + 128] = rows

    @pl.loop(0, 2)
    def _(pair):
        rows = pl.ds(pl.multiple_of(pair * 16, 16), 16)
        for q in range(8):
            for i in range(2):
                for b in range(2):
                    upper = picked[q, 4 * i + b, rows, :].astype(jnp.float32)
                    lower = picked[q, 4 * i + 2 + b, rows, :].astype(jnp.float32)
                    at = 32 * q + 16 * i
                    cols = slice(128 * b, 128 * b + 128)
                    tbuf[at : at + 16, cols] = jnp.concatenate([upper[0:8], lower[0:8]], axis=0).astype(
                        jnp.bfloat16
                    )
                    tbuf[SIDE + at : SIDE + at + 16, cols] = jnp.concatenate(
                        [upper[8:16], lower[8:16]], axis=0
                    ).astype(jnp.bfloat16)
        for half in range(2):
            t = pl.program_id(0) * 4 + pair * 2 + half
            for j in range(NF):
                strip = None
                for k in range(len(BASIS_COLS)):
                    if BASIS_COLS[k] == j:
                        term = coeff_s[t, k] * back[BASIS_ROWS[k]]
                        strip = term if strip is None else strip + term
                diag, right, left = toeplitz_blocks(strip)
                cols = slice(128 * j, 128 * j + 128)
                mband[half, 0:16, cols] = right
                for i in range(8):
                    mband[half, 16 + 16 * i : 32 + 16 * i, cols] = diag[i]
                mband[half, 144:160, cols] = left
        for j in range(NF):
            filtered = jnp.dot(tbuf[...], fmat[j], preferred_element_type=jnp.float32).astype(jnp.bfloat16)
            for i in range(4):
                hbuf[i, 128 * j : 128 * j + 128, :] = filtered[128 * i : 128 * i + 128]
        for half in range(2):
            t = pair * 2 + half
            top = jnp.dot(mband[half, 16:160, :], hbuf[2 * half], preferred_element_type=jnp.float32)
            low = jnp.dot(mband[half, 0:144, :], hbuf[2 * half + 1], preferred_element_type=jnp.float32)
            whole = jnp.concatenate([top[0:112], top[112:144] + low[0:32], low[32:144]], axis=0)
            for b in range(2):
                cols = slice(128 * b, 128 * b + 128)
                diff[t, :, cols] = warp[b, pl.ds(pl.multiple_of(t * SIDE, SIDE), SIDE), :] - whole[:, cols]


def shards(tiles, shift_int, shift_frac, tile_weight, tile_patch, al_coeff):
    ahead, back = factor_strips()
    smem = pl.BlockSpec(memory_space=pltpu.SMEM)
    hbm = pl.BlockSpec(memory_space=pl.ANY)
    bf16, f32, i32 = jnp.bfloat16, jnp.float32, jnp.int32
    dma = pltpu.SemaphoreType.DMA
    lanes = (8, UNITS, TILES_DEV, 1024)
    block = (8, UNITS, TILES_DEV * 8, 128)
    warp, picked, coadd_units = pl.pallas_call(
        exchange,
        out_shape=(
            jax.ShapeDtypeStruct((2, TILES_DEV * SIDE, 128), f32),
            jax.ShapeDtypeStruct(block, bf16),
            jax.ShapeDtypeStruct((UNITS, 4, 1024), f32),
        ),
        in_specs=[hbm, smem, smem, hbm, hbm],
        out_specs=(hbm, hbm, hbm),
        scratch_shapes=[
            pltpu.VMEM((TILES_DEV, SIDE, SIDE), bf16),
            pltpu.VMEM((2, TILES_DEV * SIDE, 128), f32),
            pltpu.VMEM(lanes, bf16),
            pltpu.VMEM(lanes, bf16),
            pltpu.VMEM((3, 64, 128), bf16),
            pltpu.VMEM((3, 128, 128), bf16),
            pltpu.VMEM((4, UNITS, 16, 1024), bf16),
            pltpu.VMEM((3, UNITS, 16, 1024), bf16),
            pltpu.VMEM((UNITS, 16, 1024), bf16),
            pltpu.VMEM((3, UNITS, 16, 1024), bf16),
            pltpu.VMEM((4, UNITS, 16, 1024), bf16),
            pltpu.VMEM((1024, 128), f32),
            pltpu.VMEM(block, bf16),
            pltpu.VMEM((UNITS, 4, 4, 1024), f32),
            pltpu.VMEM((UNITS, 4, 1024), f32),
            pltpu.VMEM((48, 8, 128), f32),
            pltpu.VMEM((3, 16, 128), f32),
            pltpu.VMEM((2 * TILES_DEV, 8, 128), f32),
            pltpu.VMEM((4, SIDE, SIDE), bf16),
            pltpu.VMEM((16, 128), i32),
            pltpu.VMEM((16, 128), f32),
            pltpu.VMEM((TILES_DEV, 128), f32),
            dma((UNITS,)),
            dma((UNITS,)),
            dma((UNITS,)),
            dma((UNITS,)),
            dma((UNITS,)),
            dma((UNITS,)),
            dma((UNITS,)),
            dma((UNITS,)),
            dma((UNITS,)),
            dma((UNITS,)),
            dma((UNITS,)),
            dma((UNITS,)),
            dma((2,)),
            dma((2,)),
            dma((UNITS,)),
            dma((UNITS,)),
            dma((3,)),
        ],
        compiler_params=pltpu.CompilerParams(
            collective_id=0, has_side_effects=True, vmem_limit_bytes=56 << 20
        ),
    )(
        tiles,
        shift_int.T,
        shift_frac.T,
        tile_patch.reshape(16, 128),
        tile_weight.reshape(16, 128),
    )
    difference, coadd = pl.pallas_call(
        subtract,
        grid=(TILES_DEV // 4,),
        out_shape=(
            jax.ShapeDtypeStruct((TILES_DEV, SIDE, SIDE), f32),
            jax.ShapeDtypeStruct((4, 32, SIDE), f32),
        ),
        in_specs=[
            smem,
            pl.BlockSpec((2, 4 * SIDE, 128), lambda i: (0, i, 0)),
            pl.BlockSpec((8, UNITS, 32, 128), lambda i: (0, 0, i, 0)),
            pl.BlockSpec((NF, 8, 128), lambda i: (0, 0, 0)),
            pl.BlockSpec((NF, 8, 128), lambda i: (0, 0, 0)),
            pl.BlockSpec((UNITS, 4, 1024), lambda i: (0, 0, 0)),
        ],
        out_specs=(
            pl.BlockSpec((4, SIDE, SIDE), lambda i: (i, 0, 0)),
            pl.BlockSpec((4, 32, SIDE), lambda i: (0, 0, 0)),
        ),
        scratch_shapes=[
            pltpu.VMEM((NF, SIDE, SIDE), bf16),
            pltpu.VMEM((2, 160, 128 * NF), bf16),
            pltpu.VMEM((2 * SIDE, SIDE), bf16),
            pltpu.VMEM((4, 128 * NF, SIDE), bf16),
        ],
        compiler_params=pltpu.CompilerParams(vmem_limit_bytes=60 << 20),
    )(al_coeff, warp, picked, jnp.asarray(ahead), jnp.asarray(back), coadd_units)
    return coadd, difference


def solution(mesh):
    return jax.shard_map(
        shards,
        mesh=mesh,
        in_specs=(
            P(("visit", "sky"), None, None),
            P(("visit", "sky"), None),
            P(("visit", "sky"), None),
            P(),
            P(),
            P(("visit", "sky"), None),
        ),
        out_specs=(P("sky", "visit", None), P(("visit", "sky"), None, None)),
        check_vma=False,
    )
```

```python
import functools
import math

import jax
import jax.numpy as jnp
import numpy as np
from jax import lax
from jax.experimental import pallas as pl
from jax.experimental.pallas import tpu as pltpu
from jax.sharding import PartitionSpec as P

MESH = pl.DeviceIdType.MESH
KHALF = 10
SIDE = 256
TILES_DEV = 16
SIGMAS = (1.0, 2.5, 5.0)
FACTORS = ((0, 0), (0, 1), (0, 2), (1, 0), (1, 1), (2, 0))
BASIS_ROWS = (0, 1, 0, 2, 0, 1, 3, 4, 3, 5)
BASIS_COLS = (0, 0, 1, 0, 2, 1, 3, 3, 4, 5)
NF = len(FACTORS)

UNITS = 8
LAGS = (0, 5, 10, 15)


def wrapped_diff():
    diff = np.arange(128)[None, :] - np.arange(8)[:, None]
    return ((diff + 64) % 128) - 64


def factor_strips():
    diff = wrapped_diff().astype(np.float64)
    reach = np.arange(-KHALF, KHALF + 1).astype(np.float64)
    ahead, back = [], []
    for sigma_index, power in FACTORS:
        sigma = SIGMAS[sigma_index]
        norm = np.sum(np.exp(-reach * reach / (2.0 * sigma * sigma)))
        for out, u in ((ahead, diff), (back, -diff)):
            value = np.exp(-u * u / (2.0 * sigma * sigma)) * (u / sigma) ** power / norm
            out.append(np.where(np.abs(u) <= KHALF, value, 0.0))
    return np.stack(ahead).astype(np.float32), np.stack(back).astype(np.float32)


def sinc(v):
    scaled = math.pi * jnp.where(v == 0.0, 1.0, v)
    return jnp.where(v == 0.0, 1.0, jnp.sin(scaled) / scaled)


def lanczos(offset):
    return jnp.where(jnp.abs(offset) < 3.0, sinc(offset) * sinc(offset / 3.0), 0.0)


def by_portion(p, values):
    return jnp.where(p == 0, values[0], jnp.where(p == 1, values[1], values[2]))


def toeplitz_blocks(strip):
    lane = lax.broadcasted_iota(jnp.int32, (8, 128), 1)
    rows = [strip if b == 0 else pltpu.roll(strip, 8 * b, 1) for b in range(16)]
    low = lane < 64
    zero = jnp.zeros_like(strip)
    left = [jnp.where(low, zero, rows[b]) for b in (0, 1)]
    right = [jnp.where(low, rows[b], zero) for b in (14, 15)]
    for b in (0, 1):
        rows[b] = jnp.where(low, rows[b], zero)
    for b in (14, 15):
        rows[b] = jnp.where(low, zero, rows[b])

    def pack(pair):
        return jnp.concatenate(pair, axis=0).astype(jnp.bfloat16)

    return [pack(rows[2 * i : 2 * i + 2]) for i in range(8)], pack(right), pack(left)


def write_square(strip, ref):
    diag, right, left = toeplitz_blocks(strip)
    for i in range(8):
        ref[16 * i : 16 * i + 16, 0:128] = diag[i]
        ref[128 + 16 * i : 144 + 16 * i, 128:256] = diag[i]
    ref[112:128, 128:256] = right
    ref[128:144, 0:128] = left


def exchange(
    tiles_hbm,
    whole_hbm,
    part_hbm,
    patch_2d,
    weight_2d,
    warp_hbm,
    recv4,
    coadd_hbm,
    tiles,
    warp,
    send1,
    recv1,
    sel,
    selt,
    asend,
    arecv,
    bsend,
    brecv,
    gath,
    spread,
    send4,
    cfull,
    crecv,
    coadd,
    hits,
    den,
    strips,
    rmat,
    patch_v,
    weight_v,
    wcol,
    whole_s,
    part_s,
    s1,
    r1,
    sa,
    ra,
    sb,
    rb,
    sga,
    rga,
    s4,
    r4,
    sc,
    rc,
    in_sem,
    small_sem,
    own1,
    own4,
    out_sem,
):
    visit, sky = lax.axis_index("visit"), lax.axis_index("sky")
    y, c = lax.div(visit, 2), lax.rem(visit, 2)
    z, x = lax.div(sky, 4), lax.rem(sky, 4)

    def dev(y_, c_, z_, x_):
        return (y_ * 2 + c_, z_ * 4 + x_)

    ring_of = (y, z, x)
    first_of, second_of = (x, y, z), (z, x, y)

    def on_ring(p, pos, core):
        return (dev(pos, core, z, x), dev(y, core, pos, x), dev(y, core, z, pos))[p]

    def on_first(p, pos):
        return (dev(y, c, z, pos), dev(pos, c, z, x), dev(y, c, pos, x))[p]

    def on_second(p, pos):
        return (dev(y, c, pos, x), dev(y, c, z, pos), dev(pos, c, z, x))[p]

    def partner(p, k):
        d, core = lax.div(k, 2), lax.rem(c + lax.rem(k, 2), 2)
        return lax.rem(ring_of[p] + d, 4), lax.rem(ring_of[p] + 4 - d, 4), core

    swap = (dev(z, c, y, x), dev(x, c, z, y))
    moved = (y != z, y != x)

    def fetch(i):
        half = pl.ds(i * (TILES_DEV // 2), TILES_DEV // 2)
        return pltpu.make_async_copy(tiles_hbm.at[half], tiles.at[half], in_sem.at[i])

    small = [
        pltpu.make_async_copy(here, there, small_sem.at[i])
        for i, (here, there) in enumerate(
            (
                (weight_2d, weight_v),
                (patch_2d, patch_v),
                (whole_hbm, whole_s),
                (part_hbm, part_s),
            )
        )
    ]

    barrier = pltpu.get_barrier_semaphore()
    pl.semaphore_signal(barrier, inc=1, device_id=dev(y, 1 - c, z, x), device_id_type=MESH)
    for p in range(3):

        @pl.loop(2, 8)
        def _(k, p=p):
            pos, unused, core = partner(p, k)
            pl.semaphore_signal(barrier, inc=1, device_id=on_ring(p, pos, core), device_id_type=MESH)

    for i in range(2):

        @pl.when(moved[i])
        def _(i=i):
            pl.semaphore_signal(barrier, inc=1, device_id=swap[i], device_id_type=MESH)

    for copy in small:
        copy.start()
    for i in range(2):
        fetch(i).start()

    lane = lax.broadcasted_iota(jnp.int32, (8, 128), 1)
    down = lax.broadcasted_iota(jnp.int32, (8, 128), 0)
    reach = jnp.where(lane < 64, lane, lane - 128).astype(jnp.float32)
    reach = jnp.where((down & 1) == 0, reach, -reach)

    for copy in small[2:]:
        copy.wait()

    @pl.loop(0, 4)
    def _(i):
        shift = jnp.zeros((8, 128), jnp.float32)
        for r in range(8):
            t = i * 4 + r // 2
            value = whole_s[r % 2, t].astype(jnp.float32) + part_s[r % 2, t]
            shift = jnp.where(down == r, value, shift)
        taps = lanczos(reach - shift)
        for r in range(8):
            row = jnp.broadcast_to(taps[r : r + 1], (8, 128))
            strips[i * 8 + r] = pltpu.roll(row, 0, 1, stride=1, stride_axis=0)

    @pl.loop(0, 4)
    def _(j):
        rmat[j] = jnp.zeros((SIDE, SIDE), jnp.bfloat16)

    def own_first(p, u):
        return pltpu.make_async_copy(send1.at[ring_of[p] * 2 + c, u], recv1.at[0, u], own1.at[u])

    def first(p, u, k):
        pos, unused, core = partner(p, k)
        return pltpu.make_async_remote_copy(
            src_ref=send1.at[pos * 2 + core, u],
            dst_ref=recv1.at[k, u],
            send_sem=s1.at[u],
            recv_sem=r1.at[u],
            device_id=on_ring(p, pos, core),
            device_id_type=MESH,
        )

    def start_wave(w):
        for p in range(3):
            u = 3 * w + p
            if u < UNITS:

                @pl.loop(0, 8)
                def _(q, u=u):
                    for r in range(8):
                        row = pl.ds(32 * q + 8 * (u // 2) + r, TILES_DEV, stride=SIDE)
                        send1[q, u, :, 128 * r : 128 * r + 128] = (wcol[...] * warp[u % 2, row]).astype(
                            jnp.bfloat16
                        )

                @pl.loop(1, 8)
                def _(k, p=p, u=u):
                    first(p, u, k).start()

                own_first(p, u).start()

    fetch(0).wait()

    @pl.loop(0, TILES_DEV // 2)
    def _(pair):
        @pl.when(pair == TILES_DEV // 4)
        def _():
            fetch(1).wait()

        for half in range(2):
            t = pair * 2 + half
            write_square(strips[2 * t], rmat.at[2 * half])
            write_square(strips[2 * t + 1], rmat.at[2 * half + 1])
            rowpass = jnp.dot(
                tiles[t], rmat[2 * half + 1], preferred_element_type=jnp.float32
            ).astype(jnp.bfloat16)
            value = jnp.dot(rmat[2 * half], rowpass, preferred_element_type=jnp.float32)
            for b in range(2):
                warp[b, pl.ds(pl.multiple_of(t * SIDE, SIDE), SIDE), :] = value[:, 128 * b : 128 * b + 128]

    small[0].wait()
    mine_row = weight_v[pl.ds(visit * 2 + lax.div(sky, 8), 1), :]
    mine_row = pltpu.roll(jnp.broadcast_to(mine_row, (8, 128)), lax.rem(128 - lax.rem(sky, 8) * 16, 128), 1)
    diagonal = lax.broadcasted_iota(jnp.int32, (TILES_DEV, 128), 0) == lax.broadcasted_iota(
        jnp.int32, (TILES_DEV, 128), 1
    )
    one_each = jnp.where(diagonal, jnp.broadcast_to(mine_row[0:1], (TILES_DEV, 128)), 0.0)
    wcol[...] = jnp.broadcast_to(jnp.sum(one_each, axis=1, keepdims=True), (TILES_DEV, 128))

    pl.semaphore_wait(barrier, 19 + moved[0].astype(jnp.int32) + moved[1].astype(jnp.int32))
    start_wave(0)

    keep_warp = pltpu.make_async_copy(warp, warp_hbm, out_sem.at[0])
    keep_warp.start()
    small[1].wait()

    line = lax.broadcasted_iota(jnp.int32, (1, 128), 1)
    for p in range(3):
        key = jnp.zeros((1, 128), jnp.int32)
        for k in range(8):
            unused, pos, core = partner(p, k)
            v, s = on_ring(p, pos, core)
            found = jnp.broadcast_to(patch_v[pl.ds(v * 2 + lax.div(s, 8), 1), :], (8, 128))
            found = pltpu.roll(found, lax.rem(128 + 16 * k - lax.rem(s, 8) * 16, 128), 1)
            key = jnp.where((line >> 4) == k, found[0:1], key)
        if p == 0:
            key = ((key >> 2) & 3) * 16 + (key >> 4) * 4 + (key & 3)
        hot = jnp.where(
            jnp.broadcast_to(key, (128, 128)) == lax.broadcasted_iota(jnp.int32, (128, 128), 0), 1.0, 0.0
        )
        sel[p] = hot[0:64].astype(jnp.bfloat16)
        selt[p] = hot.T.astype(jnp.bfloat16)

    start_wave(1)

    @pl.loop(0, 48)
    def _(n):
        p, second, k = lax.div(n, 16), lax.rem(lax.div(n, 4), 4), lax.rem(n, 4)
        owner = by_portion(p, (second * 4 + x, y * 4 + second, z * 4 + second))
        hit = jnp.where(patch_v[...] == owner * 4 + k, weight_v[...], 0.0)
        hits[n] = hit[0:8] + hit[8:16]

    weights = 1.0 + jnp.sum(jnp.sum(hits[...], axis=1), axis=1, keepdims=True)
    for p in range(3):
        den[p] = jnp.broadcast_to(weights[16 * p : 16 * p + 16], (16, 128))

    start_wave(2)

    def second(p, u, d):
        pos = lax.rem(first_of[p] + d, 4)
        return pltpu.make_async_remote_copy(
            src_ref=asend.at[pos, u],
            dst_ref=arecv.at[d - 1, u],
            send_sem=sa.at[u],
            recv_sem=ra.at[u],
            device_id=on_first(p, pos),
            device_id_type=MESH,
        )

    def third(p, u, d):
        return pltpu.make_async_remote_copy(
            src_ref=bsend.at[u],
            dst_ref=brecv.at[d - 1, u],
            send_sem=sb.at[u],
            recv_sem=rb.at[u],
            device_id=on_second(p, lax.rem(second_of[p] + d, 4)),
            device_id_type=MESH,
        )

    def fourth(p, u, d):
        mine = gath.at[first_of[p], u]
        return pltpu.make_async_remote_copy(
            src_ref=mine,
            dst_ref=mine,
            send_sem=sga.at[u],
            recv_sem=rga.at[u],
            device_id=on_first(p, lax.rem(first_of[p] + d, 4)),
            device_id_type=MESH,
        )

    def to_owner(p, u):
        return pltpu.make_async_remote_copy(
            src_ref=cfull.at[u, second_of[p]],
            dst_ref=crecv.at[u],
            send_sem=sc.at[u],
            recv_sem=rc.at[u],
            device_id=swap[p - 1],
            device_id_type=MESH,
        )

    def own_last(p, u):
        return pltpu.make_async_copy(send4.at[0, u], recv4.at[ring_of[p] * 2 + c, u], own4.at[u])

    def last(p, u, k):
        unused, pos, core = partner(p, k)
        return pltpu.make_async_remote_copy(
            src_ref=send4.at[k, u],
            dst_ref=recv4.at[ring_of[p] * 2 + c, u],
            send_sem=s4.at[u],
            recv_sem=r4.at[u],
            device_id=on_ring(p, pos, core),
            device_id_type=MESH,
        )

    def one_unit(u, before, body, after):
        @pl.when((u >= 0) & (u < UNITS))
        def _():
            portion = lax.rem(u, 3)
            for p in range(3):

                @pl.when(portion == p)
                def _(p=p):
                    before(p, u)

            body(u, portion)
            for p in range(3):

                @pl.when(portion == p)
                def _(p=p):
                    after(p, u)

    def all_three(act):
        @pl.loop(1, 4)
        def _(d):
            act(d)

    def all_seven(act):
        @pl.loop(1, 8)
        def _(k):
            act(k)

    def await_bytes(ref, sem):
        pltpu.make_async_copy(ref, ref, sem).wait()

    def seven(ref, u):
        return ref.at[pl.ds(1, 7), u]

    def three(ref, u):
        return ref.at[pl.ds(0, 3), u]

    def tiles_here(p, u):
        own_first(p, u).wait()
        await_bytes(seven(recv1, u), r1.at[u])

    def add_tiles(u, p):
        total = jnp.dot(sel[p], recv1[:, u].reshape(128, 1024), preferred_element_type=jnp.float32)
        asend[:, u] = total.astype(jnp.bfloat16).reshape(4, 16, 1024)

    def add_first(u, p):
        total = asend[by_portion(p, first_of), u].astype(jnp.float32)
        for d in range(3):
            total = total + arecv[d, u].astype(jnp.float32)
        bsend[u] = total.astype(jnp.bfloat16)

    def add_second(u, p):
        total = bsend[u].astype(jnp.float32)
        for d in range(3):
            total = total + brecv[d, u].astype(jnp.float32)
        total = total / jnp.concatenate([den[p]] * 8, axis=1)
        for b in range(4):
            cfull[u, b] = total[4 * b : 4 * b + 4]
        gath[by_portion(p, first_of), u] = total.astype(jnp.bfloat16)

    def templates_out(p, u):
        all_three(lambda d: fourth(p, u, d).start())
        if p > 0:

            @pl.when(moved[p - 1])
            def _():
                to_owner(p, u).start()

    def pick(u, p):
        found = jnp.dot(
            selt[p, :, 0:64], gath[:, u].reshape(64, 1024), preferred_element_type=jnp.float32
        )
        for r in range(8):
            spread[pl.ds(r, 128, stride=8), :] = found[:, 128 * r : 128 * r + 128]
        send4[:, u] = spread[...].astype(jnp.bfloat16).reshape(8, 128, 128)

    def picks_out(p, u):
        all_seven(lambda k: last(p, u, k).start())
        own_last(p, u).start()

    @pl.loop(0, UNITS + LAGS[3])
    def _(step):
        one_unit(
            step - LAGS[0],
            tiles_here,
            add_tiles,
            lambda p, u: all_three(lambda d: second(p, u, d).start()),
        )
        one_unit(
            step - LAGS[1],
            lambda p, u: await_bytes(three(arecv, u), ra.at[u]),
            add_first,
            lambda p, u: all_three(lambda d: third(p, u, d).start()),
        )
        one_unit(
            step - LAGS[2],
            lambda p, u: await_bytes(three(brecv, u), rb.at[u]),
            add_second,
            templates_out,
        )
        one_unit(
            step - LAGS[3],
            lambda p, u: await_bytes(three(gath, u), rga.at[u]),
            pick,
            picks_out,
        )

    for u in range(UNITS):
        p = u % 3
        if p == 0:
            crecv[u] = cfull[u, second_of[p]]
        else:

            @pl.when(moved[p - 1])
            def _(p=p, u=u):
                to_owner(p, u).wait()

            @pl.when(jnp.logical_not(moved[p - 1]))
            def _(p=p, u=u):
                crecv[u] = cfull[u, second_of[p]]

    @pl.loop(0, UNITS // 2)
    def _(rb):
        for cb in range(2):
            unit = crecv[2 * rb + cb]
            for k in range(4):
                rows = jnp.zeros((8, 128), jnp.float32)
                for r in range(8):
                    row = jnp.broadcast_to(unit[k : k + 1, 128 * r : 128 * r + 128], (8, 128))
                    rows = jnp.where(down == r, row, rows)
                coadd[k, pl.ds(pl.multiple_of(rb * 8, 8), 8), 128 * cb : 128 * cb + 128] = rows

    keep_coadd = pltpu.make_async_copy(coadd, coadd_hbm, out_sem.at[2])
    keep_coadd.start()

    @pl.loop(0, UNITS)
    def _(u):
        own_last(0, u).wait()
        await_bytes(seven(recv4, u), r4.at[u])
        await_bytes(seven(send4, u), s4.at[u])
        await_bytes(seven(send1, u), s1.at[u])
        await_bytes(three(asend, u), sa.at[u])
        await_bytes(three(brecv, u), sb.at[u])
        await_bytes(three(gath, u), sga.at[u])

    keep_warp.wait()
    keep_coadd.wait()


def subtract(
    coeff_s,
    ahead_hbm,
    back_hbm,
    warp_hbm,
    picked_hbm,
    coadd_in,
    diff_hbm,
    coadd_out,
    ahead,
    back,
    warp,
    picked,
    diff,
    fmat,
    mband,
    tbuf,
    hbuf,
    strip_sem,
    in_sem,
    out_sem,
    coadd_sem,
):
    pairs = TILES_DEV // 2

    def enter(pair):
        chunk = (slice(None), slice(None), pl.ds(pair * 16, 16))
        rows = (slice(None), pl.ds(pair * 2 * SIDE, 2 * SIDE))
        return (
            pltpu.make_async_copy(picked_hbm.at[chunk], picked.at[chunk], in_sem.at[pair, 0]),
            pltpu.make_async_copy(warp_hbm.at[rows], warp.at[rows], in_sem.at[pair, 1]),
        )

    def leave(pair):
        here = pl.ds(pair * 2, 2)
        return pltpu.make_async_copy(diff.at[here], diff_hbm.at[here], out_sem.at[pair])

    strip_copies = (
        pltpu.make_async_copy(ahead_hbm, ahead, strip_sem.at[0]),
        pltpu.make_async_copy(back_hbm, back, strip_sem.at[1]),
    )
    for copy in strip_copies:
        copy.start()

    @pl.loop(0, pairs)
    def _(pair):
        for copy in enter(pair):
            copy.start()

    pass_coadd = pltpu.make_async_copy(coadd_in, coadd_out, coadd_sem)
    pass_coadd.start()
    for copy in strip_copies:
        copy.wait()

    @pl.loop(0, NF)
    def _(j):
        fmat[j] = jnp.zeros((SIDE, SIDE), jnp.bfloat16)
        write_square(ahead[j], fmat.at[j])

    def assemble(pair, slot):
        rows = pl.ds(pl.multiple_of(pair * 16, 16), 16)
        for q in range(8):
            for i in range(2):
                for b in range(2):
                    upper = picked[q, 4 * i + b, rows, :].astype(jnp.float32)
                    lower = picked[q, 4 * i + 2 + b, rows, :].astype(jnp.float32)
                    at = 32 * q + 16 * i
                    cols = slice(128 * b, 128 * b + 128)
                    tbuf[slot, at : at + 16, cols] = jnp.concatenate(
                        [upper[0:8], lower[0:8]], axis=0
                    ).astype(jnp.bfloat16)
                    tbuf[slot, SIDE + at : SIDE + at + 16, cols] = jnp.concatenate(
                        [upper[8:16], lower[8:16]], axis=0
                    ).astype(jnp.bfloat16)

    def mix(pair, slot):
        for half in range(2):
            t = pair * 2 + half
            for j in range(NF):
                strip = None
                for k in range(len(BASIS_COLS)):
                    if BASIS_COLS[k] == j:
                        term = coeff_s[t, k] * back[BASIS_ROWS[k]]
                        strip = term if strip is None else strip + term
                diag, right, left = toeplitz_blocks(strip)
                cols = slice(128 * j, 128 * j + 128)
                mband[slot, half, 0:16, cols] = right
                for i in range(8):
                    mband[slot, half, 16 + 16 * i : 32 + 16 * i, cols] = diag[i]
                mband[slot, half, 144:160, cols] = left

    def columns(slot):
        for j in range(NF):
            filtered = jnp.dot(tbuf[slot], fmat[j], preferred_element_type=jnp.float32).astype(jnp.bfloat16)
            for i in range(4):
                hbuf[slot, i, 128 * j : 128 * j + 128, :] = filtered[128 * i : 128 * i + 128]

    def rest(pair, slot):
        for half in range(2):
            t = pair * 2 + half
            top = jnp.dot(mband[slot, half, 16:160, :], hbuf[slot, 2 * half], preferred_element_type=jnp.float32)
            low = jnp.dot(
                mband[slot, half, 0:144, :], hbuf[slot, 2 * half + 1], preferred_element_type=jnp.float32
            )
            whole = jnp.concatenate([top[0:112], top[112:144] + low[0:32], low[32:144]], axis=0)
            for b in range(2):
                cols = slice(128 * b, 128 * b + 128)
                diff[t, :, cols] = warp[b, pl.ds(pl.multiple_of(t * SIDE, SIDE), SIDE), :] - whole[:, cols]
        leave(pair).start()

    @pl.loop(0, pairs // 2)
    def _(step):
        chosen = [step * 2 + slot for slot in range(2)]
        for pair in chosen:
            for copy in enter(pair):
                copy.wait()
        for slot, pair in enumerate(chosen):
            assemble(pair, slot)
            mix(pair, slot)
            columns(slot)
        for slot, pair in enumerate(chosen):
            rest(pair, slot)

    @pl.loop(0, pairs)
    def _(pair):
        leave(pair).wait()

    pass_coadd.wait()


def shards(tiles, shift_int, shift_frac, tile_weight, tile_patch, al_coeff):
    ahead, back = factor_strips()
    smem = pl.BlockSpec(memory_space=pltpu.SMEM)
    hbm = pl.BlockSpec(memory_space=pl.ANY)
    bf16, f32, i32 = jnp.bfloat16, jnp.float32, jnp.int32
    dma = pltpu.SemaphoreType.DMA
    lanes = (8, UNITS, TILES_DEV, 1024)
    block = (8, UNITS, TILES_DEV * 8, 128)
    warp, picked, coadd_units = pl.pallas_call(
        exchange,
        out_shape=(
            jax.ShapeDtypeStruct((2, TILES_DEV * SIDE, 128), f32),
            jax.ShapeDtypeStruct(block, bf16),
            jax.ShapeDtypeStruct((4, 32, SIDE), f32),
        ),
        in_specs=[hbm, hbm, hbm, hbm, hbm],
        out_specs=(hbm, hbm, hbm),
        scratch_shapes=[
            pltpu.VMEM((TILES_DEV, SIDE, SIDE), bf16),
            pltpu.VMEM((2, TILES_DEV * SIDE, 128), f32),
            pltpu.VMEM(lanes, bf16),
            pltpu.VMEM(lanes, bf16),
            pltpu.VMEM((3, 64, 128), bf16),
            pltpu.VMEM((3, 128, 128), bf16),
            pltpu.VMEM((4, UNITS, 16, 1024), bf16),
            pltpu.VMEM((3, UNITS, 16, 1024), bf16),
            pltpu.VMEM((UNITS, 16, 1024), bf16),
            pltpu.VMEM((3, UNITS, 16, 1024), bf16),
            pltpu.VMEM((4, UNITS, 16, 1024), bf16),
            pltpu.VMEM((1024, 128), f32),
            pltpu.VMEM(block, bf16),
            pltpu.VMEM((UNITS, 4, 4, 1024), f32),
            pltpu.VMEM((UNITS, 4, 1024), f32),
            pltpu.VMEM((4, 32, SIDE), f32),
            pltpu.VMEM((48, 8, 128), f32),
            pltpu.VMEM((3, 16, 128), f32),
            pltpu.VMEM((2 * TILES_DEV, 8, 128), f32),
            pltpu.VMEM((4, SIDE, SIDE), bf16),
            pltpu.VMEM((16, 128), i32),
            pltpu.VMEM((16, 128), f32),
            pltpu.VMEM((TILES_DEV, 128), f32),
            pltpu.SMEM((2, TILES_DEV), i32),
            pltpu.SMEM((2, TILES_DEV), f32),
            dma((UNITS,)),
            dma((UNITS,)),
            dma((UNITS,)),
            dma((UNITS,)),
            dma((UNITS,)),
            dma((UNITS,)),
            dma((UNITS,)),
            dma((UNITS,)),
            dma((UNITS,)),
            dma((UNITS,)),
            dma((UNITS,)),
            dma((UNITS,)),
            dma((2,)),
            dma((4,)),
            dma((UNITS,)),
            dma((UNITS,)),
            dma((3,)),
        ],
        compiler_params=pltpu.CompilerParams(
            collective_id=0, has_side_effects=True, vmem_limit_bytes=56 << 20
        ),
    )(
        tiles,
        shift_int.T,
        shift_frac.T,
        tile_patch.reshape(16, 128),
        tile_weight.reshape(16, 128),
    )
    difference, coadd = pl.pallas_call(
        subtract,
        out_shape=(
            jax.ShapeDtypeStruct((TILES_DEV, SIDE, SIDE), f32),
            jax.ShapeDtypeStruct((4, 32, SIDE), f32),
        ),
        in_specs=[smem, hbm, hbm, hbm, hbm, hbm],
        out_specs=(hbm, hbm),
        scratch_shapes=[
            pltpu.VMEM((NF, 8, 128), f32),
            pltpu.VMEM((NF, 8, 128), f32),
            pltpu.VMEM((2, TILES_DEV * SIDE, 128), f32),
            pltpu.VMEM(block, bf16),
            pltpu.VMEM((TILES_DEV, SIDE, SIDE), f32),
            pltpu.VMEM((NF, SIDE, SIDE), bf16),
            pltpu.VMEM((2, 2, 160, 128 * NF), bf16),
            pltpu.VMEM((2, 2 * SIDE, SIDE), bf16),
            pltpu.VMEM((2, 4, 128 * NF, SIDE), bf16),
            dma((2,)),
            dma((TILES_DEV // 2, 2)),
            dma((TILES_DEV // 2,)),
            dma,
        ],
        compiler_params=pltpu.CompilerParams(vmem_limit_bytes=60 << 20),
    )(al_coeff, jnp.asarray(ahead), jnp.asarray(back), warp, picked, coadd_units)
    return coadd, difference


def solution(mesh):
    return jax.shard_map(
        shards,
        mesh=mesh,
        in_specs=(
            P(("visit", "sky"), None, None),
            P(("visit", "sky"), None),
            P(("visit", "sky"), None),
            P(),
            P(),
            P(("visit", "sky"), None),
        ),
        out_specs=(P("sky", "visit", None), P(("visit", "sky"), None, None)),
        check_vma=False,
    )
```

```python
import functools
import math

import jax
import jax.numpy as jnp
import numpy as np
from jax import lax
from jax.experimental import pallas as pl
from jax.experimental.pallas import tpu as pltpu
from jax.sharding import PartitionSpec as P

MESH = pl.DeviceIdType.MESH
KHALF = 10
SIDE = 256
TILES_DEV = 16
SIGMAS = (1.0, 2.5, 5.0)
FACTORS = ((0, 0), (0, 1), (0, 2), (1, 0), (1, 1), (2, 0))
BASIS_ROWS = (0, 1, 0, 2, 0, 1, 3, 4, 3, 5)
BASIS_COLS = (0, 0, 1, 0, 2, 1, 3, 3, 4, 5)
NF = len(FACTORS)

UNITS = 8
LAGS = (0, 5, 10, 15)


def wrapped_diff():
    diff = np.arange(128)[None, :] - np.arange(8)[:, None]
    return ((diff + 64) % 128) - 64


def factor_strips():
    diff = wrapped_diff().astype(np.float64)
    reach = np.arange(-KHALF, KHALF + 1).astype(np.float64)
    ahead, back = [], []
    for sigma_index, power in FACTORS:
        sigma = SIGMAS[sigma_index]
        norm = np.sum(np.exp(-reach * reach / (2.0 * sigma * sigma)))
        for out, u in ((ahead, diff), (back, -diff)):
            value = np.exp(-u * u / (2.0 * sigma * sigma)) * (u / sigma) ** power / norm
            out.append(np.where(np.abs(u) <= KHALF, value, 0.0))
    return np.stack(ahead).astype(np.float32), np.stack(back).astype(np.float32)


def sinc(v):
    scaled = math.pi * jnp.where(v == 0.0, 1.0, v)
    return jnp.where(v == 0.0, 1.0, jnp.sin(scaled) / scaled)


def lanczos(offset):
    return jnp.where(jnp.abs(offset) < 3.0, sinc(offset) * sinc(offset / 3.0), 0.0)


def by_portion(p, values):
    return jnp.where(p == 0, values[0], jnp.where(p == 1, values[1], values[2]))


def toeplitz_blocks(strip):
    lane = lax.broadcasted_iota(jnp.int32, (8, 128), 1)
    rows = [strip if b == 0 else pltpu.roll(strip, 8 * b, 1) for b in range(16)]
    low = lane < 64
    zero = jnp.zeros_like(strip)
    left = [jnp.where(low, zero, rows[b]) for b in (0, 1)]
    right = [jnp.where(low, rows[b], zero) for b in (14, 15)]
    for b in (0, 1):
        rows[b] = jnp.where(low, rows[b], zero)
    for b in (14, 15):
        rows[b] = jnp.where(low, zero, rows[b])

    def pack(pair):
        return jnp.concatenate(pair, axis=0).astype(jnp.bfloat16)

    return [pack(rows[2 * i : 2 * i + 2]) for i in range(8)], pack(right), pack(left)


def write_square(strip, ref):
    diag, right, left = toeplitz_blocks(strip)
    for i in range(8):
        ref[16 * i : 16 * i + 16, 0:128] = diag[i]
        ref[128 + 16 * i : 144 + 16 * i, 128:256] = diag[i]
    ref[112:128, 128:256] = right
    ref[128:144, 0:128] = left


def exchange(
    tiles_hbm,
    whole_hbm,
    part_hbm,
    patch_2d,
    weight_2d,
    warp_hbm,
    recv4,
    coadd_hbm,
    tiles,
    warp,
    send1,
    recv1,
    sel,
    selt,
    asend,
    arecv,
    bsend,
    brecv,
    gath,
    spread,
    send4,
    cfull,
    crecv,
    coadd,
    hits,
    den,
    strips,
    rmat,
    patch_v,
    weight_v,
    wcol,
    whole_s,
    part_s,
    s1,
    r1,
    sa,
    ra,
    sb,
    rb,
    sga,
    rga,
    s4,
    r4,
    sc,
    rc,
    in_sem,
    small_sem,
    own1,
    own4,
    out_sem,
):
    visit, sky = lax.axis_index("visit"), lax.axis_index("sky")
    y, c = lax.div(visit, 2), lax.rem(visit, 2)
    z, x = lax.div(sky, 4), lax.rem(sky, 4)

    def dev(y_, c_, z_, x_):
        return (y_ * 2 + c_, z_ * 4 + x_)

    ring_of = (y, z, x)
    first_of, second_of = (x, y, z), (z, x, y)

    def on_ring(p, pos, core):
        return (dev(pos, core, z, x), dev(y, core, pos, x), dev(y, core, z, pos))[p]

    def on_first(p, pos):
        return (dev(y, c, z, pos), dev(pos, c, z, x), dev(y, c, pos, x))[p]

    def on_second(p, pos):
        return (dev(y, c, pos, x), dev(y, c, z, pos), dev(pos, c, z, x))[p]

    def partner(p, k):
        d, core = lax.div(k, 2), lax.rem(c + lax.rem(k, 2), 2)
        return lax.rem(ring_of[p] + d, 4), lax.rem(ring_of[p] + 4 - d, 4), core

    swap = (dev(z, c, y, x), dev(x, c, z, y))
    moved = (y != z, y != x)

    def fetch(i):
        half = pl.ds(i * (TILES_DEV // 2), TILES_DEV // 2)
        return pltpu.make_async_copy(tiles_hbm.at[half], tiles.at[half], in_sem.at[i])

    small = [
        pltpu.make_async_copy(here, there, small_sem.at[i])
        for i, (here, there) in enumerate(
            (
                (weight_2d, weight_v),
                (patch_2d, patch_v),
                (whole_hbm, whole_s),
                (part_hbm, part_s),
            )
        )
    ]

    barrier = pltpu.get_barrier_semaphore()
    pl.semaphore_signal(barrier, inc=1, device_id=dev(y, 1 - c, z, x), device_id_type=MESH)
    for p in range(3):

        @pl.loop(2, 8)
        def _(k, p=p):
            pos, unused, core = partner(p, k)
            pl.semaphore_signal(barrier, inc=1, device_id=on_ring(p, pos, core), device_id_type=MESH)

    for i in range(2):

        @pl.when(moved[i])
        def _(i=i):
            pl.semaphore_signal(barrier, inc=1, device_id=swap[i], device_id_type=MESH)

    for copy in small:
        copy.start()
    for i in range(2):
        fetch(i).start()

    lane = lax.broadcasted_iota(jnp.int32, (8, 128), 1)
    down = lax.broadcasted_iota(jnp.int32, (8, 128), 0)
    reach = jnp.where(lane < 64, lane, lane - 128).astype(jnp.float32)
    reach = jnp.where((down & 1) == 0, reach, -reach)

    for copy in small[2:]:
        copy.wait()

    @pl.loop(0, 4)
    def _(i):
        shift = jnp.zeros((8, 128), jnp.float32)
        for r in range(8):
            t = i * 4 + r // 2
            value = whole_s[r % 2, t].astype(jnp.float32) + part_s[r % 2, t]
            shift = jnp.where(down == r, value, shift)
        taps = lanczos(reach - shift)
        for r in range(8):
            row = jnp.broadcast_to(taps[r : r + 1], (8, 128))
            strips[i * 8 + r] = pltpu.roll(row, 0, 1, stride=1, stride_axis=0)

    @pl.loop(0, 16)
    def _(j):
        rmat[j] = jnp.zeros((SIDE, SIDE), jnp.bfloat16)

    def own_first(p, u):
        return pltpu.make_async_copy(send1.at[ring_of[p] * 2 + c, u], recv1.at[0, u], own1.at[u])

    def first(p, u, k):
        pos, unused, core = partner(p, k)
        return pltpu.make_async_remote_copy(
            src_ref=send1.at[pos * 2 + core, u],
            dst_ref=recv1.at[k, u],
            send_sem=s1.at[u],
            recv_sem=r1.at[u],
            device_id=on_ring(p, pos, core),
            device_id_type=MESH,
        )

    def start_wave(w):
        for p in range(3):
            u = 3 * w + p
            if u < UNITS:

                @pl.loop(0, 8)
                def _(q, u=u):
                    for r in range(8):
                        row = pl.ds(32 * q + 8 * (u // 2) + r, TILES_DEV, stride=SIDE)
                        send1[q, u, :, 128 * r : 128 * r + 128] = (wcol[...] * warp[u % 2, row]).astype(
                            jnp.bfloat16
                        )

                @pl.loop(1, 8)
                def _(k, p=p, u=u):
                    first(p, u, k).start()

                own_first(p, u).start()

    fetch(0).wait()

    @pl.loop(0, TILES_DEV // 8)
    def _(octet):
        @pl.when(octet == TILES_DEV // 16)
        def _():
            fetch(1).wait()

        for i in range(8):
            t = octet * 8 + i
            write_square(strips[2 * t], rmat.at[2 * i])
            write_square(strips[2 * t + 1], rmat.at[2 * i + 1])
        rowpasses = [
            jnp.dot(tiles[octet * 8 + i], rmat[2 * i + 1], preferred_element_type=jnp.float32).astype(
                jnp.bfloat16
            )
            for i in range(8)
        ]
        for i in range(8):
            value = jnp.dot(rmat[2 * i], rowpasses[i], preferred_element_type=jnp.float32)
            rows = pl.ds(pl.multiple_of((octet * 8 + i) * SIDE, SIDE), SIDE)
            for b in range(2):
                warp[b, rows, :] = value[:, 128 * b : 128 * b + 128]

    small[0].wait()
    mine_row = weight_v[pl.ds(visit * 2 + lax.div(sky, 8), 1), :]
    mine_row = pltpu.roll(jnp.broadcast_to(mine_row, (8, 128)), lax.rem(128 - lax.rem(sky, 8) * 16, 128), 1)
    diagonal = lax.broadcasted_iota(jnp.int32, (TILES_DEV, 128), 0) == lax.broadcasted_iota(
        jnp.int32, (TILES_DEV, 128), 1
    )
    one_each = jnp.where(diagonal, jnp.broadcast_to(mine_row[0:1], (TILES_DEV, 128)), 0.0)
    wcol[...] = jnp.broadcast_to(jnp.sum(one_each, axis=1, keepdims=True), (TILES_DEV, 128))

    pl.semaphore_wait(barrier, 19 + moved[0].astype(jnp.int32) + moved[1].astype(jnp.int32))
    start_wave(0)

    keep_warp = pltpu.make_async_copy(warp, warp_hbm, out_sem.at[0])
    keep_warp.start()
    small[1].wait()

    line = lax.broadcasted_iota(jnp.int32, (1, 128), 1)
    for p in range(3):
        key = jnp.zeros((1, 128), jnp.int32)
        for k in range(8):
            unused, pos, core = partner(p, k)
            v, s = on_ring(p, pos, core)
            found = jnp.broadcast_to(patch_v[pl.ds(v * 2 + lax.div(s, 8), 1), :], (8, 128))
            found = pltpu.roll(found, lax.rem(128 + 16 * k - lax.rem(s, 8) * 16, 128), 1)
            key = jnp.where((line >> 4) == k, found[0:1], key)
        if p == 0:
            key = ((key >> 2) & 3) * 16 + (key >> 4) * 4 + (key & 3)
        hot = jnp.where(
            jnp.broadcast_to(key, (128, 128)) == lax.broadcasted_iota(jnp.int32, (128, 128), 0), 1.0, 0.0
        )
        sel[p] = hot[0:64].astype(jnp.bfloat16)
        selt[p] = hot.T.astype(jnp.bfloat16)

    start_wave(1)

    @pl.loop(0, 48)
    def _(n):
        p, second, k = lax.div(n, 16), lax.rem(lax.div(n, 4), 4), lax.rem(n, 4)
        owner = by_portion(p, (second * 4 + x, y * 4 + second, z * 4 + second))
        hit = jnp.where(patch_v[...] == owner * 4 + k, weight_v[...], 0.0)
        hits[n] = hit[0:8] + hit[8:16]

    weights = 1.0 + jnp.sum(jnp.sum(hits[...], axis=1), axis=1, keepdims=True)
    for p in range(3):
        den[p] = jnp.broadcast_to(weights[16 * p : 16 * p + 16], (16, 128))

    start_wave(2)

    def second(p, u, d):
        pos = lax.rem(first_of[p] + d, 4)
        return pltpu.make_async_remote_copy(
            src_ref=asend.at[pos, u],
            dst_ref=arecv.at[d - 1, u],
            send_sem=sa.at[u],
            recv_sem=ra.at[u],
            device_id=on_first(p, pos),
            device_id_type=MESH,
        )

    def third(p, u, d):
        return pltpu.make_async_remote_copy(
            src_ref=bsend.at[u],
            dst_ref=brecv.at[d - 1, u],
            send_sem=sb.at[u],
            recv_sem=rb.at[u],
            device_id=on_second(p, lax.rem(second_of[p] + d, 4)),
            device_id_type=MESH,
        )

    def fourth(p, u, d):
        mine = gath.at[first_of[p], u]
        return pltpu.make_async_remote_copy(
            src_ref=mine,
            dst_ref=mine,
            send_sem=sga.at[u],
            recv_sem=rga.at[u],
            device_id=on_first(p, lax.rem(first_of[p] + d, 4)),
            device_id_type=MESH,
        )

    def to_owner(p, u):
        return pltpu.make_async_remote_copy(
            src_ref=cfull.at[u, second_of[p]],
            dst_ref=crecv.at[u],
            send_sem=sc.at[u],
            recv_sem=rc.at[u],
            device_id=swap[p - 1],
            device_id_type=MESH,
        )

    def own_last(p, u):
        return pltpu.make_async_copy(send4.at[0, u], recv4.at[ring_of[p] * 2 + c, u], own4.at[u])

    def last(p, u, k):
        unused, pos, core = partner(p, k)
        return pltpu.make_async_remote_copy(
            src_ref=send4.at[k, u],
            dst_ref=recv4.at[ring_of[p] * 2 + c, u],
            send_sem=s4.at[u],
            recv_sem=r4.at[u],
            device_id=on_ring(p, pos, core),
            device_id_type=MESH,
        )

    def one_unit(u, before, body, after):
        @pl.when((u >= 0) & (u < UNITS))
        def _():
            portion = lax.rem(u, 3)
            for p in range(3):

                @pl.when(portion == p)
                def _(p=p):
                    before(p, u)

            body(u, portion)
            for p in range(3):

                @pl.when(portion == p)
                def _(p=p):
                    after(p, u)

    def all_three(act):
        @pl.loop(1, 4)
        def _(d):
            act(d)

    def all_seven(act):
        @pl.loop(1, 8)
        def _(k):
            act(k)

    def await_bytes(ref, sem):
        pltpu.make_async_copy(ref, ref, sem).wait()

    def seven(ref, u):
        return ref.at[pl.ds(1, 7), u]

    def three(ref, u):
        return ref.at[pl.ds(0, 3), u]

    def tiles_here(p, u):
        own_first(p, u).wait()
        await_bytes(seven(recv1, u), r1.at[u])

    def add_tiles(u, p):
        total = jnp.dot(sel[p], recv1[:, u].reshape(128, 1024), preferred_element_type=jnp.float32)
        asend[:, u] = total.astype(jnp.bfloat16).reshape(4, 16, 1024)

    def add_first(u, p):
        total = asend[by_portion(p, first_of), u].astype(jnp.float32)
        for d in range(3):
            total = total + arecv[d, u].astype(jnp.float32)
        bsend[u] = total.astype(jnp.bfloat16)

    def add_second(u, p):
        total = bsend[u].astype(jnp.float32)
        for d in range(3):
            total = total + brecv[d, u].astype(jnp.float32)
        total = total / jnp.concatenate([den[p]] * 8, axis=1)
        for b in range(4):
            cfull[u, b] = total[4 * b : 4 * b + 4]
        gath[by_portion(p, first_of), u] = total.astype(jnp.bfloat16)

    def templates_out(p, u):
        all_three(lambda d: fourth(p, u, d).start())
        if p > 0:

            @pl.when(moved[p - 1])
            def _():
                to_owner(p, u).start()

    def pick(u, p):
        found = jnp.dot(
            selt[p, :, 0:64], gath[:, u].reshape(64, 1024), preferred_element_type=jnp.float32
        )
        for r in range(8):
            spread[pl.ds(r, 128, stride=8), :] = found[:, 128 * r : 128 * r + 128]
        send4[:, u] = spread[...].astype(jnp.bfloat16).reshape(8, 128, 128)

    def picks_out(p, u):
        all_seven(lambda k: last(p, u, k).start())
        own_last(p, u).start()

    @pl.loop(0, UNITS + LAGS[3])
    def _(step):
        one_unit(
            step - LAGS[0],
            tiles_here,
            add_tiles,
            lambda p, u: all_three(lambda d: second(p, u, d).start()),
        )
        one_unit(
            step - LAGS[1],
            lambda p, u: await_bytes(three(arecv, u), ra.at[u]),
            add_first,
            lambda p, u: all_three(lambda d: third(p, u, d).start()),
        )
        one_unit(
            step - LAGS[2],
            lambda p, u: await_bytes(three(brecv, u), rb.at[u]),
            add_second,
            templates_out,
        )
        one_unit(
            step - LAGS[3],
            lambda p, u: await_bytes(three(gath, u), rga.at[u]),
            pick,
            picks_out,
        )

    for u in range(UNITS):
        p = u % 3
        if p == 0:
            crecv[u] = cfull[u, second_of[p]]
        else:

            @pl.when(moved[p - 1])
            def _(p=p, u=u):
                to_owner(p, u).wait()

            @pl.when(jnp.logical_not(moved[p - 1]))
            def _(p=p, u=u):
                crecv[u] = cfull[u, second_of[p]]

    @pl.loop(0, UNITS // 2)
    def _(rb):
        for cb in range(2):
            unit = crecv[2 * rb + cb]
            for k in range(4):
                rows = jnp.zeros((8, 128), jnp.float32)
                for r in range(8):
                    row = jnp.broadcast_to(unit[k : k + 1, 128 * r : 128 * r + 128], (8, 128))
                    rows = jnp.where(down == r, row, rows)
                coadd[k, pl.ds(pl.multiple_of(rb * 8, 8), 8), 128 * cb : 128 * cb + 128] = rows

    keep_coadd = pltpu.make_async_copy(coadd, coadd_hbm, out_sem.at[2])
    keep_coadd.start()

    @pl.loop(0, UNITS)
    def _(u):
        own_last(0, u).wait()
        await_bytes(seven(recv4, u), r4.at[u])
        await_bytes(seven(send4, u), s4.at[u])
        await_bytes(seven(send1, u), s1.at[u])
        await_bytes(three(asend, u), sa.at[u])
        await_bytes(three(brecv, u), sb.at[u])
        await_bytes(three(gath, u), sga.at[u])

    keep_warp.wait()
    keep_coadd.wait()


def subtract(
    coeff_s,
    ahead_hbm,
    back_hbm,
    warp_hbm,
    picked_hbm,
    coadd_in,
    diff_hbm,
    coadd_out,
    ahead,
    back,
    warp,
    picked,
    diff,
    fmat,
    mband,
    tbuf,
    hbuf,
    strip_sem,
    in_sem,
    out_sem,
    coadd_sem,
):
    pairs = TILES_DEV // 2

    def enter(pair):
        chunk = (slice(None), slice(None), pl.ds(pair * 16, 16))
        rows = (slice(None), pl.ds(pair * 2 * SIDE, 2 * SIDE))
        return (
            pltpu.make_async_copy(picked_hbm.at[chunk], picked.at[chunk], in_sem.at[pair, 0]),
            pltpu.make_async_copy(warp_hbm.at[rows], warp.at[rows], in_sem.at[pair, 1]),
        )

    def leave(pair):
        here = pl.ds(pair * 2, 2)
        return pltpu.make_async_copy(diff.at[here], diff_hbm.at[here], out_sem.at[pair])

    strip_copies = (
        pltpu.make_async_copy(ahead_hbm, ahead, strip_sem.at[0]),
        pltpu.make_async_copy(back_hbm, back, strip_sem.at[1]),
    )
    for copy in strip_copies:
        copy.start()

    @pl.loop(0, pairs)
    def _(pair):
        for copy in enter(pair):
            copy.start()

    pass_coadd = pltpu.make_async_copy(coadd_in, coadd_out, coadd_sem)
    pass_coadd.start()
    for copy in strip_copies:
        copy.wait()

    @pl.loop(0, NF)
    def _(j):
        fmat[j] = jnp.zeros((SIDE, SIDE), jnp.bfloat16)
        write_square(ahead[j], fmat.at[j])

    def assemble(pair, slot):
        rows = pl.ds(pl.multiple_of(pair * 16, 16), 16)
        for q in range(8):
            for i in range(2):
                for b in range(2):
                    upper = picked[q, 4 * i + b, rows, :].astype(jnp.float32)
                    lower = picked[q, 4 * i + 2 + b, rows, :].astype(jnp.float32)
                    at = 32 * q + 16 * i
                    cols = slice(128 * b, 128 * b + 128)
                    tbuf[slot, at : at + 16, cols] = jnp.concatenate(
                        [upper[0:8], lower[0:8]], axis=0
                    ).astype(jnp.bfloat16)
                    tbuf[slot, SIDE + at : SIDE + at + 16, cols] = jnp.concatenate(
                        [upper[8:16], lower[8:16]], axis=0
                    ).astype(jnp.bfloat16)

    def mix(pair, slot):
        for half in range(2):
            t = pair * 2 + half
            for j in range(NF):
                strip = None
                for k in range(len(BASIS_COLS)):
                    if BASIS_COLS[k] == j:
                        term = coeff_s[t, k] * back[BASIS_ROWS[k]]
                        strip = term if strip is None else strip + term
                diag, right, left = toeplitz_blocks(strip)
                cols = slice(128 * j, 128 * j + 128)
                mband[slot, half, 0:16, cols] = right
                for i in range(8):
                    mband[slot, half, 16 + 16 * i : 32 + 16 * i, cols] = diag[i]
                mband[slot, half, 144:160, cols] = left

    def columns(slot):
        for j in range(NF):
            filtered = jnp.dot(tbuf[slot], fmat[j], preferred_element_type=jnp.float32).astype(jnp.bfloat16)
            for i in range(4):
                hbuf[slot, i, 128 * j : 128 * j + 128, :] = filtered[128 * i : 128 * i + 128]

    def rest(pair, slot):
        for half in range(2):
            t = pair * 2 + half
            top = jnp.dot(mband[slot, half, 16:160, :], hbuf[slot, 2 * half], preferred_element_type=jnp.float32)
            low = jnp.dot(
                mband[slot, half, 0:144, :], hbuf[slot, 2 * half + 1], preferred_element_type=jnp.float32
            )
            whole = jnp.concatenate([top[0:112], top[112:144] + low[0:32], low[32:144]], axis=0)
            for b in range(2):
                cols = slice(128 * b, 128 * b + 128)
                diff[t, :, cols] = warp[b, pl.ds(pl.multiple_of(t * SIDE, SIDE), SIDE), :] - whole[:, cols]
        leave(pair).start()

    @pl.loop(0, pairs // 2)
    def _(step):
        chosen = [step * 2 + slot for slot in range(2)]
        for pair in chosen:
            for copy in enter(pair):
                copy.wait()
        for slot, pair in enumerate(chosen):
            assemble(pair, slot)
            mix(pair, slot)
            columns(slot)
        for slot, pair in enumerate(chosen):
            rest(pair, slot)

    @pl.loop(0, pairs)
    def _(pair):
        leave(pair).wait()

    pass_coadd.wait()


def shards(tiles, shift_int, shift_frac, tile_weight, tile_patch, al_coeff):
    ahead, back = factor_strips()
    smem = pl.BlockSpec(memory_space=pltpu.SMEM)
    hbm = pl.BlockSpec(memory_space=pl.ANY)
    bf16, f32, i32 = jnp.bfloat16, jnp.float32, jnp.int32
    dma = pltpu.SemaphoreType.DMA
    lanes = (8, UNITS, TILES_DEV, 1024)
    block = (8, UNITS, TILES_DEV * 8, 128)
    warp, picked, coadd_units = pl.pallas_call(
        exchange,
        out_shape=(
            jax.ShapeDtypeStruct((2, TILES_DEV * SIDE, 128), f32),
            jax.ShapeDtypeStruct(block, bf16),
            jax.ShapeDtypeStruct((4, 32, SIDE), f32),
        ),
        in_specs=[hbm, hbm, hbm, hbm, hbm],
        out_specs=(hbm, hbm, hbm),
        scratch_shapes=[
            pltpu.VMEM((TILES_DEV, SIDE, SIDE), bf16),
            pltpu.VMEM((2, TILES_DEV * SIDE, 128), f32),
            pltpu.VMEM(lanes, bf16),
            pltpu.VMEM(lanes, bf16),
            pltpu.VMEM((3, 64, 128), bf16),
            pltpu.VMEM((3, 128, 128), bf16),
            pltpu.VMEM((4, UNITS, 16, 1024), bf16),
            pltpu.VMEM((3, UNITS, 16, 1024), bf16),
            pltpu.VMEM((UNITS, 16, 1024), bf16),
            pltpu.VMEM((3, UNITS, 16, 1024), bf16),
            pltpu.VMEM((4, UNITS, 16, 1024), bf16),
            pltpu.VMEM((1024, 128), f32),
            pltpu.VMEM(block, bf16),
            pltpu.VMEM((UNITS, 4, 4, 1024), f32),
            pltpu.VMEM((UNITS, 4, 1024), f32),
            pltpu.VMEM((4, 32, SIDE), f32),
            pltpu.VMEM((48, 8, 128), f32),
            pltpu.VMEM((3, 16, 128), f32),
            pltpu.VMEM((2 * TILES_DEV, 8, 128), f32),
            pltpu.VMEM((16, SIDE, SIDE), bf16),
            pltpu.VMEM((16, 128), i32),
            pltpu.VMEM((16, 128), f32),
            pltpu.VMEM((TILES_DEV, 128), f32),
            pltpu.SMEM((2, TILES_DEV), i32),
            pltpu.SMEM((2, TILES_DEV), f32),
            dma((UNITS,)),
            dma((UNITS,)),
            dma((UNITS,)),
            dma((UNITS,)),
            dma((UNITS,)),
            dma((UNITS,)),
            dma((UNITS,)),
            dma((UNITS,)),
            dma((UNITS,)),
            dma((UNITS,)),
            dma((UNITS,)),
            dma((UNITS,)),
            dma((2,)),
            dma((4,)),
            dma((UNITS,)),
            dma((UNITS,)),
            dma((3,)),
        ],
        compiler_params=pltpu.CompilerParams(
            collective_id=0, has_side_effects=True, vmem_limit_bytes=56 << 20
        ),
    )(
        tiles,
        shift_int.T,
        shift_frac.T,
        tile_patch.reshape(16, 128),
        tile_weight.reshape(16, 128),
    )
    difference, coadd = pl.pallas_call(
        subtract,
        out_shape=(
            jax.ShapeDtypeStruct((TILES_DEV, SIDE, SIDE), f32),
            jax.ShapeDtypeStruct((4, 32, SIDE), f32),
        ),
        in_specs=[smem, hbm, hbm, hbm, hbm, hbm],
        out_specs=(hbm, hbm),
        scratch_shapes=[
            pltpu.VMEM((NF, 8, 128), f32),
            pltpu.VMEM((NF, 8, 128), f32),
            pltpu.VMEM((2, TILES_DEV * SIDE, 128), f32),
            pltpu.VMEM(block, bf16),
            pltpu.VMEM((TILES_DEV, SIDE, SIDE), f32),
            pltpu.VMEM((NF, SIDE, SIDE), bf16),
            pltpu.VMEM((2, 2, 160, 128 * NF), bf16),
            pltpu.VMEM((2, 2 * SIDE, SIDE), bf16),
            pltpu.VMEM((2, 4, 128 * NF, SIDE), bf16),
            dma((2,)),
            dma((TILES_DEV // 2, 2)),
            dma((TILES_DEV // 2,)),
            dma,
        ],
        compiler_params=pltpu.CompilerParams(vmem_limit_bytes=60 << 20),
    )(al_coeff, jnp.asarray(ahead), jnp.asarray(back), warp, picked, coadd_units)
    return coadd, difference


def solution(mesh):
    return jax.shard_map(
        shards,
        mesh=mesh,
        in_specs=(
            P(("visit", "sky"), None, None),
            P(("visit", "sky"), None),
            P(("visit", "sky"), None),
            P(),
            P(),
            P(("visit", "sky"), None),
        ),
        out_specs=(P("sky", "visit", None), P(("visit", "sky"), None, None)),
        check_vma=False,
    )
```

```python
import functools
import math

import jax
import jax.numpy as jnp
import numpy as np
from jax import lax
from jax.experimental import pallas as pl
from jax.experimental.pallas import tpu as pltpu
from jax.sharding import PartitionSpec as P

MESH = pl.DeviceIdType.MESH
KHALF = 10
SIDE = 256
TILES_DEV = 16
SIGMAS = (1.0, 2.5, 5.0)
FACTORS = ((0, 0), (0, 1), (0, 2), (1, 0), (1, 1), (2, 0))
BASIS_ROWS = (0, 1, 0, 2, 0, 1, 3, 4, 3, 5)
BASIS_COLS = (0, 0, 1, 0, 2, 1, 3, 3, 4, 5)
NF = len(FACTORS)

UNITS = 8
LAGS = (0, 5, 10, 15)


def wrapped_diff():
    diff = np.arange(128)[None, :] - np.arange(8)[:, None]
    return ((diff + 64) % 128) - 64


def factor_strips():
    diff = wrapped_diff().astype(np.float64)
    reach = np.arange(-KHALF, KHALF + 1).astype(np.float64)
    ahead, back = [], []
    for sigma_index, power in FACTORS:
        sigma = SIGMAS[sigma_index]
        norm = np.sum(np.exp(-reach * reach / (2.0 * sigma * sigma)))
        for out, u in ((ahead, diff), (back, -diff)):
            value = np.exp(-u * u / (2.0 * sigma * sigma)) * (u / sigma) ** power / norm
            out.append(np.where(np.abs(u) <= KHALF, value, 0.0))
    return np.stack(ahead).astype(np.float32), np.stack(back).astype(np.float32)


def sinc(v):
    scaled = math.pi * jnp.where(v == 0.0, 1.0, v)
    return jnp.where(v == 0.0, 1.0, jnp.sin(scaled) / scaled)


def lanczos(offset):
    return jnp.where(jnp.abs(offset) < 3.0, sinc(offset) * sinc(offset / 3.0), 0.0)


def by_portion(p, values):
    return jnp.where(p == 0, values[0], jnp.where(p == 1, values[1], values[2]))


def toeplitz_blocks(strip):
    lane = lax.broadcasted_iota(jnp.int32, (8, 128), 1)
    rows = [strip if b == 0 else pltpu.roll(strip, 8 * b, 1) for b in range(16)]
    low = lane < 64
    zero = jnp.zeros_like(strip)
    left = [jnp.where(low, zero, rows[b]) for b in (0, 1)]
    right = [jnp.where(low, rows[b], zero) for b in (14, 15)]
    for b in (0, 1):
        rows[b] = jnp.where(low, rows[b], zero)
    for b in (14, 15):
        rows[b] = jnp.where(low, zero, rows[b])

    def pack(pair):
        return jnp.concatenate(pair, axis=0).astype(jnp.bfloat16)

    return [pack(rows[2 * i : 2 * i + 2]) for i in range(8)], pack(right), pack(left)


def write_square(strip, ref):
    diag, right, left = toeplitz_blocks(strip)
    for i in range(8):
        ref[16 * i : 16 * i + 16, 0:128] = diag[i]
        ref[128 + 16 * i : 144 + 16 * i, 128:256] = diag[i]
    ref[112:128, 128:256] = right
    ref[128:144, 0:128] = left


def exchange(
    tiles_hbm,
    whole_hbm,
    part_hbm,
    patch_2d,
    weight_2d,
    warp_hbm,
    recv4,
    coadd_hbm,
    tiles,
    warp,
    send1,
    recv1,
    sel,
    selt,
    asend,
    arecv,
    bsend,
    brecv,
    gath,
    spread,
    send4,
    cfull,
    crecv,
    coadd,
    hits,
    den,
    strips,
    rmat,
    patch_v,
    weight_v,
    wcol,
    whole_s,
    part_s,
    s1,
    r1,
    sa,
    ra,
    sb,
    rb,
    sga,
    rga,
    s4,
    r4,
    sc,
    rc,
    in_sem,
    small_sem,
    own1,
    own4,
    out_sem,
):
    visit, sky = lax.axis_index("visit"), lax.axis_index("sky")
    y, c = lax.div(visit, 2), lax.rem(visit, 2)
    z, x = lax.div(sky, 4), lax.rem(sky, 4)

    def dev(y_, c_, z_, x_):
        return (y_ * 2 + c_, z_ * 4 + x_)

    ring_of = (y, z, x)
    first_of, second_of = (x, y, z), (z, x, y)

    def on_ring(p, pos, core):
        return (dev(pos, core, z, x), dev(y, core, pos, x), dev(y, core, z, pos))[p]

    def on_first(p, pos):
        return (dev(y, c, z, pos), dev(pos, c, z, x), dev(y, c, pos, x))[p]

    def on_second(p, pos):
        return (dev(y, c, pos, x), dev(y, c, z, pos), dev(pos, c, z, x))[p]

    def partner(p, k):
        d, core = lax.div(k, 2), lax.rem(c + lax.rem(k, 2), 2)
        return lax.rem(ring_of[p] + d, 4), lax.rem(ring_of[p] + 4 - d, 4), core

    swap = (dev(z, c, y, x), dev(x, c, z, y))
    moved = (y != z, y != x)

    def fetch(i):
        half = pl.ds(i * (TILES_DEV // 2), TILES_DEV // 2)
        return pltpu.make_async_copy(tiles_hbm.at[half], tiles.at[half], in_sem.at[i])

    small = [
        pltpu.make_async_copy(here, there, small_sem.at[i])
        for i, (here, there) in enumerate(
            (
                (weight_2d, weight_v),
                (patch_2d, patch_v),
                (whole_hbm, whole_s),
                (part_hbm, part_s),
            )
        )
    ]

    barrier = pltpu.get_barrier_semaphore()
    pl.semaphore_signal(barrier, inc=1, device_id=dev(y, 1 - c, z, x), device_id_type=MESH)
    for p in range(3):

        @pl.loop(2, 8)
        def _(k, p=p):
            pos, unused, core = partner(p, k)
            pl.semaphore_signal(barrier, inc=1, device_id=on_ring(p, pos, core), device_id_type=MESH)

    for i in range(2):

        @pl.when(moved[i])
        def _(i=i):
            pl.semaphore_signal(barrier, inc=1, device_id=swap[i], device_id_type=MESH)

    for copy in small:
        copy.start()
    for i in range(2):
        fetch(i).start()

    lane = lax.broadcasted_iota(jnp.int32, (8, 128), 1)
    down = lax.broadcasted_iota(jnp.int32, (8, 128), 0)
    reach = jnp.where(lane < 64, lane, lane - 128).astype(jnp.float32)
    reach = jnp.where((down & 1) == 0, reach, -reach)

    @pl.loop(0, 16)
    def _(j):
        rmat[j] = jnp.zeros((SIDE, SIDE), jnp.bfloat16)

    for copy in small[2:]:
        copy.wait()

    for i in range(4):
        shift = jnp.zeros((8, 128), jnp.float32)
        for r in range(8):
            t = i * 4 + r // 2
            value = whole_s[r % 2, t].astype(jnp.float32) + part_s[r % 2, t]
            shift = jnp.where(down == r, value, shift)
        taps = lanczos(reach - shift)
        for r in range(8):
            row = jnp.broadcast_to(taps[r : r + 1], (8, 128))
            strips[i * 8 + r] = pltpu.roll(row, 0, 1, stride=1, stride_axis=0)

    def own_first(p, u):
        return pltpu.make_async_copy(send1.at[ring_of[p] * 2 + c, u], recv1.at[0, u], own1.at[u])

    def first(p, u, k):
        pos, unused, core = partner(p, k)
        return pltpu.make_async_remote_copy(
            src_ref=send1.at[pos * 2 + core, u],
            dst_ref=recv1.at[k, u],
            send_sem=s1.at[u],
            recv_sem=r1.at[u],
            device_id=on_ring(p, pos, core),
            device_id_type=MESH,
        )

    def start_wave(w):
        for p in range(3):
            u = 3 * w + p
            if u < UNITS:

                @pl.loop(0, 8)
                def _(q, u=u):
                    for r in range(8):
                        row = pl.ds(32 * q + 8 * (u // 2) + r, TILES_DEV, stride=SIDE)
                        send1[q, u, :, 128 * r : 128 * r + 128] = (wcol[...] * warp[u % 2, row]).astype(
                            jnp.bfloat16
                        )

                @pl.loop(1, 8)
                def _(k, p=p, u=u):
                    first(p, u, k).start()

                own_first(p, u).start()

    fetch(0).wait()

    @pl.loop(0, TILES_DEV // 8)
    def _(octet):
        @pl.when(octet == TILES_DEV // 16)
        def _():
            fetch(1).wait()

        for i in range(8):
            t = octet * 8 + i
            write_square(strips[2 * t], rmat.at[2 * i])
            write_square(strips[2 * t + 1], rmat.at[2 * i + 1])
        rowpasses = [
            jnp.dot(tiles[octet * 8 + i], rmat[2 * i + 1], preferred_element_type=jnp.float32).astype(
                jnp.bfloat16
            )
            for i in range(8)
        ]
        for i in range(8):
            value = jnp.dot(rmat[2 * i], rowpasses[i], preferred_element_type=jnp.float32)
            rows = pl.ds(pl.multiple_of((octet * 8 + i) * SIDE, SIDE), SIDE)
            for b in range(2):
                warp[b, rows, :] = value[:, 128 * b : 128 * b + 128]

    small[0].wait()
    mine_row = weight_v[pl.ds(visit * 2 + lax.div(sky, 8), 1), :]
    mine_row = pltpu.roll(jnp.broadcast_to(mine_row, (8, 128)), lax.rem(128 - lax.rem(sky, 8) * 16, 128), 1)
    diagonal = lax.broadcasted_iota(jnp.int32, (TILES_DEV, 128), 0) == lax.broadcasted_iota(
        jnp.int32, (TILES_DEV, 128), 1
    )
    one_each = jnp.where(diagonal, jnp.broadcast_to(mine_row[0:1], (TILES_DEV, 128)), 0.0)
    wcol[...] = jnp.broadcast_to(jnp.sum(one_each, axis=1, keepdims=True), (TILES_DEV, 128))

    pl.semaphore_wait(barrier, 19 + moved[0].astype(jnp.int32) + moved[1].astype(jnp.int32))
    start_wave(0)

    keep_warp = pltpu.make_async_copy(warp, warp_hbm, out_sem.at[0])
    keep_warp.start()
    small[1].wait()

    line = lax.broadcasted_iota(jnp.int32, (1, 128), 1)
    for p in range(3):
        key = jnp.zeros((1, 128), jnp.int32)
        for k in range(8):
            unused, pos, core = partner(p, k)
            v, s = on_ring(p, pos, core)
            found = jnp.broadcast_to(patch_v[pl.ds(v * 2 + lax.div(s, 8), 1), :], (8, 128))
            found = pltpu.roll(found, lax.rem(128 + 16 * k - lax.rem(s, 8) * 16, 128), 1)
            key = jnp.where((line >> 4) == k, found[0:1], key)
        if p == 0:
            key = ((key >> 2) & 3) * 16 + (key >> 4) * 4 + (key & 3)
        hot = jnp.where(
            jnp.broadcast_to(key, (128, 128)) == lax.broadcasted_iota(jnp.int32, (128, 128), 0), 1.0, 0.0
        )
        sel[p] = hot[0:64].astype(jnp.bfloat16)
        selt[p] = hot.T.astype(jnp.bfloat16)

    start_wave(1)

    @pl.loop(0, 48)
    def _(n):
        p, second, k = lax.div(n, 16), lax.rem(lax.div(n, 4), 4), lax.rem(n, 4)
        owner = by_portion(p, (second * 4 + x, y * 4 + second, z * 4 + second))
        hit = jnp.where(patch_v[...] == owner * 4 + k, weight_v[...], 0.0)
        hits[n] = hit[0:8] + hit[8:16]

    weights = 1.0 + jnp.sum(jnp.sum(hits[...], axis=1), axis=1, keepdims=True)
    for p in range(3):
        den[p] = jnp.broadcast_to(weights[16 * p : 16 * p + 16], (16, 128))

    start_wave(2)

    def second(p, u, d):
        pos = lax.rem(first_of[p] + d, 4)
        return pltpu.make_async_remote_copy(
            src_ref=asend.at[pos, u],
            dst_ref=arecv.at[d - 1, u],
            send_sem=sa.at[u],
            recv_sem=ra.at[u],
            device_id=on_first(p, pos),
            device_id_type=MESH,
        )

    def third(p, u, d):
        return pltpu.make_async_remote_copy(
            src_ref=bsend.at[u],
            dst_ref=brecv.at[d - 1, u],
            send_sem=sb.at[u],
            recv_sem=rb.at[u],
            device_id=on_second(p, lax.rem(second_of[p] + d, 4)),
            device_id_type=MESH,
        )

    def fourth(p, u, d):
        mine = gath.at[first_of[p], u]
        return pltpu.make_async_remote_copy(
            src_ref=mine,
            dst_ref=mine,
            send_sem=sga.at[u],
            recv_sem=rga.at[u],
            device_id=on_first(p, lax.rem(first_of[p] + d, 4)),
            device_id_type=MESH,
        )

    def to_owner(p, u):
        return pltpu.make_async_remote_copy(
            src_ref=cfull.at[u, second_of[p]],
            dst_ref=crecv.at[u],
            send_sem=sc.at[u],
            recv_sem=rc.at[u],
            device_id=swap[p - 1],
            device_id_type=MESH,
        )

    def own_last(p, u):
        return pltpu.make_async_copy(send4.at[0, u], recv4.at[ring_of[p] * 2 + c, u], own4.at[u])

    def last(p, u, k):
        unused, pos, core = partner(p, k)
        return pltpu.make_async_remote_copy(
            src_ref=send4.at[k, u],
            dst_ref=recv4.at[ring_of[p] * 2 + c, u],
            send_sem=s4.at[u],
            recv_sem=r4.at[u],
            device_id=on_ring(p, pos, core),
            device_id_type=MESH,
        )

    def one_unit(u, before, body, after):
        @pl.when((u >= 0) & (u < UNITS))
        def _():
            portion = lax.rem(u, 3)
            for p in range(3):

                @pl.when(portion == p)
                def _(p=p):
                    before(p, u)

            body(u, portion)
            for p in range(3):

                @pl.when(portion == p)
                def _(p=p):
                    after(p, u)

    def all_three(act):
        @pl.loop(1, 4)
        def _(d):
            act(d)

    def all_seven(act):
        @pl.loop(1, 8)
        def _(k):
            act(k)

    def await_bytes(ref, sem):
        pltpu.make_async_copy(ref, ref, sem).wait()

    def seven(ref, u):
        return ref.at[pl.ds(1, 7), u]

    def three(ref, u):
        return ref.at[pl.ds(0, 3), u]

    def tiles_here(p, u):
        own_first(p, u).wait()
        await_bytes(seven(recv1, u), r1.at[u])

    def add_tiles(u, p):
        total = jnp.dot(sel[p], recv1[:, u].reshape(128, 1024), preferred_element_type=jnp.float32)
        asend[:, u] = total.astype(jnp.bfloat16).reshape(4, 16, 1024)

    def add_first(u, p):
        total = asend[by_portion(p, first_of), u].astype(jnp.float32)
        for d in range(3):
            total = total + arecv[d, u].astype(jnp.float32)
        bsend[u] = total.astype(jnp.bfloat16)

    def add_second(u, p):
        total = bsend[u].astype(jnp.float32)
        for d in range(3):
            total = total + brecv[d, u].astype(jnp.float32)
        total = total / jnp.concatenate([den[p]] * 8, axis=1)
        for b in range(4):
            cfull[u, b] = total[4 * b : 4 * b + 4]
        gath[by_portion(p, first_of), u] = total.astype(jnp.bfloat16)

    def templates_out(p, u):
        all_three(lambda d: fourth(p, u, d).start())
        if p > 0:

            @pl.when(moved[p - 1])
            def _():
                to_owner(p, u).start()

    def pick(u, p):
        found = jnp.dot(
            selt[p, :, 0:64], gath[:, u].reshape(64, 1024), preferred_element_type=jnp.float32
        )
        for r in range(8):
            spread[pl.ds(r, 128, stride=8), :] = found[:, 128 * r : 128 * r + 128]
        send4[:, u] = spread[...].astype(jnp.bfloat16).reshape(8, 128, 128)

    def picks_out(p, u):
        all_seven(lambda k: last(p, u, k).start())
        own_last(p, u).start()

    @pl.loop(0, UNITS + LAGS[3])
    def _(step):
        one_unit(
            step - LAGS[0],
            tiles_here,
            add_tiles,
            lambda p, u: all_three(lambda d: second(p, u, d).start()),
        )
        one_unit(
            step - LAGS[1],
            lambda p, u: await_bytes(three(arecv, u), ra.at[u]),
            add_first,
            lambda p, u: all_three(lambda d: third(p, u, d).start()),
        )
        one_unit(
            step - LAGS[2],
            lambda p, u: await_bytes(three(brecv, u), rb.at[u]),
            add_second,
            templates_out,
        )
        one_unit(
            step - LAGS[3],
            lambda p, u: await_bytes(three(gath, u), rga.at[u]),
            pick,
            picks_out,
        )

    for u in range(UNITS):
        p = u % 3
        if p == 0:
            crecv[u] = cfull[u, second_of[p]]
        else:

            @pl.when(moved[p - 1])
            def _(p=p, u=u):
                to_owner(p, u).wait()

            @pl.when(jnp.logical_not(moved[p - 1]))
            def _(p=p, u=u):
                crecv[u] = cfull[u, second_of[p]]

    @pl.loop(0, UNITS // 2)
    def _(rb):
        for cb in range(2):
            unit = crecv[2 * rb + cb]
            for k in range(4):
                rows = jnp.zeros((8, 128), jnp.float32)
                for r in range(8):
                    row = jnp.broadcast_to(unit[k : k + 1, 128 * r : 128 * r + 128], (8, 128))
                    rows = jnp.where(down == r, row, rows)
                coadd[k, pl.ds(pl.multiple_of(rb * 8, 8), 8), 128 * cb : 128 * cb + 128] = rows

    keep_coadd = pltpu.make_async_copy(coadd, coadd_hbm, out_sem.at[2])
    keep_coadd.start()

    @pl.loop(0, UNITS)
    def _(u):
        own_last(0, u).wait()
        await_bytes(seven(recv4, u), r4.at[u])
        await_bytes(seven(send4, u), s4.at[u])
        await_bytes(seven(send1, u), s1.at[u])
        await_bytes(three(asend, u), sa.at[u])
        await_bytes(three(brecv, u), sb.at[u])
        await_bytes(three(gath, u), sga.at[u])

    keep_warp.wait()
    keep_coadd.wait()


def subtract(
    coeff_s,
    ahead_hbm,
    back_hbm,
    warp_hbm,
    picked_hbm,
    coadd_in,
    diff_hbm,
    coadd_out,
    ahead,
    back,
    warp,
    picked,
    diff,
    fmat,
    mband,
    tbuf,
    hbuf,
    strip_sem,
    in_sem,
    out_sem,
    coadd_sem,
):
    pairs = TILES_DEV // 2

    def enter(pair):
        chunk = (slice(None), slice(None), pl.ds(pair * 16, 16))
        rows = (slice(None), pl.ds(pair * 2 * SIDE, 2 * SIDE))
        return (
            pltpu.make_async_copy(picked_hbm.at[chunk], picked.at[chunk], in_sem.at[pair, 0]),
            pltpu.make_async_copy(warp_hbm.at[rows], warp.at[rows], in_sem.at[pair, 1]),
        )

    def leave(pair):
        here = pl.ds(pair * 2, 2)
        return pltpu.make_async_copy(diff.at[here], diff_hbm.at[here], out_sem.at[pair])

    strip_copies = (
        pltpu.make_async_copy(ahead_hbm, ahead, strip_sem.at[0]),
        pltpu.make_async_copy(back_hbm, back, strip_sem.at[1]),
    )
    for copy in strip_copies:
        copy.start()

    @pl.loop(0, pairs)
    def _(pair):
        for copy in enter(pair):
            copy.start()

    pass_coadd = pltpu.make_async_copy(coadd_in, coadd_out, coadd_sem)
    pass_coadd.start()
    for copy in strip_copies:
        copy.wait()

    @pl.loop(0, NF)
    def _(j):
        fmat[j] = jnp.zeros((SIDE, SIDE), jnp.bfloat16)
        write_square(ahead[j], fmat.at[j])

    def assemble(pair, slot):
        rows = pl.ds(pl.multiple_of(pair * 16, 16), 16)
        for q in range(8):
            for i in range(2):
                for b in range(2):
                    upper = picked[q, 4 * i + b, rows, :].astype(jnp.float32)
                    lower = picked[q, 4 * i + 2 + b, rows, :].astype(jnp.float32)
                    at = 32 * q + 16 * i
                    cols = slice(128 * b, 128 * b + 128)
                    tbuf[slot, at : at + 16, cols] = jnp.concatenate(
                        [upper[0:8], lower[0:8]], axis=0
                    ).astype(jnp.bfloat16)
                    tbuf[slot, SIDE + at : SIDE + at + 16, cols] = jnp.concatenate(
                        [upper[8:16], lower[8:16]], axis=0
                    ).astype(jnp.bfloat16)

    def mix(pair, slot):
        for half in range(2):
            t = pair * 2 + half
            for j in range(NF):
                strip = None
                for k in range(len(BASIS_COLS)):
                    if BASIS_COLS[k] == j:
                        term = coeff_s[t, k] * back[BASIS_ROWS[k]]
                        strip = term if strip is None else strip + term
                diag, right, left = toeplitz_blocks(strip)
                cols = slice(128 * j, 128 * j + 128)
                mband[slot, half, 0:16, cols] = right
                for i in range(8):
                    mband[slot, half, 16 + 16 * i : 32 + 16 * i, cols] = diag[i]
                mband[slot, half, 144:160, cols] = left

    def columns(slot):
        for j in range(NF):
            filtered = jnp.dot(tbuf[slot], fmat[j], preferred_element_type=jnp.float32).astype(jnp.bfloat16)
            for i in range(4):
                hbuf[slot, i, 128 * j : 128 * j + 128, :] = filtered[128 * i : 128 * i + 128]

    def rest(pair, slot):
        for half in range(2):
            t = pair * 2 + half
            top = jnp.dot(mband[slot, half, 16:160, :], hbuf[slot, 2 * half], preferred_element_type=jnp.float32)
            low = jnp.dot(
                mband[slot, half, 0:144, :], hbuf[slot, 2 * half + 1], preferred_element_type=jnp.float32
            )
            whole = jnp.concatenate([top[0:112], top[112:144] + low[0:32], low[32:144]], axis=0)
            for b in range(2):
                cols = slice(128 * b, 128 * b + 128)
                diff[t, :, cols] = warp[b, pl.ds(pl.multiple_of(t * SIDE, SIDE), SIDE), :] - whole[:, cols]
        leave(pair).start()

    @pl.loop(0, pairs // 2)
    def _(step):
        chosen = [step * 2 + slot for slot in range(2)]
        for pair in chosen:
            for copy in enter(pair):
                copy.wait()
        for slot, pair in enumerate(chosen):
            assemble(pair, slot)
            mix(pair, slot)
            columns(slot)
        for slot, pair in enumerate(chosen):
            rest(pair, slot)

    @pl.loop(0, pairs)
    def _(pair):
        leave(pair).wait()

    pass_coadd.wait()


def shards(tiles, shift_int, shift_frac, tile_weight, tile_patch, al_coeff):
    ahead, back = factor_strips()
    smem = pl.BlockSpec(memory_space=pltpu.SMEM)
    hbm = pl.BlockSpec(memory_space=pl.ANY)
    bf16, f32, i32 = jnp.bfloat16, jnp.float32, jnp.int32
    dma = pltpu.SemaphoreType.DMA
    lanes = (8, UNITS, TILES_DEV, 1024)
    block = (8, UNITS, TILES_DEV * 8, 128)
    warp, picked, coadd_units = pl.pallas_call(
        exchange,
        out_shape=(
            jax.ShapeDtypeStruct((2, TILES_DEV * SIDE, 128), f32),
            jax.ShapeDtypeStruct(block, bf16),
            jax.ShapeDtypeStruct((4, 32, SIDE), f32),
        ),
        in_specs=[hbm, hbm, hbm, hbm, hbm],
        out_specs=(hbm, hbm, hbm),
        scratch_shapes=[
            pltpu.VMEM((TILES_DEV, SIDE, SIDE), bf16),
            pltpu.VMEM((2, TILES_DEV * SIDE, 128), f32),
            pltpu.VMEM(lanes, bf16),
            pltpu.VMEM(lanes, bf16),
            pltpu.VMEM((3, 64, 128), bf16),
            pltpu.VMEM((3, 128, 128), bf16),
            pltpu.VMEM((4, UNITS, 16, 1024), bf16),
            pltpu.VMEM((3, UNITS, 16, 1024), bf16),
            pltpu.VMEM((UNITS, 16, 1024), bf16),
            pltpu.VMEM((3, UNITS, 16, 1024), bf16),
            pltpu.VMEM((4, UNITS, 16, 1024), bf16),
            pltpu.VMEM((1024, 128), f32),
            pltpu.VMEM(block, bf16),
            pltpu.VMEM((UNITS, 4, 4, 1024), f32),
            pltpu.VMEM((UNITS, 4, 1024), f32),
            pltpu.VMEM((4, 32, SIDE), f32),
            pltpu.VMEM((48, 8, 128), f32),
            pltpu.VMEM((3, 16, 128), f32),
            pltpu.VMEM((2 * TILES_DEV, 8, 128), f32),
            pltpu.VMEM((16, SIDE, SIDE), bf16),
            pltpu.VMEM((16, 128), i32),
            pltpu.VMEM((16, 128), f32),
            pltpu.VMEM((TILES_DEV, 128), f32),
            pltpu.SMEM((2, TILES_DEV), i32),
            pltpu.SMEM((2, TILES_DEV), f32),
            dma((UNITS,)),
            dma((UNITS,)),
            dma((UNITS,)),
            dma((UNITS,)),
            dma((UNITS,)),
            dma((UNITS,)),
            dma((UNITS,)),
            dma((UNITS,)),
            dma((UNITS,)),
            dma((UNITS,)),
            dma((UNITS,)),
            dma((UNITS,)),
            dma((2,)),
            dma((4,)),
            dma((UNITS,)),
            dma((UNITS,)),
            dma((3,)),
        ],
        compiler_params=pltpu.CompilerParams(
            collective_id=0, has_side_effects=True, vmem_limit_bytes=56 << 20
        ),
    )(
        tiles,
        shift_int.T,
        shift_frac.T,
        tile_patch.reshape(16, 128),
        tile_weight.reshape(16, 128),
    )
    difference, coadd = pl.pallas_call(
        subtract,
        out_shape=(
            jax.ShapeDtypeStruct((TILES_DEV, SIDE, SIDE), f32),
            jax.ShapeDtypeStruct((4, 32, SIDE), f32),
        ),
        in_specs=[smem, hbm, hbm, hbm, hbm, hbm],
        out_specs=(hbm, hbm),
        scratch_shapes=[
            pltpu.VMEM((NF, 8, 128), f32),
            pltpu.VMEM((NF, 8, 128), f32),
            pltpu.VMEM((2, TILES_DEV * SIDE, 128), f32),
            pltpu.VMEM(block, bf16),
            pltpu.VMEM((TILES_DEV, SIDE, SIDE), f32),
            pltpu.VMEM((NF, SIDE, SIDE), bf16),
            pltpu.VMEM((2, 2, 160, 128 * NF), bf16),
            pltpu.VMEM((2, 2 * SIDE, SIDE), bf16),
            pltpu.VMEM((2, 4, 128 * NF, SIDE), bf16),
            dma((2,)),
            dma((TILES_DEV // 2, 2)),
            dma((TILES_DEV // 2,)),
            dma,
        ],
        compiler_params=pltpu.CompilerParams(vmem_limit_bytes=60 << 20),
    )(al_coeff, jnp.asarray(ahead), jnp.asarray(back), warp, picked, coadd_units)
    return coadd, difference


def solution(mesh):
    return jax.shard_map(
        shards,
        mesh=mesh,
        in_specs=(
            P(("visit", "sky"), None, None),
            P(("visit", "sky"), None),
            P(("visit", "sky"), None),
            P(),
            P(),
            P(("visit", "sky"), None),
        ),
        out_specs=(P("sky", "visit", None), P(("visit", "sky"), None, None)),
        check_vma=False,
    )
```

```python
import functools
import math

import jax
import jax.numpy as jnp
import numpy as np
from jax import lax
from jax.experimental import pallas as pl
from jax.experimental.pallas import tpu as pltpu
from jax.sharding import PartitionSpec as P

MESH = pl.DeviceIdType.MESH
KHALF = 10
SIDE = 256
TILES_DEV = 16
SIGMAS = (1.0, 2.5, 5.0)
FACTORS = ((0, 0), (0, 1), (0, 2), (1, 0), (1, 1), (2, 0))
BASIS_ROWS = (0, 1, 0, 2, 0, 1, 3, 4, 3, 5)
BASIS_COLS = (0, 0, 1, 0, 2, 1, 3, 3, 4, 5)
NF = len(FACTORS)

UNITS = 8
LAGS = (0, 5, 10, 15)


def wrapped_diff():
    diff = np.arange(128)[None, :] - np.arange(8)[:, None]
    return ((diff + 64) % 128) - 64


def factor_strips():
    diff = wrapped_diff().astype(np.float64)
    reach = np.arange(-KHALF, KHALF + 1).astype(np.float64)
    ahead, back = [], []
    for sigma_index, power in FACTORS:
        sigma = SIGMAS[sigma_index]
        norm = np.sum(np.exp(-reach * reach / (2.0 * sigma * sigma)))
        for out, u in ((ahead, diff), (back, -diff)):
            value = np.exp(-u * u / (2.0 * sigma * sigma)) * (u / sigma) ** power / norm
            out.append(np.where(np.abs(u) <= KHALF, value, 0.0))
    return np.stack(ahead).astype(np.float32), np.stack(back).astype(np.float32)


def sinc(v):
    scaled = math.pi * jnp.where(v == 0.0, 1.0, v)
    return jnp.where(v == 0.0, 1.0, jnp.sin(scaled) / scaled)


def lanczos(offset):
    return jnp.where(jnp.abs(offset) < 3.0, sinc(offset) * sinc(offset / 3.0), 0.0)


def by_portion(p, values):
    return jnp.where(p == 0, values[0], jnp.where(p == 1, values[1], values[2]))


def toeplitz_blocks(strip):
    lane = lax.broadcasted_iota(jnp.int32, (8, 128), 1)
    rows = [strip if b == 0 else pltpu.roll(strip, 8 * b, 1) for b in range(16)]
    low = lane < 64
    zero = jnp.zeros_like(strip)
    left = [jnp.where(low, zero, rows[b]) for b in (0, 1)]
    right = [jnp.where(low, rows[b], zero) for b in (14, 15)]
    for b in (0, 1):
        rows[b] = jnp.where(low, rows[b], zero)
    for b in (14, 15):
        rows[b] = jnp.where(low, zero, rows[b])

    def pack(pair):
        return jnp.concatenate(pair, axis=0).astype(jnp.bfloat16)

    return [pack(rows[2 * i : 2 * i + 2]) for i in range(8)], pack(right), pack(left)


def write_square(strip, ref):
    diag, right, left = toeplitz_blocks(strip)
    for i in range(8):
        ref[16 * i : 16 * i + 16, 0:128] = diag[i]
        ref[128 + 16 * i : 144 + 16 * i, 128:256] = diag[i]
    ref[112:128, 128:256] = right
    ref[128:144, 0:128] = left


def exchange(
    tiles_hbm,
    whole_hbm,
    part_hbm,
    patch_2d,
    weight_2d,
    ahead_hbm,
    warp_hbm,
    recv4,
    coadd_hbm,
    fmat_hbm,
    tiles,
    warp,
    send1,
    recv1,
    sel,
    selt,
    asend,
    arecv,
    bsend,
    brecv,
    gath,
    spread,
    send4,
    cfull,
    crecv,
    coadd,
    hits,
    den,
    strips,
    rmat,
    patch_v,
    weight_v,
    wcol,
    ahead,
    fmat,
    whole_s,
    part_s,
    s1,
    r1,
    sa,
    ra,
    sb,
    rb,
    sga,
    rga,
    s4,
    r4,
    sc,
    rc,
    in_sem,
    small_sem,
    own1,
    own4,
    out_sem,
):
    visit, sky = lax.axis_index("visit"), lax.axis_index("sky")
    y, c = lax.div(visit, 2), lax.rem(visit, 2)
    z, x = lax.div(sky, 4), lax.rem(sky, 4)

    def dev(y_, c_, z_, x_):
        return (y_ * 2 + c_, z_ * 4 + x_)

    ring_of = (y, z, x)
    first_of, second_of = (x, y, z), (z, x, y)

    def on_ring(p, pos, core):
        return (dev(pos, core, z, x), dev(y, core, pos, x), dev(y, core, z, pos))[p]

    def on_first(p, pos):
        return (dev(y, c, z, pos), dev(pos, c, z, x), dev(y, c, pos, x))[p]

    def on_second(p, pos):
        return (dev(y, c, pos, x), dev(y, c, z, pos), dev(pos, c, z, x))[p]

    def partner(p, k):
        d, core = lax.div(k, 2), lax.rem(c + lax.rem(k, 2), 2)
        return lax.rem(ring_of[p] + d, 4), lax.rem(ring_of[p] + 4 - d, 4), core

    swap = (dev(z, c, y, x), dev(x, c, z, y))
    moved = (y != z, y != x)

    def fetch(i):
        half = pl.ds(i * (TILES_DEV // 2), TILES_DEV // 2)
        return pltpu.make_async_copy(tiles_hbm.at[half], tiles.at[half], in_sem.at[i])

    small = [
        pltpu.make_async_copy(here, there, small_sem.at[i])
        for i, (here, there) in enumerate(
            (
                (weight_2d, weight_v),
                (patch_2d, patch_v),
                (whole_hbm, whole_s),
                (part_hbm, part_s),
                (ahead_hbm, ahead),
            )
        )
    ]

    barrier = pltpu.get_barrier_semaphore()
    pl.semaphore_signal(barrier, inc=1, device_id=dev(y, 1 - c, z, x), device_id_type=MESH)
    for p in range(3):

        @pl.loop(2, 8)
        def _(k, p=p):
            pos, unused, core = partner(p, k)
            pl.semaphore_signal(barrier, inc=1, device_id=on_ring(p, pos, core), device_id_type=MESH)

    for i in range(2):

        @pl.when(moved[i])
        def _(i=i):
            pl.semaphore_signal(barrier, inc=1, device_id=swap[i], device_id_type=MESH)

    for copy in small:
        copy.start()
    for i in range(2):
        fetch(i).start()

    lane = lax.broadcasted_iota(jnp.int32, (8, 128), 1)
    down = lax.broadcasted_iota(jnp.int32, (8, 128), 0)
    reach = jnp.where(lane < 64, lane, lane - 128).astype(jnp.float32)
    reach = jnp.where((down & 1) == 0, reach, -reach)

    @pl.loop(0, 16)
    def _(j):
        rmat[j] = jnp.zeros((SIDE, SIDE), jnp.bfloat16)

    for copy in small[2:4]:
        copy.wait()

    for i in range(4):
        shift = jnp.zeros((8, 128), jnp.float32)
        for r in range(8):
            t = i * 4 + r // 2
            value = whole_s[r % 2, t].astype(jnp.float32) + part_s[r % 2, t]
            shift = jnp.where(down == r, value, shift)
        taps = lanczos(reach - shift)
        for r in range(8):
            row = jnp.broadcast_to(taps[r : r + 1], (8, 128))
            strips[i * 8 + r] = pltpu.roll(row, 0, 1, stride=1, stride_axis=0)

    def own_first(p, u):
        return pltpu.make_async_copy(send1.at[ring_of[p] * 2 + c, u], recv1.at[0, u], own1.at[u])

    def first(p, u, k):
        pos, unused, core = partner(p, k)
        return pltpu.make_async_remote_copy(
            src_ref=send1.at[pos * 2 + core, u],
            dst_ref=recv1.at[k, u],
            send_sem=s1.at[u],
            recv_sem=r1.at[u],
            device_id=on_ring(p, pos, core),
            device_id_type=MESH,
        )

    def start_wave(w):
        for p in range(3):
            u = 3 * w + p
            if u < UNITS:

                @pl.loop(0, 8)
                def _(q, u=u):
                    for r in range(8):
                        row = pl.ds(32 * q + 8 * (u // 2) + r, TILES_DEV, stride=SIDE)
                        send1[q, u, :, 128 * r : 128 * r + 128] = (wcol[...] * warp[u % 2, row]).astype(
                            jnp.bfloat16
                        )

                @pl.loop(1, 8)
                def _(k, p=p, u=u):
                    first(p, u, k).start()

                own_first(p, u).start()

    fetch(0).wait()

    @pl.loop(0, TILES_DEV // 8)
    def _(octet):
        @pl.when(octet == TILES_DEV // 16)
        def _():
            fetch(1).wait()

        for i in range(8):
            t = octet * 8 + i
            write_square(strips[2 * t], rmat.at[2 * i])
            write_square(strips[2 * t + 1], rmat.at[2 * i + 1])
        rowpasses = [
            jnp.dot(tiles[octet * 8 + i], rmat[2 * i + 1], preferred_element_type=jnp.float32).astype(
                jnp.bfloat16
            )
            for i in range(8)
        ]
        for i in range(8):
            value = jnp.dot(rmat[2 * i], rowpasses[i], preferred_element_type=jnp.float32)
            rows = pl.ds(pl.multiple_of((octet * 8 + i) * SIDE, SIDE), SIDE)
            for b in range(2):
                warp[b, rows, :] = value[:, 128 * b : 128 * b + 128]

    small[0].wait()
    mine_row = weight_v[pl.ds(visit * 2 + lax.div(sky, 8), 1), :]
    mine_row = pltpu.roll(jnp.broadcast_to(mine_row, (8, 128)), lax.rem(128 - lax.rem(sky, 8) * 16, 128), 1)
    diagonal = lax.broadcasted_iota(jnp.int32, (TILES_DEV, 128), 0) == lax.broadcasted_iota(
        jnp.int32, (TILES_DEV, 128), 1
    )
    one_each = jnp.where(diagonal, jnp.broadcast_to(mine_row[0:1], (TILES_DEV, 128)), 0.0)
    wcol[...] = jnp.broadcast_to(jnp.sum(one_each, axis=1, keepdims=True), (TILES_DEV, 128))

    pl.semaphore_wait(barrier, 19 + moved[0].astype(jnp.int32) + moved[1].astype(jnp.int32))
    start_wave(0)

    keep_warp = pltpu.make_async_copy(warp, warp_hbm, out_sem.at[0])
    keep_warp.start()
    small[1].wait()

    line = lax.broadcasted_iota(jnp.int32, (1, 128), 1)
    for p in range(3):
        key = jnp.zeros((1, 128), jnp.int32)
        for k in range(8):
            unused, pos, core = partner(p, k)
            v, s = on_ring(p, pos, core)
            found = jnp.broadcast_to(patch_v[pl.ds(v * 2 + lax.div(s, 8), 1), :], (8, 128))
            found = pltpu.roll(found, lax.rem(128 + 16 * k - lax.rem(s, 8) * 16, 128), 1)
            key = jnp.where((line >> 4) == k, found[0:1], key)
        if p == 0:
            key = ((key >> 2) & 3) * 16 + (key >> 4) * 4 + (key & 3)
        hot = jnp.where(
            jnp.broadcast_to(key, (128, 128)) == lax.broadcasted_iota(jnp.int32, (128, 128), 0), 1.0, 0.0
        )
        sel[p] = hot[0:64].astype(jnp.bfloat16)
        selt[p] = hot.T.astype(jnp.bfloat16)

    start_wave(1)

    @pl.loop(0, 48)
    def _(n):
        p, second, k = lax.div(n, 16), lax.rem(lax.div(n, 4), 4), lax.rem(n, 4)
        owner = by_portion(p, (second * 4 + x, y * 4 + second, z * 4 + second))
        hit = jnp.where(patch_v[...] == owner * 4 + k, weight_v[...], 0.0)
        hits[n] = hit[0:8] + hit[8:16]

    weights = 1.0 + jnp.sum(jnp.sum(hits[...], axis=1), axis=1, keepdims=True)
    for p in range(3):
        den[p] = jnp.broadcast_to(weights[16 * p : 16 * p + 16], (16, 128))

    start_wave(2)

    small[4].wait()

    @pl.loop(0, NF)
    def _(j):
        fmat[j] = jnp.zeros((SIDE, SIDE), jnp.bfloat16)
        write_square(ahead[j], fmat.at[j])

    keep_fmat = pltpu.make_async_copy(fmat, fmat_hbm, out_sem.at[1])
    keep_fmat.start()

    def second(p, u, d):
        pos = lax.rem(first_of[p] + d, 4)
        return pltpu.make_async_remote_copy(
            src_ref=asend.at[pos, u],
            dst_ref=arecv.at[d - 1, u],
            send_sem=sa.at[u],
            recv_sem=ra.at[u],
            device_id=on_first(p, pos),
            device_id_type=MESH,
        )

    def third(p, u, d):
        return pltpu.make_async_remote_copy(
            src_ref=bsend.at[u],
            dst_ref=brecv.at[d - 1, u],
            send_sem=sb.at[u],
            recv_sem=rb.at[u],
            device_id=on_second(p, lax.rem(second_of[p] + d, 4)),
            device_id_type=MESH,
        )

    def fourth(p, u, d):
        mine = gath.at[first_of[p], u]
        return pltpu.make_async_remote_copy(
            src_ref=mine,
            dst_ref=mine,
            send_sem=sga.at[u],
            recv_sem=rga.at[u],
            device_id=on_first(p, lax.rem(first_of[p] + d, 4)),
            device_id_type=MESH,
        )

    def to_owner(p, u):
        return pltpu.make_async_remote_copy(
            src_ref=cfull.at[u, second_of[p]],
            dst_ref=crecv.at[u],
            send_sem=sc.at[u],
            recv_sem=rc.at[u],
            device_id=swap[p - 1],
            device_id_type=MESH,
        )

    def own_last(p, u):
        return pltpu.make_async_copy(send4.at[0, u], recv4.at[ring_of[p] * 2 + c, u], own4.at[u])

    def last(p, u, k):
        unused, pos, core = partner(p, k)
        return pltpu.make_async_remote_copy(
            src_ref=send4.at[k, u],
            dst_ref=recv4.at[ring_of[p] * 2 + c, u],
            send_sem=s4.at[u],
            recv_sem=r4.at[u],
            device_id=on_ring(p, pos, core),
            device_id_type=MESH,
        )

    def one_unit(u, before, body, after):
        @pl.when((u >= 0) & (u < UNITS))
        def _():
            portion = lax.rem(u, 3)
            for p in range(3):

                @pl.when(portion == p)
                def _(p=p):
                    before(p, u)

            body(u, portion)
            for p in range(3):

                @pl.when(portion == p)
                def _(p=p):
                    after(p, u)

    def all_three(act):
        @pl.loop(1, 4)
        def _(d):
            act(d)

    def all_seven(act):
        @pl.loop(1, 8)
        def _(k):
            act(k)

    def await_bytes(ref, sem):
        pltpu.make_async_copy(ref, ref, sem).wait()

    def seven(ref, u):
        return ref.at[pl.ds(1, 7), u]

    def three(ref, u):
        return ref.at[pl.ds(0, 3), u]

    def tiles_here(p, u):
        own_first(p, u).wait()
        await_bytes(seven(recv1, u), r1.at[u])

    def add_tiles(u, p):
        total = jnp.dot(sel[p], recv1[:, u].reshape(128, 1024), preferred_element_type=jnp.float32)
        asend[:, u] = total.astype(jnp.bfloat16).reshape(4, 16, 1024)

    def add_first(u, p):
        total = asend[by_portion(p, first_of), u].astype(jnp.float32)
        for d in range(3):
            total = total + arecv[d, u].astype(jnp.float32)
        bsend[u] = total.astype(jnp.bfloat16)

    def add_second(u, p):
        total = bsend[u].astype(jnp.float32)
        for d in range(3):
            total = total + brecv[d, u].astype(jnp.float32)
        total = total / jnp.concatenate([den[p]] * 8, axis=1)
        for b in range(4):
            cfull[u, b] = total[4 * b : 4 * b + 4]
        gath[by_portion(p, first_of), u] = total.astype(jnp.bfloat16)

    def templates_out(p, u):
        all_three(lambda d: fourth(p, u, d).start())
        if p > 0:

            @pl.when(moved[p - 1])
            def _():
                to_owner(p, u).start()

    def pick(u, p):
        found = jnp.dot(
            selt[p, :, 0:64], gath[:, u].reshape(64, 1024), preferred_element_type=jnp.float32
        )
        for r in range(8):
            spread[pl.ds(r, 128, stride=8), :] = found[:, 128 * r : 128 * r + 128]
        send4[:, u] = spread[...].astype(jnp.bfloat16).reshape(8, 128, 128)

    def picks_out(p, u):
        all_seven(lambda k: last(p, u, k).start())
        own_last(p, u).start()

    @pl.loop(0, UNITS + LAGS[3])
    def _(step):
        one_unit(
            step - LAGS[0],
            tiles_here,
            add_tiles,
            lambda p, u: all_three(lambda d: second(p, u, d).start()),
        )
        one_unit(
            step - LAGS[1],
            lambda p, u: await_bytes(three(arecv, u), ra.at[u]),
            add_first,
            lambda p, u: all_three(lambda d: third(p, u, d).start()),
        )
        one_unit(
            step - LAGS[2],
            lambda p, u: await_bytes(three(brecv, u), rb.at[u]),
            add_second,
            templates_out,
        )
        one_unit(
            step - LAGS[3],
            lambda p, u: await_bytes(three(gath, u), rga.at[u]),
            pick,
            picks_out,
        )

    for u in range(UNITS):
        p = u % 3
        if p == 0:
            crecv[u] = cfull[u, second_of[p]]
        else:

            @pl.when(moved[p - 1])
            def _(p=p, u=u):
                to_owner(p, u).wait()

            @pl.when(jnp.logical_not(moved[p - 1]))
            def _(p=p, u=u):
                crecv[u] = cfull[u, second_of[p]]

    @pl.loop(0, UNITS // 2)
    def _(rb):
        for cb in range(2):
            unit = crecv[2 * rb + cb]
            for k in range(4):
                rows = jnp.zeros((8, 128), jnp.float32)
                for r in range(8):
                    row = jnp.broadcast_to(unit[k : k + 1, 128 * r : 128 * r + 128], (8, 128))
                    rows = jnp.where(down == r, row, rows)
                coadd[k, pl.ds(pl.multiple_of(rb * 8, 8), 8), 128 * cb : 128 * cb + 128] = rows

    keep_coadd = pltpu.make_async_copy(coadd, coadd_hbm, out_sem.at[2])
    keep_coadd.start()

    @pl.loop(0, UNITS)
    def _(u):
        own_last(0, u).wait()
        await_bytes(seven(recv4, u), r4.at[u])
        await_bytes(seven(send4, u), s4.at[u])
        await_bytes(seven(send1, u), s1.at[u])
        await_bytes(three(asend, u), sa.at[u])
        await_bytes(three(brecv, u), sb.at[u])
        await_bytes(three(gath, u), sga.at[u])

    keep_warp.wait()
    keep_fmat.wait()
    keep_coadd.wait()


def subtract(
    coeff_s,
    fmat_hbm,
    back_hbm,
    warp_hbm,
    picked_hbm,
    coadd_in,
    diff_hbm,
    coadd_out,
    back,
    warp,
    picked,
    diff,
    fmat,
    mband,
    tbuf,
    hbuf,
    strip_sem,
    in_sem,
    out_sem,
    coadd_sem,
):
    pairs = TILES_DEV // 2

    def enter(pair):
        chunk = (slice(None), slice(None), pl.ds(pair * 16, 16))
        rows = (slice(None), pl.ds(pair * 2 * SIDE, 2 * SIDE))
        return (
            pltpu.make_async_copy(picked_hbm.at[chunk], picked.at[chunk], in_sem.at[pair, 0]),
            pltpu.make_async_copy(warp_hbm.at[rows], warp.at[rows], in_sem.at[pair, 1]),
        )

    def leave(pair):
        here = pl.ds(pair * 2, 2)
        return pltpu.make_async_copy(diff.at[here], diff_hbm.at[here], out_sem.at[pair])

    strip_copies = (
        pltpu.make_async_copy(fmat_hbm, fmat, strip_sem.at[0]),
        pltpu.make_async_copy(back_hbm, back, strip_sem.at[1]),
    )
    for copy in strip_copies:
        copy.start()

    @pl.loop(0, pairs)
    def _(pair):
        for copy in enter(pair):
            copy.start()

    pass_coadd = pltpu.make_async_copy(coadd_in, coadd_out, coadd_sem)
    pass_coadd.start()
    for copy in strip_copies:
        copy.wait()

    def assemble(pair, slot):
        rows = pl.ds(pl.multiple_of(pair * 16, 16), 16)
        for q in range(8):
            for i in range(2):
                for b in range(2):
                    upper = picked[q, 4 * i + b, rows, :].astype(jnp.float32)
                    lower = picked[q, 4 * i + 2 + b, rows, :].astype(jnp.float32)
                    at = 32 * q + 16 * i
                    cols = slice(128 * b, 128 * b + 128)
                    tbuf[slot, at : at + 16, cols] = jnp.concatenate(
                        [upper[0:8], lower[0:8]], axis=0
                    ).astype(jnp.bfloat16)
                    tbuf[slot, SIDE + at : SIDE + at + 16, cols] = jnp.concatenate(
                        [upper[8:16], lower[8:16]], axis=0
                    ).astype(jnp.bfloat16)

    def mix(pair, slot):
        for half in range(2):
            t = pair * 2 + half
            for j in range(NF):
                strip = None
                for k in range(len(BASIS_COLS)):
                    if BASIS_COLS[k] == j:
                        term = coeff_s[t, k] * back[BASIS_ROWS[k]]
                        strip = term if strip is None else strip + term
                diag, right, left = toeplitz_blocks(strip)
                cols = slice(128 * j, 128 * j + 128)
                mband[slot, half, 0:16, cols] = right
                for i in range(8):
                    mband[slot, half, 16 + 16 * i : 32 + 16 * i, cols] = diag[i]
                mband[slot, half, 144:160, cols] = left

    def columns(slot):
        for j in range(NF):
            filtered = jnp.dot(tbuf[slot], fmat[j], preferred_element_type=jnp.float32).astype(jnp.bfloat16)
            for i in range(4):
                hbuf[slot, i, 128 * j : 128 * j + 128, :] = filtered[128 * i : 128 * i + 128]

    def rest(pair, slot):
        for half in range(2):
            t = pair * 2 + half
            top = jnp.dot(mband[slot, half, 16:160, :], hbuf[slot, 2 * half], preferred_element_type=jnp.float32)
            low = jnp.dot(
                mband[slot, half, 0:144, :], hbuf[slot, 2 * half + 1], preferred_element_type=jnp.float32
            )
            whole = jnp.concatenate([top[0:112], top[112:144] + low[0:32], low[32:144]], axis=0)
            for b in range(2):
                cols = slice(128 * b, 128 * b + 128)
                diff[t, :, cols] = warp[b, pl.ds(pl.multiple_of(t * SIDE, SIDE), SIDE), :] - whole[:, cols]
        leave(pair).start()

    @pl.loop(0, pairs // 2)
    def _(step):
        chosen = [step * 2 + slot for slot in range(2)]
        for pair in chosen:
            for copy in enter(pair):
                copy.wait()
        for slot, pair in enumerate(chosen):
            assemble(pair, slot)
            mix(pair, slot)
            columns(slot)
        for slot, pair in enumerate(chosen):
            rest(pair, slot)

    @pl.loop(0, pairs)
    def _(pair):
        leave(pair).wait()

    pass_coadd.wait()


def shards(tiles, shift_int, shift_frac, tile_weight, tile_patch, al_coeff):
    ahead, back = factor_strips()
    smem = pl.BlockSpec(memory_space=pltpu.SMEM)
    hbm = pl.BlockSpec(memory_space=pl.ANY)
    bf16, f32, i32 = jnp.bfloat16, jnp.float32, jnp.int32
    dma = pltpu.SemaphoreType.DMA
    lanes = (8, UNITS, TILES_DEV, 1024)
    block = (8, UNITS, TILES_DEV * 8, 128)
    warp, picked, coadd_units, columns = pl.pallas_call(
        exchange,
        out_shape=(
            jax.ShapeDtypeStruct((2, TILES_DEV * SIDE, 128), f32),
            jax.ShapeDtypeStruct(block, bf16),
            jax.ShapeDtypeStruct((4, 32, SIDE), f32),
            jax.ShapeDtypeStruct((NF, SIDE, SIDE), bf16),
        ),
        in_specs=[hbm] * 6,
        out_specs=(hbm, hbm, hbm, hbm),
        scratch_shapes=[
            pltpu.VMEM((TILES_DEV, SIDE, SIDE), bf16),
            pltpu.VMEM((2, TILES_DEV * SIDE, 128), f32),
            pltpu.VMEM(lanes, bf16),
            pltpu.VMEM(lanes, bf16),
            pltpu.VMEM((3, 64, 128), bf16),
            pltpu.VMEM((3, 128, 128), bf16),
            pltpu.VMEM((4, UNITS, 16, 1024), bf16),
            pltpu.VMEM((3, UNITS, 16, 1024), bf16),
            pltpu.VMEM((UNITS, 16, 1024), bf16),
            pltpu.VMEM((3, UNITS, 16, 1024), bf16),
            pltpu.VMEM((4, UNITS, 16, 1024), bf16),
            pltpu.VMEM((1024, 128), f32),
            pltpu.VMEM(block, bf16),
            pltpu.VMEM((UNITS, 4, 4, 1024), f32),
            pltpu.VMEM((UNITS, 4, 1024), f32),
            pltpu.VMEM((4, 32, SIDE), f32),
            pltpu.VMEM((48, 8, 128), f32),
            pltpu.VMEM((3, 16, 128), f32),
            pltpu.VMEM((2 * TILES_DEV, 8, 128), f32),
            pltpu.VMEM((16, SIDE, SIDE), bf16),
            pltpu.VMEM((16, 128), i32),
            pltpu.VMEM((16, 128), f32),
            pltpu.VMEM((TILES_DEV, 128), f32),
            pltpu.VMEM((NF, 8, 128), f32),
            pltpu.VMEM((NF, SIDE, SIDE), bf16),
            pltpu.SMEM((2, TILES_DEV), i32),
            pltpu.SMEM((2, TILES_DEV), f32),
            dma((UNITS,)),
            dma((UNITS,)),
            dma((UNITS,)),
            dma((UNITS,)),
            dma((UNITS,)),
            dma((UNITS,)),
            dma((UNITS,)),
            dma((UNITS,)),
            dma((UNITS,)),
            dma((UNITS,)),
            dma((UNITS,)),
            dma((UNITS,)),
            dma((2,)),
            dma((5,)),
            dma((UNITS,)),
            dma((UNITS,)),
            dma((3,)),
        ],
        compiler_params=pltpu.CompilerParams(
            collective_id=0, has_side_effects=True, vmem_limit_bytes=56 << 20
        ),
    )(
        tiles,
        shift_int.T,
        shift_frac.T,
        tile_patch.reshape(16, 128),
        tile_weight.reshape(16, 128),
        jnp.asarray(ahead),
    )
    difference, coadd = pl.pallas_call(
        subtract,
        out_shape=(
            jax.ShapeDtypeStruct((TILES_DEV, SIDE, SIDE), f32),
            jax.ShapeDtypeStruct((4, 32, SIDE), f32),
        ),
        in_specs=[smem, hbm, hbm, hbm, hbm, hbm],
        out_specs=(hbm, hbm),
        scratch_shapes=[
            pltpu.VMEM((NF, 8, 128), f32),
            pltpu.VMEM((2, TILES_DEV * SIDE, 128), f32),
            pltpu.VMEM(block, bf16),
            pltpu.VMEM((TILES_DEV, SIDE, SIDE), f32),
            pltpu.VMEM((NF, SIDE, SIDE), bf16),
            pltpu.VMEM((2, 2, 160, 128 * NF), bf16),
            pltpu.VMEM((2, 2 * SIDE, SIDE), bf16),
            pltpu.VMEM((2, 4, 128 * NF, SIDE), bf16),
            dma((2,)),
            dma((TILES_DEV // 2, 2)),
            dma((TILES_DEV // 2,)),
            dma,
        ],
        compiler_params=pltpu.CompilerParams(vmem_limit_bytes=60 << 20),
    )(al_coeff, columns, jnp.asarray(back), warp, picked, coadd_units)
    return coadd, difference


def solution(mesh):
    return jax.shard_map(
        shards,
        mesh=mesh,
        in_specs=(
            P(("visit", "sky"), None, None),
            P(("visit", "sky"), None),
            P(("visit", "sky"), None),
            P(),
            P(),
            P(("visit", "sky"), None),
        ),
        out_specs=(P("sky", "visit", None), P(("visit", "sky"), None, None)),
        check_vma=False,
    )
```
